32 devices in a mesh: ctx: 2 (over core), exp: 16 (over z, y, x).
Axes of the slice: x: 2, y: 2, z: 4, core: 2. Of those that a mesh axis runs over, the one named last changes fastest.
Arguments:
- tokens: bfloat16 [16, 2, 512, 768], P('exp', 'ctx'), may hold values from -6 to 6
- cotangent: bfloat16 [16, 2, 512, 768], P('exp', 'ctx'), may hold values from -6 to 6
- norm_gains: float32 [2, 768], replicated, may hold values from 0.1 to 1.9
- query_key_value_weight: bfloat16 [768, 2304], replicated, may hold values from -0.21875 to 0.21875
- attention_out_weight: bfloat16 [768, 768], replicated, may hold values from -1.5 to 1.5
- rel_bias: float32 [12, 32], replicated, may hold values from -4 to 4
- router_matrix: bfloat16 [768, 16], replicated, may hold values from -0.15625 to 0.15625
- expert_in: bfloat16 [16, 768, 3072], P('exp'), may hold values from -0.21875 to 0.21875
- expert_out: bfloat16 [16, 3072, 768], P('exp'), may hold values from -0.109375 to 0.109375
- adapters: float32 [8, 233728], P(None, 'exp'), may hold values from -0.5 to 0.5
- first_moment: float32 [8, 233728], P(None, 'exp'), as said below
- second_moment: float32 [8, 233728], P(None, 'exp'), may hold values from 2.048 to 8.192
- segment_ids: int32 [16, 1024], P('exp'), may hold values from 0 to 4, as said below
- routes: int32 [16, 2, 512, 2], P('exp', 'ctx'), may hold values from 0 to 15, all different within a row; in each aligned block of 512 rows (0 to 511, 512 to 1023, ..., all dimensions but the last counted through in order) at most 80 rows name the same one
- adapter_pick: int32 [16], replicated, may hold values from 0 to 7
Outputs:
- mixed: bfloat16 [16, 2, 512, 768], P('exp', 'ctx')
- input_grad: float32 [16, 2, 512, 768], P('exp', 'ctx')
- new_adapters: float32 [8, 233728], P(None, 'exp')
- new_first: float32 [8, 233728], P(None, 'exp')
- new_second: float32 [8, 233728], P(None, 'exp')
The draws below stay inside these ranges and needn't reach their ends.
Inputs may be any that keep to these rules, and one draw needn't show every extreme that they name: `segment_ids`: ids never fall along a sequence; in every sequence one document runs from a position under 512/2 to one at 768 or later. `routes`: the two experts of a row differ; the rows of one device name each expert at most 80 times, and that bound is reached. `first_moment`: no entry is zero.
All inputs are finite; a program needn't handle non-finite values.
Results may differ from the reference program's by a relative error of at most 0.018.
Values may be sent and summed in bfloat16 or wider, within the bound.
A program may use at most 320 MiB of HBM per device.

```python
import math
import jax
import jax.numpy as jnp
import numpy as np
from jax import lax

MODEL_WIDTH = 768
HEADS = 12
HEAD_DIM = 64
FF = 3072
ADAPTER_RANK = 16
ADAPTER_COUNT = 8
BUCKETS = 32
STEP_NUM = 5
TOK_DEV = 512
SEQ_PARTS = 2
SEQ_LEN = 1024
SEQS = 16
TOKENS = 16384
EXPERT_COUNT = 16
CAP = 80
PARAMS = 233728
N_CTX = 2


def draw_first_moment(key, part):
    key = jax.random.fold_in(key, 11)
    sign_key, size_key = jax.random.split(key)
    signs = jnp.where(jax.random.bernoulli(sign_key, 0.5, (ADAPTER_COUNT, PARAMS)), 1.0, -1.0)
    sizes_drawn = jnp.exp(jax.random.uniform(size_key, (ADAPTER_COUNT, PARAMS), jnp.float32, -0.6931, 0.6931))
    return (signs * sizes_drawn * ((TOKENS / ADAPTER_COUNT) ** 0.5 / 9.0)).astype(jnp.float32)


def draw_segment_ids(key, part):
    key = jax.random.fold_in(key, 7)
    lead_key, start_key, finish_key, tail_key = jax.random.split(key, 4)
    half_rows = TOK_DEV // 2
    doc_start = jax.random.randint(start_key, (SEQS, 1), 1, half_rows)
    finish = SEQ_LEN - jax.random.randint(finish_key, (SEQS, 1), 1, half_rows + 1)
    leading = jax.random.randint(lead_key, (SEQS, 1), 0, doc_start)
    trailing = finish + jax.random.randint(tail_key, (SEQS, 1), 0, SEQ_LEN - finish)
    places = jnp.arange(SEQ_LEN, dtype=jnp.int32)[None, :]
    segment_rows = ((places >= leading) & (leading > 0)).astype(jnp.int32)
    segment_rows = segment_rows + (places >= doc_start).astype(jnp.int32)
    segment_rows = segment_rows + (places >= finish).astype(jnp.int32)
    segment_rows = segment_rows + ((places >= trailing) & (trailing > finish)).astype(jnp.int32)
    return segment_rows


def touch_ends(drawn, own_key, smallest, top_value):
    dims = drawn.shape
    place = [jax.random.randint(jax.random.fold_in(own_key, axis), (), 0, dims[axis]) for axis in range(len(dims))]
    drawn = drawn.at[tuple(place)].set(smallest)
    longest = dims.index(max(dims))
    place[longest] = (place[longest] + 1) % dims[longest]
    return drawn.at[tuple(place)].set(top_value)


def block_scale(stream_key, shape, shards, low, top_value):
    def one(axis_at, blocks):
        steps = jax.random.uniform(jax.random.fold_in(jax.random.fold_in(stream_key, 6), axis_at), (blocks,), jnp.float32, low / len(shards), top_value / len(shards))
        return jnp.repeat(jnp.exp(steps), shape[axis_at] // blocks).reshape((-1,) + (1,) * (len(shape) - axis_at - 1))

    gain = one(*shards[0])
    for cut in shards[1:]:
        gain = gain * one(*cut)
    return gain


def assign_block(rng, own, number, rows, number_of, top, bound, skew):
    order = jax.random.permutation(rng, number_of)
    packed, common = load_shares(number_of, rows * top, bound, skew, True), load_shares(number_of, rows * top, bound, skew, False)
    places = jnp.arange(number_of)

    def named(tallies, turn):
        used = int((tallies > 0).sum())
        fixed = max(1, used // 4)
        passed = fixed + (places - fixed + turn * (used - fixed)) % max(1, number_of - fixed)
        return jnp.zeros((number_of,), jnp.int32).at[order[jnp.where(places < fixed, places, passed)]].set(jnp.asarray(tallies, jnp.int32))

    tallies = jnp.where(number % 4 == 0, named(packed, number // 4), named(common, number - number // 4 - 1))
    mixed = jax.random.permutation(jax.random.fold_in(own, 3), number_of)
    donor, receiver = mixed[0:number_of // 2 * 2:2], mixed[1:number_of // 2 * 2:2]
    margin = jnp.minimum(tallies[donor] - 1, bound - tallies[receiver]) // 2
    margin = jnp.where((donor == order[0]) | (receiver == order[0]) | (tallies[receiver] == 0), 0, jnp.maximum(margin, 0))
    passed = jax.random.randint(jax.random.fold_in(own, 4), (number_of // 2,), 0, 1 << 20) % (margin + 1)
    tallies = tallies.at[donor].add(-passed).at[receiver].add(passed)
    items = jnp.searchsorted(jnp.cumsum(tallies), jnp.arange(rows * top), side="right").astype(jnp.int32)
    grid = items.reshape(top, rows).T
    grid = grid[jax.random.permutation(jax.random.fold_in(own, 1), rows)]
    turn = jax.random.randint(jax.random.fold_in(own, 2), (rows, 1), 0, top)
    return jnp.take_along_axis(grid, (jnp.arange(top)[None, :] + turn) % top, axis=1)


def load_shares(number_of, total, most, lean, full):
    loads = [(1 << 20) // math.isqrt(grade ** lean) + 1 for grade in range(1, number_of + 1)]
    largest = most if full else min(most, max(-(-total // number_of), total * loads[0] // sum(loads)))
    least = 1 if total - largest >= number_of - 1 else 0
    given, rest = [largest] + [least] * (number_of - 1), total - largest - least * (number_of - 1)
    while rest > 0:
        free = [i for i in range(1, number_of) if given[i] < largest] or [i for i in range(1, number_of) if given[i] < most]
        whole, left = sum([loads[i] for i in free]), rest
        for i in free:
            more = min(most - given[i], max(1, left * loads[i] // whole), rest)
            given[i] = given[i] + more
            rest = rest - more
    return np.array(given)


def scatter_about(stream_key, dims, deviation, limit, pieces=(), kind=jnp.bfloat16):
    loudness = block_scale(stream_key, dims, pieces, -0.22, 0.18) if pieces else 1.0
    array = jax.random.normal(stream_key, dims, jnp.float32) * deviation * loudness
    return jnp.minimum(jnp.maximum(array, -limit), limit).astype(kind)


def setup_inputs(seed: int = 0) -> dict:
    keys = jax.random.split(jax.random.key(seed), 16)
    tokens = scatter_about(keys[0], (SEQS, SEQ_PARTS, TOK_DEV, MODEL_WIDTH), 1.0, 6.0, ((0, 16), (1, 2)))
    cotangent = scatter_about(keys[1], (SEQS, SEQ_PARTS, TOK_DEV, MODEL_WIDTH), 1.0, 6.0, ((0, 16), (1, 2)))
    norm_gains = jnp.clip(1.0 + 0.18 * jax.random.normal(keys[2], (2, MODEL_WIDTH), jnp.float32), 0.1, 1.9)
    query_key_value_weight = scatter_about(keys[3], (MODEL_WIDTH, 3 * MODEL_WIDTH), MODEL_WIDTH ** -0.5, 0.21875)
    attention_out_weight = scatter_about(keys[4], (MODEL_WIDTH, MODEL_WIDTH), (HEAD_DIM // 4) ** -0.5, 1.5)
    rel_bias = scatter_about(keys[5], (HEADS, BUCKETS), 1.0, 4.0, (), jnp.float32)
    router_matrix = scatter_about(keys[6], (MODEL_WIDTH, EXPERT_COUNT), (2 * MODEL_WIDTH) ** -0.5, 0.15625)
    expert_in = scatter_about(keys[7], (EXPERT_COUNT, MODEL_WIDTH, FF), MODEL_WIDTH ** -0.5, 0.21875, ((0, 16),))
    expert_out = scatter_about(keys[8], (EXPERT_COUNT, FF, MODEL_WIDTH), FF ** -0.5, 0.109375, ((0, 16),))
    adapters = scatter_about(keys[9], (ADAPTER_COUNT, PARAMS), (0.37 * (MODEL_WIDTH * ADAPTER_RANK) ** -0.25), 0.5, ((1, 16),), jnp.float32)
    first_moment = draw_first_moment(jax.random.fold_in(keys[15], 71), 0)
    second_moment = jnp.clip(jnp.exp(math.log(8.192) - 1.3862944 * jax.random.uniform(keys[11], (ADAPTER_COUNT, PARAMS), jnp.float32) ** block_scale(keys[11], (ADAPTER_COUNT, PARAMS), ((1, 16),), -0.2, 0.2)), 2.048, 8.192)
    segment_ids = draw_segment_ids(jax.random.fold_in(keys[15], 71), 0)
    routes_keys = jax.random.split(jax.random.fold_in(keys[13], 1), SEQS * SEQ_PARTS * TOK_DEV // TOK_DEV)
    routes_turns = jax.random.permutation(jax.random.fold_in(keys[13], 3), SEQS * SEQ_PARTS * TOK_DEV // TOK_DEV)
    routes = jax.vmap(lambda own, number: assign_block(jax.random.fold_in(keys[13], 2), own, number, TOK_DEV, EXPERT_COUNT, 2, CAP, 1))(routes_keys, routes_turns).reshape((SEQS, SEQ_PARTS, TOK_DEV, 2))
    adapter_pick = touch_ends(jax.random.randint(keys[14], (SEQS,), 0, ADAPTER_COUNT), jax.random.fold_in(keys[14], 1), 0, ADAPTER_COUNT - 1).astype(jnp.int32)
    return {"tokens": tokens, "cotangent": cotangent, "norm_gains": norm_gains, "query_key_value_weight": query_key_value_weight, "attention_out_weight": attention_out_weight, "rel_bias": rel_bias, "router_matrix": router_matrix, "expert_in": expert_in, "expert_out": expert_out, "adapters": adapters, "first_moment": first_moment, "second_moment": second_moment, "segment_ids": segment_ids, "routes": routes, "adapter_pick": adapter_pick}


PRECISE = lax.Precision.HIGHEST
NORM_EPS = 1e-06
ADAPTER_SCALE = 2.0
MASKED = -1e+30
BETA_ONE = 0.9
BETA_TWO = 0.999
LEARN_RATE = 0.05
WEIGHT_DECAY = 0.01
ADAM_EPS = 1e-08

@jax.custom_vjp
def low(v):
    return lax.optimization_barrier(v.astype(jnp.bfloat16)).astype(jnp.float32)

@jax.custom_vjp
def low_back(v):
    return v

def low_keep(v):
    return (low(v), None)

def low_pass(kept, grad):
    return (grad,)

def back_keep(v):
    return (v, None)

def back_low(kept, grad):
    return (low(grad),)
low.defvjp(low_keep, low_pass)
low_back.defvjp(back_keep, back_low)

def both_directions(values):
    return low_back(low(values))

def matrix_product(former, latter):
    return jnp.dot(former, latter, precision=PRECISE)

def precise_einsum(pattern, former, latter):
    return jnp.einsum(pattern, former, latter, precision=PRECISE)

def bucket_bounds():
    bounds = list(range(1, 16))
    for level_index in range(16):
        bounds.append(int(np.ceil(16.0 * 8.0 ** (level_index / 16.0) - 1e-09)))
    return bounds

def bucket_of(distance):
    bucket_sum = jnp.zeros(distance.shape, jnp.int32)
    for threshold in bucket_bounds():
        bucket_sum = bucket_sum + (distance >= threshold).astype(jnp.int32)
    return bucket_sum

def rms_scale(values, gain_row):
    return values * lax.rsqrt(lax.optimization_barrier(jnp.mean(values * values, axis=-1, keepdims=True)) + NORM_EPS) * gain_row

def dealt_positions():
    half_rows = TOK_DEV // 2
    offsets = jnp.arange(half_rows, dtype=jnp.int32)
    part_ids = jnp.arange(N_CTX, dtype=jnp.int32)
    first_half = part_ids[:, None] * half_rows + offsets[None, :]
    second_half = (2 * N_CTX - 1 - part_ids)[:, None] * half_rows + offsets[None, :]
    return jnp.concatenate([first_half, second_half], axis=1).reshape(-1)

def unpack(flat_rows):
    cut_one = 6 * ADAPTER_RANK * MODEL_WIDTH
    cut_two = cut_one + 5 * ADAPTER_RANK * MODEL_WIDTH
    cut_three = cut_two + 2 * ADAPTER_RANK * FF
    adapt_count = flat_rows.shape[0]
    down_all = flat_rows[:, :cut_one].reshape(adapt_count, MODEL_WIDTH, 6 * ADAPTER_RANK)
    ups_model = flat_rows[:, cut_one:cut_two].reshape(adapt_count, 5, ADAPTER_RANK, MODEL_WIDTH)
    ups_hidden = flat_rows[:, cut_two:cut_three].reshape(adapt_count, 2, ADAPTER_RANK, FF)
    router_up_weights = flat_rows[:, cut_three:].reshape(adapt_count, ADAPTER_RANK, -1)
    return (down_all, ups_model, ups_hidden, router_up_weights)

def attend_block(query_rows, query_pos, query_seg, key_rows, value_rows, key_pos, key_seg, rel_bias):
    scores = precise_einsum('qhd,khd->hqk', query_rows, key_rows) * HEAD_DIM ** (-0.5)
    distance = query_pos[:, None] - key_pos[None, :]
    scores = low_back(scores + jnp.take(rel_bias, bucket_of(distance), axis=1))
    allowed = (distance >= 0) & (query_seg[:, None] == key_seg[None, :])
    scores = jnp.where(allowed[None], scores, MASKED)
    row_top = lax.optimization_barrier(jnp.max(scores, axis=-1, keepdims=True))
    weights = jnp.exp(scores - row_top)
    weights = low(weights / lax.optimization_barrier(jnp.sum(weights, axis=-1, keepdims=True)))
    return precise_einsum('hqk,khd->qhd', weights, value_rows)

def reference(tokens, cotangent, norm_gains, query_key_value_weight, attention_out_weight, rel_bias, router_matrix, expert_in, expert_out, adapters, first_moment, second_moment, segment_ids, routes, adapter_pick):
    seq_len = N_CTX * TOK_DEV
    row_total = SEQS * seq_len
    positions = dealt_positions()
    blocks = SEQS * N_CTX
    expert_rows = blocks * CAP
    flat_routes = routes.reshape(blocks, 2 * TOK_DEV)
    route_hot = (flat_routes[:, :, None] == jnp.arange(EXPERT_COUNT, dtype=jnp.int32)[None, None, :]).astype(jnp.int32)
    slot_rows = lax.optimization_barrier(jnp.sum((jnp.cumsum(route_hot, axis=1) - route_hot) * route_hot, axis=2))
    destination = (flat_routes * expert_rows + jnp.arange(blocks, dtype=jnp.int32)[:, None] * CAP + slot_rows).reshape(-1)
    slot_source = jnp.full((EXPERT_COUNT * expert_rows,), row_total, jnp.int32).at[destination].set(jnp.arange(2 * row_total, dtype=jnp.int32) // 2).reshape(EXPERT_COUNT, expert_rows)
    token_adapter = jnp.concatenate([jnp.repeat(adapter_pick, seq_len), jnp.full((1,), ADAPTER_COUNT, jnp.int32)])
    rank_owner = jnp.arange(ADAPTER_COUNT * ADAPTER_RANK, dtype=jnp.int32) // ADAPTER_RANK
    row_masks = (token_adapter[:, None] == rank_owner[None, :]).astype(jnp.float32)
    gain_rows = norm_gains.astype(jnp.float32)
    query_key_value_float = query_key_value_weight.astype(jnp.float32)
    output_float = attention_out_weight.astype(jnp.float32)
    router_weight_float = router_matrix.astype(jnp.float32)
    first_experts = expert_in.astype(jnp.float32)
    second_experts = expert_out.astype(jnp.float32)
    route_flat = routes.reshape(row_total, 2)
    segment_keys = segment_ids[:, positions]

    def forward(token_values, adapter_values):
        rounded = low(adapter_values)
        down_all, ups_model, ups_hidden, router_up_weights = unpack(rounded)

        def one_sequence(loop_items):
            seq_tokens, adapter_index, seq_segments = loop_items
            down_own = down_all[adapter_index]
            owned_up_weight = ups_model[adapter_index]
            normalized_rows = low(rms_scale(seq_tokens, gain_rows[0]))
            inner_qkv = both_directions(matrix_product(normalized_rows, down_own[:, :3 * ADAPTER_RANK]))
            lifted_rows = precise_einsum('tgr,grd->tgd', inner_qkv.reshape(seq_len, 3, ADAPTER_RANK), owned_up_weight[:3]).reshape(seq_len, 3 * MODEL_WIDTH)
            query_key_value_rows = both_directions(matrix_product(normalized_rows, query_key_value_float) + ADAPTER_SCALE * lifted_rows)
            key_rows = query_key_value_rows[:, MODEL_WIDTH:2 * MODEL_WIDTH].reshape(seq_len, HEADS, HEAD_DIM)
            value_rows = query_key_value_rows[:, 2 * MODEL_WIDTH:].reshape(seq_len, HEADS, HEAD_DIM)
            queries = query_key_value_rows[:, :MODEL_WIDTH].reshape(N_CTX, TOK_DEV, HEADS, HEAD_DIM)

            def one_block(block_items):
                return attend_block(block_items[0], block_items[1], block_items[2], key_rows, value_rows, positions, seq_segments, rel_bias)
            mixed_token_rows = lax.map(jax.checkpoint(one_block), (queries, positions.reshape(N_CTX, TOK_DEV), seq_segments.reshape(N_CTX, TOK_DEV)))
            mixed_token_rows = both_directions(mixed_token_rows.reshape(seq_len, MODEL_WIDTH))
            inner_output = both_directions(matrix_product(mixed_token_rows, down_own[:, 3 * ADAPTER_RANK:4 * ADAPTER_RANK]))
            branch_rows = low_back(matrix_product(mixed_token_rows, output_float) + ADAPTER_SCALE * matrix_product(inner_output, owned_up_weight[3]))
            return seq_tokens + branch_rows
        hidden = lax.map(jax.checkpoint(one_sequence), (token_values.reshape(SEQS, seq_len, MODEL_WIDTH), adapter_pick, segment_keys)).reshape(row_total, MODEL_WIDTH)
        normalized_second = both_directions(rms_scale(hidden, gain_rows[1]))
        token_masks = row_masks[:row_total]
        router_down = down_all[:, :, 4 * ADAPTER_RANK:5 * ADAPTER_RANK].transpose(1, 0, 2).reshape(MODEL_WIDTH, ADAPTER_COUNT * ADAPTER_RANK)
        inner_router_rows = both_directions(matrix_product(normalized_second, router_down) * token_masks)
        router_logits = low_back(matrix_product(normalized_second, router_weight_float) + ADAPTER_SCALE * matrix_product(inner_router_rows, router_up_weights.reshape(ADAPTER_COUNT * ADAPTER_RANK, EXPERT_COUNT)))
        gate_rows = jax.nn.softmax(jnp.take_along_axis(router_logits, route_flat, axis=1), axis=-1)
        padded = jnp.concatenate([normalized_second, jnp.zeros((1, MODEL_WIDTH), jnp.float32)], axis=0)
        in_down = down_all[:, :, 5 * ADAPTER_RANK:].transpose(1, 0, 2).reshape(MODEL_WIDTH, ADAPTER_COUNT * ADAPTER_RANK)
        input_up_weight = ups_hidden[:, 0].reshape(ADAPTER_COUNT * ADAPTER_RANK, FF)
        out_down = ups_hidden[:, 1].reshape(ADAPTER_COUNT * ADAPTER_RANK, FF)
        output_up_weight = ups_model[:, 4].reshape(ADAPTER_COUNT * ADAPTER_RANK, MODEL_WIDTH)

        def one_expert(loop_items):
            first_matrix, second_matrix, sources = loop_items
            arrived_rows = padded[sources]
            arrived_masks = row_masks[sources]
            inner_input = both_directions(matrix_product(arrived_rows, in_down) * arrived_masks)
            before_rows = low_back(matrix_product(arrived_rows, first_matrix) + ADAPTER_SCALE * matrix_product(inner_input, input_up_weight))
            active_rows = both_directions(jax.nn.gelu(before_rows, approximate=True))
            inner_second = both_directions(matrix_product(active_rows, out_down.T) * arrived_masks)
            return both_directions(matrix_product(active_rows, second_matrix) + ADAPTER_SCALE * matrix_product(inner_second, output_up_weight))
        results = lax.map(jax.checkpoint(one_expert), (first_experts, second_experts, slot_source)).reshape(EXPERT_COUNT * expert_rows, MODEL_WIDTH)
        picked = results[destination].reshape(row_total, 2, MODEL_WIDTH)
        return hidden + lax.optimization_barrier(jnp.sum(gate_rows[:, :, None] * picked, axis=1))
    outputs, pullback = jax.vjp(forward, tokens.astype(jnp.float32).reshape(row_total, MODEL_WIDTH), adapters)
    input_grad, adapter_grad = pullback(cotangent.astype(jnp.float32).reshape(row_total, MODEL_WIDTH))
    new_first = BETA_ONE * first_moment + (1.0 - BETA_ONE) * adapter_grad
    new_second = BETA_TWO * second_moment + (1.0 - BETA_TWO) * adapter_grad * adapter_grad
    corrected = new_first / (1.0 - BETA_ONE ** STEP_NUM)
    denominator = jnp.sqrt(new_second / (1.0 - BETA_TWO ** STEP_NUM)) + ADAM_EPS
    new_adapters = adapters - LEARN_RATE * (corrected / denominator + WEIGHT_DECAY * adapters)
    return (outputs.astype(jnp.bfloat16).reshape(SEQS, N_CTX, TOK_DEV, MODEL_WIDTH), input_grad.reshape(SEQS, N_CTX, TOK_DEV, MODEL_WIDTH), new_adapters, new_first, new_second)
```

```python
import functools

import jax
import jax.numpy as jnp
import numpy as np
from jax import lax
from jax.experimental import pallas as pl
from jax.experimental.pallas import tpu as pltpu
from jax.sharding import PartitionSpec as P

MODEL_WIDTH = 768
HEADS = 12
HEAD_DIM = 64
FF = 3072
ADAPTER_RANK = 16
ADAPTER_COUNT = 8
STEP_NUM = 5


NORM_EPS = 1e-06
ADAPTER_SCALE = 2.0
MASKED = -1e30
BETA_ONE = 0.9
BETA_TWO = 0.999
LEARN_RATE = 0.05
WEIGHT_DECAY = 0.01
ADAM_EPS = 1e-08
VMEM_BYTES = 56 * 1024 * 1024
MESH = pl.DeviceIdType.MESH
SMALL_COST = pl.CostEstimate(flops=1, bytes_accessed=1, transcendentals=0)


def bucket_bounds():
    bounds = list(range(1, 16))
    for level_index in range(16):
        bounds.append(int(np.ceil(16.0 * 8.0 ** (level_index / 16.0) - 1e-09)))
    return bounds


def rms_scale(values, gain_row):
    return (
        values * lax.rsqrt(jnp.mean(values * values, axis=-1, keepdims=True) + NORM_EPS) * gain_row
    )


def matrix_multiply(former, latter):
    return jnp.dot(former, latter, preferred_element_type=jnp.float32)


def product_last(former, latter):
    return lax.dot_general(
        former,
        latter,
        (((former.ndim - 1,), (latter.ndim - 1,)), ((), ())),
        preferred_element_type=jnp.float32,
    )


def product_first(former, latter):
    return lax.dot_general(
        former, latter, (((0,), (0,)), ((), ())), preferred_element_type=jnp.float32
    )


LANES = 128
FAR_BUCKET = 31


def lane_ids():
    return lax.broadcasted_iota(jnp.int32, (1, LANES), 1)


def split_three(values):
    first = values.astype(jnp.bfloat16)
    rest = values - first.astype(jnp.float32)
    second = rest.astype(jnp.bfloat16)
    third = (rest - second.astype(jnp.float32)).astype(jnp.bfloat16)
    return (first, second, third)


def place_three(base, values, lane_mod, start):
    for step, part in enumerate(split_three(values)):
        base = jnp.where(lane_mod == start + step, part.astype(jnp.float32), base)
    return base


def key_place(block, n, h):
    return (block, pl.ds(0, h)) if block < n else (2 * n - 1 - block, pl.ds(h, h))


def fill_tables(bias_ref, out, turned):
    tile = (LANES, LANES)
    rows = bias_rows(bias_ref, turned)
    for head in range(HEADS):
        out[head, 0] = jnp.full(tile, MASKED, jnp.float32)
        for step in range(2):
            wide = jnp.broadcast_to(rows[step][head : head + 1, :], (LANES, 2 * LANES))
            out[head, step + 1] = pltpu.roll(wide, 0, 1, stride=1, stride_axis=0)[:, :LANES]
        out[head, 3] = jnp.zeros(tile, jnp.float32)


def bias_rows(bias_ref, turned):
    span = lax.broadcasted_iota(jnp.int32, (1, 2 * LANES), 1)
    far = bias_ref[:, FAR_BUCKET : FAR_BUCKET + 1]
    rows = []
    for step in range(2):
        if turned:
            distance = LANES * step + jnp.where(span < LANES, span, span - 2 * LANES)
        else:
            distance = LANES * step + jnp.where(span < LANES, -span, 2 * LANES - span)
        bucket = jnp.zeros(span.shape, jnp.int32)
        for threshold in bucket_bounds():
            bucket = bucket + jnp.where(distance >= threshold, 1, 0)
        picked = jnp.zeros((HEADS, 2 * LANES), jnp.float32)
        for index in range(bias_ref.shape[1]):
            picked = jnp.where(bucket == index, bias_ref[:, index : index + 1] - far, picked)
        rows.append(jnp.where(distance < 0, MASKED, picked))
    return rows


def near_tiles(table_ref, side, query_block, block, h, turned):
    per = h // LANES
    rows = []
    for outer in range(per):
        tiles = []
        for inner in range(per):
            query_tile, key_tile = (inner, outer) if turned else (outer, inner)
            gap = per * query_block + query_tile - (per * block + key_tile)
            tiles.append(table_ref[side, jnp.clip(gap, -1, 2) + 1])
        rows.append(jnp.concatenate(tiles, axis=1))
    return jnp.concatenate(rows, axis=0)


def attend_kernel(n, h, q_ref, k_ref, v_ref, qe_ref, ke_ref, far_ref, table_ref, o_ref, lse_ref):
    part = lax.axis_index("ctx")
    lane = lane_ids()
    lane_mod = lane % HEAD_DIM
    low = lane < HEAD_DIM
    for turn in range(2):
        spot = pl.ds(turn * h, h)
        query_block = part if turn == 0 else 2 * n - 1 - part
        count = n if turn == 0 else 2 * n
        outs, logs = [], []
        for side in range(2):
            mine = low if side == 0 else jnp.logical_not(low)
            extra = place_three(jnp.zeros((1, LANES), jnp.float32), far_ref[0, side : side + 1, :], lane_mod, 5)
            query = q_ref[spot, :].astype(jnp.float32) * HEAD_DIM ** (-0.5)
            query = jnp.where(mine, query, qe_ref[spot, :].astype(jnp.float32) + extra)
            query = query.astype(jnp.bfloat16)
            scores = []
            for block in range(count):
                owner, place = key_place(block, n, h)
                ahead = lax.rem(owner - part + n, n)
                key = jnp.where(mine, k_ref[ahead, 0, place, :], ke_ref[owner, place, :])
                one = product_last(query, key)
                if turn == 0 or block >= n - 1:
                    one = one + near_tiles(table_ref, side, query_block, block, h, False)
                scores.append(one)
            top = scores[0]
            for one in scores[1:]:
                top = jnp.maximum(top, one)
            top = jnp.max(top, axis=-1, keepdims=True)
            total = jnp.zeros((h, LANES), jnp.float32)
            for block in range(count):
                owner, place = key_place(block, n, h)
                ahead = lax.rem(owner - part + n, n)
                value = jnp.where(mine, v_ref[ahead, 0, place, :], jnp.ones((), jnp.bfloat16))
                weight = jnp.exp(scores[block] - top).astype(jnp.bfloat16)
                total = total + matrix_multiply(weight, value)
            spare = HEAD_DIM if side == 0 else 0
            sums = total[:, spare : spare + 1]
            outs.append(total / sums)
            logs.append(jnp.broadcast_to(top + jnp.log(sums), (h, LANES)))
        o_ref[spot, :] = jnp.where(low, outs[0], outs[1]).astype(o_ref.dtype)
        lse_ref[spot, :] = jnp.where(low, logs[1], logs[0])


def attend_back_pair(
    n, h, pair, pairs, q_ref, k_ref, v_ref, do_ref, o_ref, lse_ref, qe_ref, ke_ref, far_ref, table_ref,
    dq_ref, dkv_ref, other_ref, qx_ref, gx_ref, dq_sum, made_ref, send_sem, recv_sem,
):
    part = lax.axis_index("ctx")
    parity = lax.rem(pair, 2)

    def pass_on(turn, pair):
        slot = lax.rem(pair, 2)
        columns = pl.ds(pl.multiple_of(pair * LANES, LANES), LANES)
        return pltpu.make_async_remote_copy(
            src_ref=made_ref.at[slot, turn], dst_ref=other_ref.at[turn - 1, :, :, columns],
            send_sem=send_sem.at[slot, turn - 1], recv_sem=recv_sem.at[pair, turn - 1],
            device_id={"ctx": lax.rem(part + turn, n)}, device_id_type=MESH,
        )

    @pl.when(pair >= 2)
    def _():
        for turn in range(1, n):
            pass_on(turn, pair - 2).wait_send()

    lane = lane_ids()
    lane_mod = lane % HEAD_DIM
    low = lane < HEAD_DIM
    spare = jnp.where(lane_mod < 3, 1.0, 0.0).astype(jnp.bfloat16)
    both = do_ref[...].astype(jnp.float32) * o_ref[...].astype(jnp.float32)
    for side in range(2):
        mine = low if side == 0 else jnp.logical_not(low)
        extra = place_three(jnp.zeros((1, LANES), jnp.float32), far_ref[0, side : side + 1, :], lane_mod, 5)
        extra = place_three(qe_ref[...].astype(jnp.float32) + extra, -lse_ref[...], lane_mod, 8)
        query = q_ref[...].astype(jnp.float32) * HEAD_DIM ** (-0.5)
        qx_ref[side] = jnp.where(mine, query, extra).astype(jnp.bfloat16)
        dots = jnp.sum(jnp.where(mine, both, 0.0), axis=-1, keepdims=True)
        dots = jnp.broadcast_to(dots, both.shape)
        extra = place_three(jnp.zeros(both.shape, jnp.float32), -dots, lane_mod, 0)
        gx_ref[side] = jnp.where(mine, do_ref[...].astype(jnp.float32), extra).astype(jnp.bfloat16)
    dq_sum[...] = jnp.zeros_like(dq_sum)
    for block in range(2 * n):
        owner, place = key_place(block, n, h)
        ahead = lax.rem(owner - part + n, n)
        key_turned = jnp.transpose(k_ref[ahead, 0, place, :].astype(jnp.float32)).astype(jnp.bfloat16)
        key_grads, value_grads = [], []
        for side in range(2):
            mine = low if side == 0 else jnp.logical_not(low)
            key = jnp.where(mine, k_ref[ahead, 0, place, :], ke_ref[owner, place, :])
            value = jnp.where(mine, v_ref[ahead, 0, place, :], spare)
            key_grad = jnp.zeros((h, LANES), jnp.float32)
            value_grad = jnp.zeros((h, LANES), jnp.float32)
            for turn in range(2):
                if turn == 0 and block >= n:
                    continue
                spot = pl.ds(turn * h, h)
                query_block = part if turn == 0 else 2 * n - 1 - part
                query = qx_ref[side, spot, :]
                scores = product_last(key, query)
                if turn == 0 or block >= n - 1:
                    scores = scores + near_tiles(table_ref, side, query_block, block, h, True)
                prob = jnp.exp(scores)
                prob_grad = product_last(value, gx_ref[side, spot, :])
                score_grad = (prob * prob_grad).astype(jnp.bfloat16)
                value_grad = value_grad + matrix_multiply(prob.astype(jnp.bfloat16), do_ref[spot, :])
                key_grad = key_grad + matrix_multiply(score_grad, query)
                dq_sum[side, :, spot] += matrix_multiply(key_turned, score_grad)
            key_grads.append(key_grad)
            value_grads.append(value_grad)
        key_grad = jnp.where(low, key_grads[0], key_grads[1])
        made_ref[parity, ahead, 0, place, :] = key_grad.astype(made_ref.dtype)
        value_grad = jnp.where(low, value_grads[0], value_grads[1])
        made_ref[parity, ahead, 1, place, :] = value_grad.astype(made_ref.dtype)
    for turn in range(1, n):
        pass_on(turn, pair).start()
    dkv_ref[...] = made_ref[parity, 0]
    upper = lax.broadcasted_iota(jnp.int32, (LANES, 1), 0) < HEAD_DIM
    grads = jnp.where(upper, dq_sum[0], dq_sum[1]) * HEAD_DIM ** (-0.5)
    dq_ref[...] = jnp.transpose(grads).astype(dq_ref.dtype)

    @pl.when(pair == pairs - 1)
    def _():
        for turn in range(1, n):
            for last in (pairs - 2, pairs - 1):
                pass_on(turn, last).wait_send()
            for one in range(HEADS // 2):
                pass_on(turn, one).wait_recv()


def pass_pieces(pieces_ref, sum_ref, landed, mirror_out, mirror_in, own_sem, send_sem, recv_sem, mirror_sem):
    me = lax.axis_index("exp")
    count = pieces_ref.shape[0]
    half = count // 2
    base = lax.div(me, half) * half
    here = lax.rem(me, half)
    mirror = lax.rem(me + half, count)

    def to(peer, slot):
        return [
            pltpu.make_async_remote_copy(
                src_ref=pieces_ref.at[lax.rem(base + peer + half * k, count)], dst_ref=landed.at[k, slot],
                send_sem=send_sem.at[k, peer], recv_sem=recv_sem.at[k, slot],
                device_id={"exp": base + peer}, device_id_type=MESH,
            )
            for k in range(2)
        ]

    own = [
        pltpu.make_async_copy(pieces_ref.at[lax.rem(me + half * k, count)], landed.at[k, here], own_sem.at[k])
        for k in range(2)
    ]
    across = pltpu.make_async_remote_copy(
        src_ref=mirror_out, dst_ref=mirror_in, send_sem=mirror_sem.at[0], recv_sem=mirror_sem.at[1],
        device_id={"exp": mirror}, device_id_type=MESH,
    )

    def total(k):
        total = landed[k, 0].astype(jnp.float32)
        for source in range(1, half):
            total = total + landed[k, source].astype(jnp.float32)
        return total

    def begin():
        for copy in own:
            copy.start()

        def push(turn, carry):
            for copy in to(lax.rem(here + turn, half), here):
                copy.start()
            return carry

        lax.fori_loop(1, half, push, 0)

    def middle():
        for copy in own:
            copy.wait()

        def settle(turn, carry):
            peer = lax.rem(here + turn, half)
            for copy in to(peer, peer):
                copy.wait_recv()
            for copy in to(peer, here):
                copy.wait_send()
            return carry

        lax.fori_loop(1, half, settle, 0)
        mirror_out[...] = total(1).astype(mirror_out.dtype)
        across.start()

    def end():
        across.wait()
        sum_ref[...] = (total(0) + mirror_in[...].astype(jnp.float32)).astype(sum_ref.dtype)

    return begin, middle, end


def pieces_scratch(pieces):
    one, half = pieces.shape[1:], pieces.shape[0] // 2
    dma = pltpu.SemaphoreType.DMA
    return [
        pltpu.VMEM((2, half) + one, pieces.dtype),
        pltpu.VMEM(one, pieces.dtype),
        pltpu.VMEM(one, pieces.dtype),
        dma((2,)),
        dma((2, half)),
        dma((2, half)),
        dma((2,)),
    ]


def attend_back_kernel(n, h, *refs):
    part = lax.axis_index("ctx")

    @pl.when(pl.program_id(0) == 0)
    def _():
        barrier = pltpu.get_barrier_semaphore()
        for turn in range(1, n):
            core = lax.rem(part + turn, n)
            pl.semaphore_signal(barrier, inc=1, device_id={"ctx": core}, device_id_type=MESH)
        pl.semaphore_wait(barrier, n - 1)

    attend_back_pair(n, h, pl.program_id(0), pl.num_programs(0), *refs)


def attend_back(query, kv, out_grad, out, lse, qe, ke, far, turned):
    rows = query.shape[0]
    n = kv.shape[0]
    every = n * rows
    h = rows // 2
    pairs = HEADS // 2
    own = pl.BlockSpec((rows, LANES), lambda i: (0, i))
    return pl.pallas_call(
        functools.partial(attend_back_kernel, n, h),
        grid=(pairs,),
        in_specs=[
            own,
            pl.BlockSpec((n, 1, rows, LANES), lambda i: (0, 0, 0, i)),
            pl.BlockSpec((n, 1, rows, LANES), lambda i: (0, 1, 0, i)),
            own,
            own,
            own,
            pl.BlockSpec((rows, LANES), lambda i: (0, 0)),
            pl.BlockSpec((n, rows, LANES), lambda i: (0, 0, 0)),
            pl.BlockSpec((1, 2, LANES), lambda i: (i, 0, 0)),
            pl.BlockSpec((2, 4, LANES, LANES), lambda i: (i, 0, 0, 0)),
        ],
        out_specs=[own, pl.BlockSpec((2, rows, LANES), lambda i: (0, 0, i)), pl.BlockSpec(memory_space=pl.ANY)],
        out_shape=[
            jax.ShapeDtypeStruct((rows, MODEL_WIDTH), jnp.bfloat16),
            jax.ShapeDtypeStruct((2, rows, MODEL_WIDTH), jnp.bfloat16),
            jax.ShapeDtypeStruct((n - 1, 2, rows, MODEL_WIDTH), jnp.bfloat16),
        ],
        scratch_shapes=[
            pltpu.VMEM((2, rows, LANES), jnp.bfloat16),
            pltpu.VMEM((2, rows, LANES), jnp.bfloat16),
            pltpu.VMEM((2, LANES, rows), jnp.float32),
            pltpu.VMEM((2, n, 2, rows, LANES), jnp.bfloat16),
            pltpu.SemaphoreType.DMA((2, n - 1)),
            pltpu.SemaphoreType.DMA((pairs, n - 1)),
        ],
        compiler_params=pltpu.CompilerParams(
            vmem_limit_bytes=VMEM_BYTES, collective_id=6, has_side_effects=True
        ),
        cost_estimate=SMALL_COST,
        name="attend_back",
    )(query, kv, kv, out_grad, out, lse, qe, ke, far, turned)


def segment_columns(row):
    wide = jnp.broadcast_to(row.astype(jnp.float32), (LANES, LANES))
    return jnp.transpose(wide).astype(jnp.int32)


def fill_segments(n, h, segments_ref, qe_ref, ke_ref):
    part = lax.axis_index("ctx")
    lane_mod = lane_ids() % HEAD_DIM
    documents = lane_mod < 5
    ones = jnp.where((lane_mod >= 5) & (lane_mod < 11), 1.0, 0.0)
    for block in range(2 * n):
        owner = block if block < n else 2 * n - 1 - block
        first = 0 if block < n else h
        for step in range(0, h, LANES):
            column = segment_columns(segments_ref[:, block * h + step : block * h + step + LANES])
            side = jnp.where(documents & (column != lane_mod), MASKED, ones)
            ke_ref[owner, first + step : first + step + LANES, :] = side.astype(jnp.bfloat16)
    for turn in range(2):
        block = part if turn == 0 else 2 * n - 1 - part
        for step in range(0, h, LANES):
            spot = pl.ds(pl.multiple_of(block * h + step, LANES), LANES)
            column = segment_columns(segments_ref[:, spot])
            side = jnp.where(documents & (column == lane_mod), 1.0, 0.0)
            qe_ref[turn * h + step : turn * h + step + LANES, :] = side.astype(jnp.bfloat16)


ROW_BLOCK = 256
FF_BLOCK = 512
GELU_SLOPE = float(np.sqrt(2.0 / np.pi))
GELU_CUBE = 0.044715


def group_mask(first, last):
    lane = lane_ids()
    return (lane >= first * ADAPTER_RANK) & (lane < last * ADAPTER_RANK)


def keep_group(values, first, last):
    return jnp.where(group_mask(first, last), values, 0.0).astype(jnp.bfloat16)


def send_rows(dest_ref, rows, out_ref):
    count = rows.shape[0]
    for start in range(0, out_ref.shape[0], ROW_BLOCK):
        size = min(ROW_BLOCK, out_ref.shape[0] - start)
        slot = lax.broadcasted_iota(jnp.int32, (size, count), 0) + start
        hot = (slot == dest_ref[0:1, :]) | (slot == dest_ref[1:2, :])
        hot = jnp.where(hot, 1.0, 0.0).astype(jnp.bfloat16)
        out_ref[start : start + size, :] = matrix_multiply(hot, rows).astype(out_ref.dtype)


def find_routes(capacity, rows_ref, grad_ref, routes_ref, dest_rows_ref, dest_cols_ref, out_ref):
    count = grad_ref.shape[0]
    wide = jnp.concatenate([rows_ref[...].astype(jnp.float32), jnp.zeros((LANES - 2, count), jnp.float32)], axis=0)
    routes_ref[...] = jnp.transpose(wide)[:, :2].astype(jnp.int32)
    experts = out_ref.shape[0] // capacity
    down = lax.broadcasted_iota(jnp.int32, (count, count), 0)
    across = lax.broadcasted_iota(jnp.int32, (count, count), 1)
    after = jnp.where(across < down, 1.0, 0.0).astype(jnp.bfloat16)
    ids = lax.broadcasted_iota(jnp.int32, (count, LANES), 1)
    hots = [jnp.where(ids == routes_ref[:, k : k + 1], 1.0, 0.0) for k in range(2)]
    ranks = matrix_multiply(after, (hots[0] + hots[1]).astype(jnp.bfloat16))
    wide = jnp.zeros((count, LANES), jnp.float32)
    for k in range(2):
        slot = jnp.sum(hots[k] * ranks, axis=1, keepdims=True).astype(jnp.int32)
        dest = routes_ref[:, k : k + 1] * capacity + slot
        dest_cols_ref[:, k : k + 1] = dest
        wide = jnp.where(ids == k, dest.astype(jnp.float32), wide)
    dest_rows_ref[...] = jnp.transpose(wide)[:2].astype(jnp.int32)
    send_rows(dest_rows_ref, grad_ref[...], out_ref)


def whole(shape):
    return jax.ShapeDtypeStruct(shape[0], shape[1])


def run(kernel, name, outs, *operands, scratch=(), outside=0, **params):
    vmem, anywhere = pl.BlockSpec(memory_space=pltpu.VMEM), pl.BlockSpec(memory_space=pl.ANY)
    return pl.pallas_call(
        kernel,
        in_specs=[vmem] * (len(operands) - outside) + [anywhere] * outside,
        out_specs=[vmem] * len(outs),
        out_shape=[whole(shape) for shape in outs],
        scratch_shapes=list(scratch),
        compiler_params=pltpu.CompilerParams(vmem_limit_bytes=VMEM_BYTES, **params),
        cost_estimate=SMALL_COST,
        name=name,
    )(*operands)


def owners_of(share, cuts):
    def has_own(owner):
        return (owner * share < cuts[1]) | ((owner + 1) * share > cuts[2])

    def owner_of(row, end):
        return lax.div(cuts[1] + row * FF + end * (FF - 1), share)

    return has_own, owner_of


def by_parity(owner, cores):
    return (lax.axis_index("ctx") == owner % 2) if cores == 2 else True


def fetch_parts(
    share, tiles, cuts, halved, capacity, adapters_ref, pick_ref, bias_ref, route_rows_ref, grad_ref,
    own_in, home_ref, table_ref, routes_ref, dest_rows_ref, dest_cols_ref, out_ref, mask_ref,
    padded_ref, by_adapter, sent, home_out, home_in, own_send, own_recv, relay_send, relay_recv, local_sem,
    home_send, home_recv,
):
    part, me = lax.axis_index("ctx"), lax.axis_index("exp")
    cores, experts = lax.axis_size("ctx"), lax.axis_size("exp")
    window = sent.shape[1]
    per_row = FF // LANES
    has_own, owner_of = owners_of(share, cuts)

    padded_ref[...] = jnp.zeros_like(padded_ref)
    offset = lax.rem(me * share, LANES)
    lane = lane_ids()
    held = jnp.zeros((ADAPTER_COUNT, LANES), jnp.float32)
    for tile in range(tiles):
        slab = adapters_ref[:, tile * LANES : min((tile + 1) * LANES, share)] if tile * LANES < share else held * 0.0
        if slab.shape[1] < LANES:
            rest = jnp.zeros((ADAPTER_COUNT, LANES - slab.shape[1]), jnp.float32)
            slab = jnp.concatenate([slab, rest], axis=1)
        slab = pltpu.roll(slab, offset, 1)
        one = jnp.where(lane < offset, held, slab)
        padded_ref[:, (per_row + tile) * LANES : (per_row + tile + 1) * LANES] = one
        by_adapter[pl.ds(tile, ADAPTER_COUNT, stride=window), :] = one
        held = slab
    for tile in range(tiles, window):
        by_adapter[pl.ds(tile, ADAPTER_COUNT, stride=window), :] = jnp.zeros((ADAPTER_COUNT, LANES), jnp.float32)
    for peer in range(experts):
        mask_ref[peer] = jnp.where(lane % ADAPTER_COUNT == pick_ref[peer], 1.0, 0.0)
        chosen = by_adapter[:window, :]
        for adapter in range(1, ADAPTER_COUNT):
            rows = by_adapter[adapter * window : (adapter + 1) * window, :]
            chosen = jnp.where(pick_ref[peer] == adapter, rows, chosen)
        sent[peer] = chosen.astype(jnp.bfloat16)

    def own_copy(peer, slot):
        return pltpu.make_async_remote_copy(
            src_ref=sent.at[peer], dst_ref=own_in.at[slot], send_sem=own_send.at[peer],
            recv_sem=own_recv.at[slot], device_id={"exp": peer}, device_id_type=MESH,
        )

    def relay(owner):
        return pltpu.make_async_remote_copy(
            src_ref=own_in.at[owner], dst_ref=own_in.at[owner], send_sem=relay_send.at[owner],
            recv_sem=relay_recv.at[owner], device_id={"ctx": 1 - part}, device_id_type=MESH,
        )

    handled = has_own(me) & (by_parity(me, cores) if cores == 2 else has_own(me))

    def each_peer(action):
        def one(turn, carry):
            action(lax.rem(me + turn, experts))
            return carry

        lax.fori_loop(1, experts, one, 0)

    kept = pltpu.make_async_copy(sent.at[me], own_in.at[me], local_sem.at[0])

    @pl.when(handled)
    def _():
        each_peer(lambda peer: own_copy(peer, me).start())
        kept.start()

    cut = FF // 2

    def home_pack(row, peer):
        tile = per_row + cuts[1] // LANES + row * per_row - lax.div(me * share, LANES)
        halves = [padded_ref[:, pl.ds(pl.multiple_of(tile * LANES + k * cut, LANES), cut)] for k in range(2)]
        home_out[peer] = jnp.concatenate(halves, axis=0).astype(jnp.bfloat16)

    def home_copy(row, peer, slot):
        return pltpu.make_async_remote_copy(
            src_ref=home_out.at[peer], dst_ref=home_in.at[slot], send_sem=home_send.at[peer],
            recv_sem=home_recv.at[slot], device_id={"exp": peer}, device_id_type=MESH,
        )

    def each_home(action):
        def one(peer, carry):
            row = part * experts + peer
            low, high = owner_of(row, 0), owner_of(row, 1)

            @pl.when((low == me) & (peer != me))
            def _():
                action(home_copy(row, peer, 0))

            @pl.when((high == me) & (low != me) & (peer != me))
            def _():
                action(home_copy(row, peer, 1))

            return carry

        lax.fori_loop(0, experts, one, 0)

    if halved:

        def pack(peer, carry):
            row = part * experts + peer

            @pl.when((owner_of(row, 0) == me) | (owner_of(row, 1) == me))
            def _():
                home_pack(row, peer)

            return carry

        lax.fori_loop(0, experts, pack, 0)
        each_home(lambda copy: copy.start())
        my_row = part * experts + me
        my_low, my_high = owner_of(my_row, 0), owner_of(my_row, 1)
        for slot, owner, needed in ((0, my_low, True), (1, my_high, my_high != my_low)):

            @pl.when(needed & (owner == me))
            def _():
                pltpu.make_async_copy(home_out.at[me], home_in.at[slot], local_sem.at[1 + slot]).start()

    find_routes(capacity, route_rows_ref, grad_ref, routes_ref, dest_rows_ref, dest_cols_ref, out_ref)
    if cores == 2:
        fill_tables(bias_ref, table_ref, False)

    def arrive():
        for owner in range(experts):
            if has_own(owner):
                here = by_parity(owner, cores)

                @pl.when((me != owner) & here)
                def _():
                    own_copy(owner, owner).wait_recv()

                if cores == 2:

                    @pl.when((me == owner) & here)
                    def _():
                        kept.wait()

                    @pl.when(here)
                    def _():
                        relay(owner).start()

        if cores != 2:

            @pl.when(has_own(me))
            def _():
                kept.wait()

        else:
            for owner in range(experts):
                if has_own(owner):
                    here = by_parity(owner, cores)

                    @pl.when(jnp.logical_not(here))
                    def _():
                        relay(owner).wait_recv()

    def make_home():
        if halved:
            for slot, owner, needed in ((0, my_low, True), (1, my_high, my_high != my_low)):

                @pl.when(needed & (owner == me))
                def _():
                    pltpu.make_async_copy(home_out.at[me], home_in.at[slot], local_sem.at[1 + slot]).wait()

                @pl.when(needed & (owner != me))
                def _():
                    home_copy(my_row, me, slot).wait_recv()

            row = home_in[0].astype(jnp.float32)
            row = row + jnp.where(my_high != my_low, home_in[1].astype(jnp.float32), 0.0)
            home_ref[...] = row.astype(jnp.bfloat16)

    def finish():
        if halved:
            each_home(lambda copy: copy.wait_send())

        @pl.when(handled)
        def _():
            each_peer(lambda peer: own_copy(peer, me).wait_send())

        if cores == 2:
            for owner in range(experts):
                if has_own(owner):

                    @pl.when(by_parity(owner, cores))
                    def _():
                        relay(owner).wait_send()

    return arrive, make_home, finish


SOURCE_GROUP = 4


def forward_kernel(
    share, tiles, cuts, halved, capacity, adapters_ref, pick_ref, tokens_ref, grad_ref, gain_ref, bias_ref, segments_ref,
    router_in_ref, route_rows_ref, weight_hbm, out_weight_hbm,
    hidden_all, routes_ref, dest_rows_ref, dest_cols_ref, mask_ref,
    q_hbm, kv_hbm, xn_hbm, u_ref, own_down_ref, own_up_ref, own_router_ref, turned_hbm, o_hbm, lse_hbm,
    qe_ref, ke_ref, far_ref, router_ref, hidden_ref, xn_two_ref, w_ref, ur_ref, gates_ref, gate_slots_ref, side_ref,
    rows_ref, came_hbm,
    q_ref, kv_ref, xn_ref, o_ref, lse_ref, kv_own, table_ref, turned_ref, weight_ref, out_weight_ref, flat, down_wide,
    load_sem, store_sem, local_sem, kv_send, kv_recv, row_send, row_recv, sent_rows, own_in,
    home_ref, hidden_rows, hidden_came, hidden_send, hidden_recv, hidden_sem, *fetching,
):
    part, me = lax.axis_index("ctx"), lax.axis_index("exp")
    cores, experts = lax.axis_size("ctx"), lax.axis_size("exp")
    has_own, _ = owners_of(share, cuts)
    if cores > 2:
        turned_ref = table_ref
    loads = [
        pltpu.make_async_copy(source, target, load_sem.at[i])
        for i, (source, target) in enumerate(
            ((weight_hbm, weight_ref), (out_weight_hbm, out_weight_ref))
        )
    ]
    for load in loads:
        load.start()
    barrier = pltpu.get_barrier_semaphore()

    def greet(turn, carry):
        peer = lax.rem(me + turn, experts)
        pl.semaphore_signal(barrier, inc=1, device_id={"exp": peer}, device_id_type=MESH)
        return carry

    lax.fori_loop(1, experts, greet, 0)
    for turn in range(1, cores):
        core = lax.rem(part + turn, cores)
        pl.semaphore_signal(barrier, inc=1, device_id={"ctx": core}, device_id_type=MESH)
    pl.semaphore_wait(barrier, experts + cores - 2)

    def row_copy(peer, slot):
        return pltpu.make_async_remote_copy(
            src_ref=sent_rows.at[pl.ds(pl.multiple_of(peer * capacity, 16), capacity)], dst_ref=came_hbm.at[slot], send_sem=row_send.at[peer],
            recv_sem=row_recv.at[slot], device_id={"exp": peer}, device_id_type=MESH,
        )

    own_rows = pltpu.make_async_copy(
        sent_rows.at[pl.ds(pl.multiple_of(me * capacity, 16), capacity)], came_hbm.at[me], local_sem.at[2]
    )

    def push_grads():
        own_rows.start()
        push_rows(me, experts, lambda peer: row_copy(peer, me).start())

    arrive, make_home, finish = fetch_parts(
        share, tiles, cuts, halved, capacity, adapters_ref, pick_ref, bias_ref, route_rows_ref, grad_ref,
        own_in, home_ref, table_ref, routes_ref, dest_rows_ref, dest_cols_ref, sent_rows, mask_ref, *fetching
    )
    xn_ref[...] = rms_scale(tokens_ref[...].astype(jnp.float32), gain_ref[0:1, :]).astype(jnp.bfloat16)
    if halved:
        make_home()
        hidden_begin, hidden_relay, hidden_cross, hidden_end = pass_hidden(
            home_ref, hidden_all, hidden_rows, hidden_came, hidden_send, hidden_recv, hidden_sem
        )
        hidden_begin()
        arrive()
        hidden_relay()
    else:
        hidden_all[...] = jnp.zeros_like(hidden_all)
        arrive()
    push_grads()

    flat[...] = jnp.zeros_like(flat)
    for owner in range(experts):
        if has_own(owner):
            first = owner * share // LANES
            rows = slice(first, first + tiles)
            flat[rows, :] = flat[rows, :] + own_in[owner].astype(jnp.float32)[:tiles]
    columns = 6 * ADAPTER_RANK
    quarter = MODEL_WIDTH // 4
    rows = [flat[pl.ds(step, quarter, stride=3), :] for step in range(3)]
    blank = jnp.zeros((quarter, LANES - columns), jnp.float32)
    for step in range(4):
        tile, place = divmod(step * columns, LANES)
        pieces = [rows[tile][:, place : place + columns]]
        if place + columns > LANES:
            pieces.append(rows[tile + 1][:, : place + columns - LANES])
        down_wide[pl.ds(step, quarter, stride=4), :] = jnp.concatenate(pieces + [blank], axis=1)
    own_down_ref[...] = down_wide[...].astype(jnp.bfloat16)
    per_model = MODEL_WIDTH // LANES
    empty = jnp.zeros((LANES - 5 * ADAPTER_RANK, LANES), jnp.float32)
    for step in range(per_model):
        one = flat[pl.ds(cuts[0] // LANES + step, 5 * ADAPTER_RANK, stride=per_model), :]
        one = jnp.concatenate([one, empty], axis=0).astype(jnp.bfloat16)
        own_up_ref[:, step * LANES : (step + 1) * LANES] = one

    u_ref[...] = keep_group(matrix_multiply(xn_ref[...], own_down_ref[...]), 0, 3)
    loads[0].wait()

    def made(group):
        inner = jnp.where(group_mask(group, group + 1), u_ref[...], jnp.zeros((), jnp.bfloat16))
        spot = slice(group * MODEL_WIDTH, (group + 1) * MODEL_WIDTH)
        base = matrix_multiply(xn_ref[...], weight_ref[:, spot])
        return (base + ADAPTER_SCALE * matrix_multiply(inner, own_up_ref[...])).astype(jnp.bfloat16)

    def kv_copy(which, turn):
        return pltpu.make_async_remote_copy(
            src_ref=kv_own.at[which], dst_ref=kv_ref.at[cores - turn, which],
            send_sem=kv_send.at[which, turn - 1], recv_sem=kv_recv.at[which, turn - 1],
            device_id={"ctx": lax.rem(part + turn, cores)}, device_id_type=MESH,
        )

    for which in range(2):
        kv_own[which] = made(which + 1)
        for turn in range(1, cores):
            kv_copy(which, turn).start()
        pltpu.make_async_copy(kv_own.at[which], kv_ref.at[0, which], local_sem.at[which]).start()
    q_ref[...] = made(0)
    stores = [
        pltpu.make_async_copy(source, target, store_sem.at[i])
        for i, (source, target) in enumerate(
            ((q_ref, q_hbm), (xn_ref, xn_hbm), (turned_ref, turned_hbm), (kv_ref, kv_hbm), (o_ref, o_hbm), (lse_ref, lse_hbm))
        )
    ]
    stores[0].start()
    stores[1].start()
    fill_tables(bias_ref, turned_ref, True)
    stores[2].start()
    if cores > 2:
        stores.pop(2).wait()
        fill_tables(bias_ref, table_ref, False)
    lane = lane_ids()
    router = []
    for row in range(ADAPTER_RANK):
        tile, place = divmod(row * experts, LANES)
        one = flat[cuts[2] // LANES + tile : cuts[2] // LANES + tile + 1, :]
        one = pltpu.roll(one, LANES - place, 1) if place else one
        router.append(jnp.where(lane < experts, one, 0.0))
    above = jnp.zeros((4 * ADAPTER_RANK, LANES), jnp.float32)
    below = jnp.zeros((LANES - 5 * ADAPTER_RANK, LANES), jnp.float32)
    own_router_ref[...] = jnp.concatenate([above] + router + [below], axis=0).astype(jnp.bfloat16)
    wide = jnp.zeros((LANES - experts, MODEL_WIDTH), jnp.float32)
    wide = jnp.concatenate([router_in_ref[...].astype(jnp.float32), wide], axis=0)
    router_ref[...] = jnp.transpose(wide).astype(jnp.bfloat16)
    half = tokens_ref.shape[0] // 2
    fill_segments(cores, half, segments_ref, qe_ref, ke_ref)
    far = jnp.broadcast_to(bias_ref[:, FAR_BUCKET : FAR_BUCKET + 1], (HEADS, LANES))
    for pair in range(HEADS // 2):
        far_ref[pair] = far[2 * pair : 2 * pair + 2]
    for which in range(2):
        for turn in range(1, cores):
            kv_copy(which, turn).wait()
        pltpu.make_async_copy(kv_own.at[which], kv_ref.at[0, which], local_sem.at[which]).wait()
    stores[-3].start()

    def attend(pair, carry):
        spot = pl.ds(pl.multiple_of(pair * LANES, LANES), LANES)
        attend_kernel(
            cores, half, q_ref.at[:, spot], kv_ref.at[:, pl.ds(0, 1), :, spot], kv_ref.at[:, pl.ds(1, 1), :, spot],
            qe_ref, ke_ref, far_ref.at[pl.ds(pair, 1)], table_ref.at[pl.ds(2 * pair, 2)],
            o_ref.at[:, spot], lse_ref.at[:, spot],
        )
        return carry

    lax.fori_loop(0, HEADS // 2, attend, 0)
    stores[-2].start()
    stores[-1].start()
    if halved:
        hidden_cross()
    loads[1].wait()
    after_kernel(
        capacity, o_ref, tokens_ref, grad_ref, out_weight_ref, own_down_ref, own_up_ref, gain_ref, router_ref,
        own_router_ref, routes_ref, dest_rows_ref, dest_cols_ref,
        hidden_ref, xn_two_ref, w_ref, ur_ref, gates_ref, gate_slots_ref, side_ref, rows_ref,
    )
    own_rows.wait()

    def settle(turn, carry):
        peer = lax.rem(me + turn, experts)
        row_copy(peer, peer).wait_recv()
        row_copy(peer, me).wait_send()
        return carry

    lax.fori_loop(1, experts, settle, 0)
    finish()
    if halved:
        hidden_end()
    for store in stores:
        store.wait()


def push_rows(me, experts, action, orders=None):
    groups = experts // SOURCE_GROUP
    count = groups if orders is None else len(orders)

    def one(step, carry):
        turn = lax.rem(step + lax.axis_index("ctx") * (count // 2), count)
        if orders is None:
            order = lax.rem(turn + groups // 2, groups)
        else:
            order = orders[0]
            for place in range(1, count):
                order = jnp.where(turn == place, orders[place], order)
        lane = lax.rem(lax.div(step, count) + me, SOURCE_GROUP)
        peer = paired(order, lax.div(me, SOURCE_GROUP), groups) * SOURCE_GROUP + lane

        @pl.when(peer != me)
        def _():
            action(peer)

        return carry

    lax.fori_loop(0, count * SOURCE_GROUP, one, 0)


def forward(
    share, tiles, cuts, halved, capacity, cores, experts, adapters, pick, tokens, grads, gains, bias, segments, router,
    routes, weight, out_weight,
):
    rows = tokens.shape[0]
    window = -(-tiles // 16) * 16
    piece = (2 * ADAPTER_COUNT, FF // 2)
    table = (HEADS, 4, LANES, LANES)
    length = -(-max(share * owner // LANES + window for owner in range(experts)) // 16) * 16
    bf16, f32 = jnp.bfloat16, jnp.float32
    vmem, anywhere = pl.BlockSpec(memory_space=pltpu.VMEM), pl.BlockSpec(memory_space=pl.ANY)
    dma = pltpu.SemaphoreType.DMA
    model, lanes = (rows, MODEL_WIDTH), (rows, LANES)
    kv = (cores, 2, rows, MODEL_WIDTH)
    outs = [
        ((2, LANES, FF) if halved else piece, bf16, vmem),
        ((rows, 2), jnp.int32, vmem),
        ((2, rows), jnp.int32, vmem),
        ((rows, 2), jnp.int32, vmem),
        ((experts, 1, LANES), f32, vmem),
        (model, bf16, anywhere),
        (kv, bf16, anywhere),
        (model, bf16, anywhere),
        (lanes, bf16, vmem),
        ((MODEL_WIDTH, LANES), bf16, vmem),
        ((LANES, MODEL_WIDTH), bf16, vmem),
        ((LANES, LANES), bf16, vmem),
        (table, f32, anywhere),
        (model, bf16, anywhere),
        (model, f32, anywhere),
        (lanes, bf16, vmem),
        ((cores, rows, LANES), bf16, vmem),
        ((HEADS // 2, 2, LANES), f32, vmem),
        ((MODEL_WIDTH, LANES), bf16, vmem),
        (model, f32, vmem),
        (model, bf16, vmem),
        (lanes, bf16, vmem),
        (lanes, bf16, vmem),
        (lanes, f32, vmem),
        ((experts, 1, LANES), f32, vmem),
        ((experts, 2 * ADAPTER_RANK, LANES), bf16, vmem),
        ((experts * capacity, MODEL_WIDTH), bf16, vmem),
        ((experts, capacity, MODEL_WIDTH), bf16, anywhere),
    ]
    return pl.pallas_call(
        functools.partial(forward_kernel, share, tiles, cuts, halved, capacity),
        in_specs=[vmem, pl.BlockSpec(memory_space=pltpu.SMEM)] + [vmem] * 7 + [anywhere] * 2,
        out_specs=[spec for _, _, spec in outs],
        out_shape=[whole(shape) for shape in outs],
        scratch_shapes=[
            pltpu.VMEM(model, bf16),
            pltpu.VMEM(kv, bf16),
            pltpu.VMEM(model, bf16),
            pltpu.VMEM(model, bf16),
            pltpu.VMEM(model, f32),
            pltpu.VMEM(kv[1:], bf16),
            pltpu.VMEM(table, f32),
            pltpu.VMEM(table if cores == 2 else (1, LANES), f32),
            pltpu.VMEM(weight.shape, bf16),
            pltpu.VMEM(out_weight.shape, bf16),
            pltpu.VMEM((length, LANES), f32),
            pltpu.VMEM((MODEL_WIDTH, LANES), f32),
            dma((2,)),
            dma((6,)),
            dma((3,)),
            dma((2, cores - 1)),
            dma((2, cores - 1)),
            dma((experts,)),
            dma((experts,)),
            pltpu.VMEM((experts * capacity, MODEL_WIDTH), bf16),
            pltpu.VMEM((experts, window, LANES), bf16),
            pltpu.VMEM(piece if halved else (1, LANES), bf16),
            pltpu.VMEM((experts,) + piece if halved else (1, LANES), bf16),
            pltpu.VMEM((experts,) + piece if halved else (1, LANES), bf16),
            dma((2, experts)),
            dma((experts,)),
            dma((3,)),
            pltpu.VMEM((ADAPTER_COUNT, (2 * (FF // LANES) + window) * LANES), f32),
            pltpu.VMEM((ADAPTER_COUNT * window, LANES), f32),
            pltpu.VMEM((experts, window, LANES), bf16),
            pltpu.VMEM((experts,) + piece if halved else (1, LANES), bf16),
            pltpu.VMEM((2,) + piece if halved else (1, LANES), bf16),
            dma((experts,)),
            dma((experts,)),
            dma((experts,)),
            dma((experts,)),
            dma((3,)),
            dma((experts,)),
            dma((2,)),
        ],
        compiler_params=pltpu.CompilerParams(
            vmem_limit_bytes=VMEM_BYTES if cores <= 2 else VMEM_BYTES + (6 << 20), collective_id=2, has_side_effects=True
        ),
        cost_estimate=SMALL_COST,
        name="forward",
    )(adapters, pick, tokens, grads, gains, bias, segments, router, routes, weight, out_weight)


def after_kernel(
    capacity, o_ref, tokens_ref, grad_ref, weight_ref, down_ref, up_ref, gain_ref, router_ref, router_up_ref,
    route_cols_ref, dest_rows_ref, dest_cols_ref,
    hidden_ref, xn_ref, w_ref, ur_ref, gates_ref, gate_slots_ref, side_ref, out_ref,
):
    mixed = o_ref[...]
    w_ref[...] = keep_group(matrix_multiply(mixed, down_ref[...]), 3, 4)
    branch = matrix_multiply(mixed, weight_ref[...])
    branch = branch + ADAPTER_SCALE * matrix_multiply(w_ref[...], up_ref[...])
    hidden = tokens_ref[...].astype(jnp.float32) + branch
    hidden_ref[...] = hidden
    xn_ref[...] = rms_scale(hidden, gain_ref[1:2, :]).astype(jnp.bfloat16)
    send_rows(dest_rows_ref, xn_ref[...], out_ref)
    normed = xn_ref[...]
    inner = matrix_multiply(normed, down_ref[...])
    ur_ref[...] = keep_group(inner, 4, 5)
    logits = matrix_multiply(normed, router_ref[...])
    logits = logits + ADAPTER_SCALE * matrix_multiply(ur_ref[...], router_up_ref[...])
    lane = lane_ids()
    chosen = [
        jnp.sum(jnp.where(lane == route_cols_ref[:, k : k + 1], logits, 0.0), axis=1, keepdims=True)
        for k in range(2)
    ]
    top = jnp.maximum(chosen[0], chosen[1])
    powers = [jnp.exp(one - top) for one in chosen]
    total = powers[0] + powers[1]
    gates = [one / total for one in powers]
    gates_ref[...] = jnp.where(lane == 0, gates[0], jnp.where(lane == 1, gates[1], 0.0))
    lifted = ADAPTER_SCALE * product_last(grad_ref[...], up_ref[...])
    side = jnp.where(group_mask(5, 6), inner, jnp.where(group_mask(4, 5), lifted, 0.0))
    turned = jnp.transpose(side)[4 * ADAPTER_RANK : 6 * ADAPTER_RANK].astype(jnp.bfloat16)
    inside = lane < capacity
    for expert in range(gate_slots_ref.shape[0]):
        hots = [
            ((dest_cols_ref[:, k : k + 1] - expert * capacity) == lane) & inside for k in range(2)
        ]
        sums = jnp.where(hots[0], gates[0], jnp.where(hots[1], gates[1], 0.0))
        gate_slots_ref[expert] = jnp.sum(sums, axis=0, keepdims=True)
        hot = jnp.where(hots[0] | hots[1], 1.0, 0.0).astype(jnp.bfloat16)
        side_ref[expert] = matrix_multiply(turned, hot).astype(jnp.bfloat16)


def paired(order, place, count):
    total, bit = 0, 1
    while bit < count:
        total = total + lax.rem(lax.div(order, bit) + lax.div(place, bit), 2) * bit
        bit *= 2
    return total


def lay_out(rows_ref, out_ref):
    cut = FF // 2
    for pair in range(ADAPTER_RANK // 2):
        ones = [rows_ref[2 * pair + k].astype(jnp.float32) for k in range(2)]
        spot = slice(2 * pair * ADAPTER_COUNT, 2 * (pair + 1) * ADAPTER_COUNT)
        for half in range(2):
            rows = [one[half * ADAPTER_COUNT : (half + 1) * ADAPTER_COUNT] for one in ones]
            out_ref[spot, half * cut : (half + 1) * cut] = jnp.concatenate(rows, axis=0).astype(jnp.bfloat16)


def pass_hidden(home_ref, all_ref, rows, came, send_sem, recv_sem, more_sem):
    part, me = lax.axis_index("ctx"), lax.axis_index("exp")
    experts = rows.shape[0]
    half = experts // 2
    base = lax.div(me, half) * half
    mirror = lax.rem(me + half, experts)

    def copy(source, piece, peer, way):
        return pltpu.make_async_remote_copy(
            src_ref=source, dst_ref=rows.at[piece], send_sem=send_sem.at[way, peer],
            recv_sem=recv_sem.at[piece], device_id={"exp": peer}, device_id_type=MESH,
        )

    def around(action):
        def one(turn, carry):
            action(base + lax.rem(me + turn, half))
            return carry

        lax.fori_loop(1, half, one, 0)

    kept = pltpu.make_async_copy(home_ref, rows.at[me], more_sem.at[0])
    swap = pltpu.make_async_remote_copy(
        src_ref=rows, dst_ref=came, send_sem=more_sem.at[1], recv_sem=more_sem.at[2],
        device_id={"ctx": 1 - part}, device_id_type=MESH,
    )

    def begin():
        kept.start()
        copy(home_ref, me, mirror, 0).start()
        around(lambda peer: copy(home_ref, me, peer, 0).start())

    def relay():
        copy(home_ref, mirror, mirror, 0).wait_recv()
        around(lambda peer: copy(rows.at[mirror], mirror, peer, 1).start())

    def cross():
        kept.wait()

        def arrive(peer):
            for piece in (peer, lax.rem(peer + half, experts)):
                copy(home_ref, piece, peer, 0).wait_recv()

        around(arrive)
        swap.start()
        lay_out(rows, all_ref.at[part])

    def end():
        swap.wait()
        lay_out(came, all_ref.at[1 - part])
        copy(home_ref, me, mirror, 0).wait_send()

        def sent(peer):
            copy(home_ref, me, peer, 0).wait_send()
            copy(home_ref, me, peer, 1).wait_send()

        around(sent)

    return begin, relay, cross, end


def expert_kernel(
    capacity, halved, x_ref, side_ref, gate_ref, g_ref, mask_ref, first_hbm, second_hbm, hidden_ref,
    eo_ref, dx_ref, back_side_ref, dgate_ref, grad_ref,
    first_ref, second_ref, x_in, side_in, gate_in, dx_out, side_out, dgate_out,
    deo_ref, ui_ref, duo_ref, lift_ref, act_ref, dpre_ref,
    grad_sum, grad_out, grad_in,
    load_sem, own_sem, send_sem, recv_sem, back_send_sem, back_recv_sem, swap_sem,
):
    other_core = 1 - lax.axis_index("ctx")
    me = lax.axis_index("exp")
    experts = x_ref.shape[0]
    groups = experts // SOURCE_GROUP
    rows = SOURCE_GROUP * capacity
    loads = [
        pltpu.make_async_copy(first_hbm.at[0], first_ref, load_sem.at[0]),
        pltpu.make_async_copy(second_hbm.at[0], second_ref, load_sem.at[1]),
    ]
    for load in loads:
        load.start()

    barrier = pltpu.get_barrier_semaphore()

    def greet(step, carry):
        peer = lax.rem(me + step, experts)
        pl.semaphore_signal(barrier, inc=1, device_id={"exp": peer}, device_id_type=MESH)
        return carry

    lax.fori_loop(1, experts, greet, 0)
    if halved:
        pl.semaphore_signal(barrier, inc=1, device_id={"ctx": other_core}, device_id_type=MESH)
    pl.semaphore_wait(barrier, experts if halved else experts - 1)

    def outward(peer, slot):
        return [
            pltpu.make_async_remote_copy(
                src_ref=source.at[peer], dst_ref=target.at[slot], send_sem=send_sem.at[i, peer],
                recv_sem=recv_sem.at[i, slot], device_id={"exp": peer}, device_id_type=MESH,
            )
            for i, (source, target) in enumerate(((x_ref, x_in), (side_ref, side_in), (gate_ref, gate_in)))
        ]

    def homeward(peer, slot, kinds=(0, 1, 2)):
        pairs = ((dx_out, dx_ref), (side_out, back_side_ref), (dgate_out, dgate_ref))
        return [
            pltpu.make_async_remote_copy(
                src_ref=pairs[i][0].at[peer], dst_ref=pairs[i][1].at[slot], send_sem=back_send_sem.at[i, peer],
                recv_sem=back_recv_sem.at[i, slot], device_id={"exp": peer}, device_id_type=MESH,
            )
            for i in kinds
        ]

    def own_in():
        return [
            pltpu.make_async_copy(source.at[me], target.at[me], own_sem.at[i])
            for i, (source, target) in enumerate(((x_ref, x_in), (side_ref, side_in), (gate_ref, gate_in)))
        ]

    def own_back():
        return [
            pltpu.make_async_copy(source.at[me], target.at[me], own_sem.at[i + 3])
            for i, (source, target) in enumerate(
                ((dx_out, dx_ref), (side_out, back_side_ref), (dgate_out, dgate_ref))
            )
        ]

    for copy in own_in():
        copy.start()
    def plane_of(order):
        return paired(order, lax.div(me, SOURCE_GROUP), groups)

    def push(step, carry):
        order, lane = lax.div(step, SOURCE_GROUP), step
        order = jnp.where(order == 1, 2, jnp.where(order == 2, 1, order))
        peer = plane_of(order) * SOURCE_GROUP + lax.rem(lane + me, SOURCE_GROUP)

        @pl.when(peer != me)
        def _():
            for copy in outward(peer, me):
                copy.start()

        return carry

    lax.fori_loop(0, experts, push, 0)
    side_out[...] = jnp.zeros_like(side_out)
    hidden_in_ref, hidden_out_ref = hidden_ref.at[0], hidden_ref.at[1]
    for load in loads:
        load.wait()

    rank = lax.broadcasted_iota(jnp.int32, (ADAPTER_RANK, LANES), 0)
    place = lax.broadcasted_iota(jnp.int32, (ADAPTER_RANK, LANES), 1)
    expand = jnp.where(lax.div(place, ADAPTER_COUNT) == rank, 1.0, 0.0).astype(jnp.bfloat16)
    eye = lax.broadcasted_iota(jnp.int32, (capacity, LANES), 0) == lax.broadcasted_iota(
        jnp.int32, (capacity, LANES), 1
    )

    def group(turn, carry):
        order = jnp.where(turn == 1, 2, jnp.where(turn == 2, 1, turn))
        base = plane_of(order) * SOURCE_GROUP
        for step in range(SOURCE_GROUP):
            source = base + step

            @pl.when(source != me)
            def _():
                for copy in outward(source, source):
                    copy.wait_recv()

            @pl.when(source == me)
            def _():
                for copy in own_in():
                    copy.wait()

            spot = pl.ds(pl.multiple_of(source * capacity, 16), capacity)
            here = pl.ds(step * capacity, capacity)
            keep = mask_ref[source]
            ui = product_first(side_in[source, ADAPTER_RANK:, :], expand)[:capacity] * keep
            lift = product_first(side_in[source, :ADAPTER_RANK, :], expand)[:capacity] * keep
            column = jnp.sum(jnp.where(eye, gate_in[source], 0.0), axis=1, keepdims=True)
            ui_ref[spot, :] = (ADAPTER_SCALE * ui).astype(jnp.bfloat16)
            duo_ref[spot, :] = (column * lift).astype(jnp.bfloat16)
            lift_ref[here, :] = lift
            deo_ref[here, :] = (column * g_ref[source].astype(jnp.float32)).astype(jnp.bfloat16)
        spot = pl.ds(pl.multiple_of(base * capacity, 16), rows)
        x = x_in[pl.ds(base, SOURCE_GROUP)].reshape(rows, MODEL_WIDTH)
        deo, ui, duo = deo_ref[...], ui_ref[spot, :], duo_ref[spot, :]
        ff = first_ref.shape[1]

        def first_products(start):
            part = slice(start, start + FF_BLOCK)
            pre = matrix_multiply(x, first_ref[:, part]) + matrix_multiply(ui, hidden_in_ref[:, part])
            dact = product_last(deo, second_ref[part, :]) + matrix_multiply(duo, hidden_out_ref[:, part])
            return pre, dact

        ahead = first_products(0)
        for start in range(0, ff, FF_BLOCK):
            pre, dact = ahead
            if start + FF_BLOCK < ff:
                ahead = first_products(start + FF_BLOCK)
            square = pre * pre
            bent = jnp.tanh(pre * (GELU_SLOPE + GELU_SLOPE * GELU_CUBE * square))
            half = 0.5 + 0.5 * bent
            made = pre * half
            slope = half + made * (1.0 - half) * (2.0 * GELU_SLOPE + 6.0 * GELU_SLOPE * GELU_CUBE * square)
            act_ref[spot, start : start + FF_BLOCK] = made.astype(jnp.bfloat16)
            dpre_ref[spot, start : start + FF_BLOCK] = (dact * slope).astype(jnp.bfloat16)
        dx = product_last(dpre_ref[spot, :], first_ref[...])
        dx_out[pl.ds(base, SOURCE_GROUP)] = dx.astype(jnp.bfloat16).reshape(SOURCE_GROUP, capacity, MODEL_WIDTH)
        for step in range(SOURCE_GROUP):
            lane = lax.rem(step + me, SOURCE_GROUP)
            source = base + lane

            @pl.when(source != me)
            def _():
                homeward(source, me, (0,))[0].start()

        dui = product_last(dpre_ref[spot, :], hidden_in_ref[...])
        uo = product_last(act_ref[spot, :], hidden_out_ref[...])
        eo = matrix_multiply(act_ref[spot, :], second_ref[...])
        eo_ref[pl.ds(base, SOURCE_GROUP)] = eo.astype(jnp.bfloat16).reshape(SOURCE_GROUP, capacity, MODEL_WIDTH)
        for step in range(SOURCE_GROUP):
            source = base + step
            here = slice(step * capacity, (step + 1) * capacity)
            keep = mask_ref[source]
            one_uo = (uo[here] * keep).astype(jnp.bfloat16)
            one_dui = (ADAPTER_SCALE * dui[here] * keep).astype(jnp.bfloat16)
            side_out[source, :ADAPTER_RANK, :capacity] = product_last(expand, one_dui).astype(jnp.bfloat16)
            side_out[source, ADAPTER_RANK:, :capacity] = product_last(expand, one_uo).astype(jnp.bfloat16)
            dots = jnp.sum(g_ref[source].astype(jnp.float32) * eo[here], axis=1, keepdims=True)
            dots = dots + jnp.sum(one_uo.astype(jnp.float32) * lift_ref[here, :], axis=1, keepdims=True)
            dgate_out[source] = jnp.sum(jnp.where(eye, dots, 0.0), axis=0, keepdims=True)

            @pl.when(source != me)
            def _():
                for copy in homeward(source, me, (1, 2)):
                    copy.start()

            @pl.when(source == me)
            def _():
                for copy in own_back():
                    copy.start()

        return carry

    lax.fori_loop(0, groups, group, 0)

    def gradients(part, carry):
        spot = pl.ds(pl.multiple_of(part * FF_BLOCK, FF_BLOCK), FF_BLOCK)
        grad_sum[0, :, spot] = product_first(ui_ref[...], dpre_ref[:, spot])
        grad_sum[1, :, spot] = product_first(duo_ref[...], act_ref[:, spot])
        return carry

    lax.fori_loop(0, first_ref.shape[1] // FF_BLOCK, gradients, 0)
    if halved:
        grad_out[...] = grad_sum[other_core].astype(jnp.bfloat16)
        swap = pltpu.make_async_remote_copy(
            src_ref=grad_out, dst_ref=grad_in, send_sem=swap_sem.at[0], recv_sem=swap_sem.at[1],
            device_id={"ctx": other_core}, device_id_type=MESH,
        )
        swap.start()
        swap.wait()
        cut = grad_ref.shape[2]
        for piece in range(grad_ref.shape[0]):
            spot = slice(piece * ADAPTER_COUNT, (piece + 1) * ADAPTER_COUNT)
            halves = [
                grad_sum[1 - other_core, spot, half * cut : (half + 1) * cut]
                + grad_in[spot, half * cut : (half + 1) * cut].astype(jnp.float32)
                for half in range(2)
            ]
            grad_ref[piece] = jnp.concatenate(halves, axis=0).astype(jnp.bfloat16)
    else:
        grad_ref[...] = grad_sum[...].astype(jnp.bfloat16)
    for copy in own_back():
        copy.wait()

    def settle(step, carry):
        peer = lax.rem(me + step, experts)
        for copy in outward(peer, me):
            copy.wait_send()
        for copy in homeward(peer, peer):
            copy.wait_recv()
        for copy in homeward(peer, me):
            copy.wait_send()
        return carry

    lax.fori_loop(1, experts, settle, 0)


def run_expert(halved, x, side, gate_slots, g, mask, first, second, hidden):
    experts, capacity, _ = x.shape
    ff = first.shape[2]
    rows = SOURCE_GROUP * capacity
    vmem, anywhere = pl.BlockSpec(memory_space=pltpu.VMEM), pl.BlockSpec(memory_space=pl.ANY)
    bf16, f32 = jnp.bfloat16, jnp.float32
    outs = [
        (x.shape, bf16),
        (x.shape, bf16),
        (side.shape, bf16),
        (gate_slots.shape, f32),
        ((ADAPTER_RANK, 2 * ADAPTER_COUNT, ff // 2) if halved else (2, LANES, ff), bf16),
    ]
    return pl.pallas_call(
        functools.partial(expert_kernel, capacity, halved),
        in_specs=[anywhere, anywhere, anywhere, vmem, vmem, anywhere, anywhere, vmem],
        out_specs=[vmem, anywhere, anywhere, anywhere, vmem],
        out_shape=[whole(shape) for shape in outs],
        scratch_shapes=[
            pltpu.VMEM(first.shape[1:], bf16),
            pltpu.VMEM(second.shape[1:], bf16),
            pltpu.VMEM(x.shape, bf16),
            pltpu.VMEM(side.shape, bf16),
            pltpu.VMEM(gate_slots.shape, f32),
            pltpu.VMEM(x.shape, bf16),
            pltpu.VMEM(side.shape, bf16),
            pltpu.VMEM(gate_slots.shape, f32),
            pltpu.VMEM((rows, MODEL_WIDTH), bf16),
            pltpu.VMEM((experts * capacity, LANES), bf16),
            pltpu.VMEM((experts * capacity, LANES), bf16),
            pltpu.VMEM((rows, LANES), f32),
            pltpu.VMEM((experts * capacity, ff), bf16),
            pltpu.VMEM((experts * capacity, ff), bf16),
            pltpu.VMEM((2, LANES, ff), f32),
            pltpu.VMEM((LANES, ff), bf16),
            pltpu.VMEM((LANES, ff), bf16),
            pltpu.SemaphoreType.DMA((2,)),
            pltpu.SemaphoreType.DMA((6,)),
            pltpu.SemaphoreType.DMA((3, experts)),
            pltpu.SemaphoreType.DMA((3, experts)),
            pltpu.SemaphoreType.DMA((3, experts)),
            pltpu.SemaphoreType.DMA((3, experts)),
            pltpu.SemaphoreType.DMA((2,)),
        ],
        compiler_params=pltpu.CompilerParams(
            vmem_limit_bytes=VMEM_BYTES, collective_id=1, has_side_effects=True
        ),
        cost_estimate=SMALL_COST,
        name="run_expert",
    )(x, side, gate_slots, g, mask, first, second, hidden)


def share_places(share, experts):
    starts = [share * owner for owner in range(experts)]
    tiles = max(-(-(start % LANES + share) // LANES) for start in starts)
    return [(start // LANES, start % LANES) for start in starts], tiles


def spread_kernel(runs, all_ref, in_ref, out_ref, sum_ref):
    for row, first, count, sources in runs:
        total = None
        for owner, start in sources:
            one = all_ref[owner, :, start * LANES : (start + count) * LANES].astype(jnp.float32)
            total = one if total is None else total + one
        sum_ref[row * ADAPTER_COUNT : (row + 1) * ADAPTER_COUNT, first * LANES : (first + count) * LANES] = total
    in_ref[...] = sum_ref[:LANES, :].astype(jnp.bfloat16)
    out_ref[...] = sum_ref[LANES:, :].astype(jnp.bfloat16)


def spread_hidden(everyone, share, experts, first_lane):
    parts = everyone.shape[0] // experts
    per_part = everyone.shape[2] // LANES
    places, tiles = share_places(share, experts)
    per_row = FF // LANES
    runs = []
    for tile in range(2 * ADAPTER_RANK * per_row):
        at = first_lane // LANES + tile
        sources = []
        for owner, (start, offset) in enumerate(places):
            local = at - start
            if 0 <= local and local * LANES < offset + share:
                sources.append((local // per_part * experts + owner, local % per_part))
        row, column = divmod(tile, per_row)
        last = runs[-1] if runs else None
        if last and last[0] == row and len(last[3]) == 1 and len(sources) == 1:
            owner, start = last[3][0]
            if sources[0] == (owner, start + last[2]):
                runs[-1] = (row, last[1], last[2] + 1, last[3])
                continue
        runs.append((row, column, 1, sources))
    shape = ((ADAPTER_COUNT * ADAPTER_RANK, FF), jnp.bfloat16)
    return run(
        functools.partial(spread_kernel, runs),
        "spread_hidden",
        [shape, shape],
        everyone,
        scratch=[pltpu.VMEM((2 * ADAPTER_COUNT * ADAPTER_RANK, FF), jnp.float32)],
    )


def own_share_kernel(share, tiles, first_tile, grad_ref, out_ref, sum_ref):
    per_row = FF // LANES
    held_rows = grad_ref.shape[0] // ADAPTER_COUNT
    start = lax.div(lax.axis_index("exp") * share, LANES)
    sum_ref[...] = grad_ref[...].astype(jnp.float32)
    for step in range(tiles):
        tile = start + step - first_tile
        held = jnp.clip(tile, 0, held_rows * per_row - 1)
        row = pl.multiple_of(lax.div(held, per_row) * ADAPTER_COUNT, ADAPTER_COUNT)
        column = pl.multiple_of(lax.rem(held, per_row) * LANES, LANES)
        slab = sum_ref[pl.ds(row, ADAPTER_COUNT), pl.ds(column, LANES)]
        out_ref[:, step * LANES : (step + 1) * LANES] = jnp.where(held == tile, slab, 0.0)


def close_parts(
    share, tiles, window, cuts, mix, down_ref, up_ref, router_ref, pick_ref, piece_ref, out_ref,
    flat, sent, came, own_in, own_wide, own_total, own_came, hidden_in, hidden_wide,
    total_sem, local_sem, swap_send, swap_recv, own_send, own_recv, hidden_send, hidden_recv,
):
    part, me = lax.axis_index("ctx"), lax.axis_index("exp")
    cores, experts = lax.axis_size("ctx"), lax.axis_size("exp")
    per_row = FF // LANES
    first_hidden, last_hidden = cuts[1] // LANES, cuts[2] // LANES
    hidden_row = part * experts + me

    def owner_of(row, end):
        return lax.div((first_hidden + row * per_row) * LANES + end * (FF - 1), share)

    def hidden_copy(row, core, owner):
        return pltpu.make_async_remote_copy(
            src_ref=piece_ref, dst_ref=hidden_in.at[row], send_sem=hidden_send.at[core, owner],
            recv_sem=hidden_recv.at[row], device_id={"ctx": core, "exp": owner}, device_id_type=MESH,
        )

    def hidden_targets(action):
        low, high = owner_of(hidden_row, 0), owner_of(hidden_row, 1)
        for core in range(cores):
            for owner, needed in ((low, True), (high, high != low)):
                elsewhere = (core != part) | (owner != me)

                @pl.when(needed & elsewhere)
                def _():
                    action(hidden_copy(hidden_row, core, owner))

    hidden_targets(lambda copy: copy.start())
    own_hidden = pltpu.make_async_copy(piece_ref, hidden_in.at[hidden_row], local_sem.at[0])
    own_hidden.start()

    flat[...] = jnp.zeros_like(flat)
    columns = 6 * ADAPTER_RANK
    quarter = MODEL_WIDTH // 4
    rows = [down_ref[pl.ds(step, quarter, stride=4), :] for step in range(4)]
    for step in range(3):
        left = rows[step][:, step * (LANES - columns) : columns]
        right = rows[step + 1][:, : LANES - left.shape[1]]
        flat[pl.ds(step, quarter, stride=3), :] = jnp.concatenate([left, right], axis=1)
    per_model = MODEL_WIDTH // LANES
    for step in range(per_model):
        spot = pl.ds(cuts[0] // LANES + step, 5 * ADAPTER_RANK, stride=per_model)
        flat[spot, :] = up_ref[: 5 * ADAPTER_RANK, step * LANES : (step + 1) * LANES]
    per_tile = LANES // experts
    for tile in range(ADAPTER_RANK // per_tile):
        total = jnp.zeros((1, LANES), jnp.float32)
        for step in range(per_tile):
            row = 4 * ADAPTER_RANK + tile * per_tile + step
            one = router_ref[row : row + 1, :]
            total = total + (pltpu.roll(one, step * experts, 1) if step else one)
        flat[last_hidden + tile : last_hidden + tile + 1, :] = total
    sent[...] = flat[...].astype(jnp.bfloat16)

    def swap(turn):
        core = lax.rem(part + turn, cores)
        return pltpu.make_async_remote_copy(
            src_ref=sent, dst_ref=came.at[turn - 1], send_sem=swap_send.at[turn - 1],
            recv_sem=swap_recv.at[turn - 1], device_id={"ctx": core}, device_id_type=MESH,
        )

    for turn in range(1, cores):
        swap(turn).start()
    for turn in range(1, cores):
        swap(turn).wait()
    total = flat[...]
    for turn in range(1, cores):
        total = total + came[turn - 1].astype(jnp.float32)
    sent[...] = total.astype(jnp.bfloat16)

    def has_own(owner):
        return (owner * share < cuts[1]) | ((owner + 1) * share > cuts[2])

    def window_of(owner):
        start = lax.div(lax.div(owner * share, LANES), 16) * 16
        return sent.at[pl.ds(pl.multiple_of(start, 16), window)]

    def own_copy(owner, slot):
        return pltpu.make_async_remote_copy(
            src_ref=window_of(owner), dst_ref=own_in.at[slot], send_sem=own_send.at[owner],
            recv_sem=own_recv.at[slot], device_id={"exp": owner}, device_id_type=MESH,
        )

    def push(turn, carry):
        owner = lax.rem(me + turn, experts)

        @pl.when(has_own(owner) & (lax.rem(owner, 2) == part))
        def _():
            own_copy(owner, me).start()

        return carry

    lax.fori_loop(1, experts, push, 0)
    kept = pltpu.make_async_copy(window_of(me), own_in.at[me], local_sem.at[1])
    kept.start()
    start = lax.div(me * share, LANES)
    offset = lax.rem(start, 16)

    mix()

    own_hidden.wait()

    def arrive(row, carry):
        sender_core, sender = lax.div(row, experts), lax.rem(row, experts)
        mine = (owner_of(row, 0) == me) | (owner_of(row, 1) == me)

        @pl.when(mine & ((sender_core != part) | (sender != me)))
        def _():
            hidden_copy(row, part, me).wait_recv()

        return carry

    lax.fori_loop(0, 2 * ADAPTER_RANK, arrive, 0)
    hidden_wide[...] = hidden_in[...].astype(jnp.float32)
    half = per_row // 2
    for step in range(tiles):
        tile = start + step - first_hidden
        held = jnp.clip(tile, 0, 2 * ADAPTER_RANK * per_row - 1)
        row, column = lax.div(held, per_row), lax.rem(held, per_row)
        upper = pl.multiple_of(lax.div(column, half) * ADAPTER_COUNT, ADAPTER_COUNT)
        column = pl.multiple_of(lax.rem(column, half) * LANES, LANES)
        slab = hidden_wide[row, pl.ds(upper, ADAPTER_COUNT), pl.ds(column, LANES)]
        out_ref[:, step * LANES : (step + 1) * LANES] = jnp.where(held == tile, slab, 0.0)

    kept.wait()
    totals = pltpu.make_async_remote_copy(
        src_ref=own_total, dst_ref=own_came, send_sem=total_sem.at[0], recv_sem=total_sem.at[1],
        device_id={"ctx": 1 - part}, device_id_type=MESH,
    )
    summing = lax.rem(me, 2) == part

    @pl.when(has_own(me) & summing)
    def _():
        def arrive(turn, carry):
            sender = lax.rem(me + turn, experts)
            own_copy(sender, sender).wait_recv()
            return carry

        lax.fori_loop(1, experts, arrive, 0)
        for adapter in range(ADAPTER_COUNT):
            total = jnp.zeros((window, LANES), jnp.float32)
            for sender in range(experts):
                total = total + jnp.where(pick_ref[sender] == adapter, own_in[sender].astype(jnp.float32), 0.0)
            own_wide[adapter * window : (adapter + 1) * window, :] = total
        for step in range(tiles):
            slab = own_wide[pl.ds(offset + step, ADAPTER_COUNT, stride=window), :]
            own_total[:, step * LANES : (step + 1) * LANES] = slab
        totals.start()
        out_ref[...] = out_ref[...] + own_total[...]
        totals.wait_send()

    @pl.when(has_own(me) & jnp.logical_not(summing))
    def _():
        totals.wait_recv()
        out_ref[...] = out_ref[...] + own_came[...]

    def settle(turn, carry):
        owner = lax.rem(me + turn, experts)

        @pl.when(has_own(owner) & (lax.rem(owner, 2) == part))
        def _():
            own_copy(owner, me).wait_send()

        return carry

    lax.fori_loop(1, experts, settle, 0)
    hidden_targets(lambda copy: copy.wait_send())


def backward_kernel(
    share, tiles, window, cuts, capacity,
    dx_ref, dgate_ref, dest_cols_ref, routes_ref, gates_ref, hidden_ref, xn_two_ref, grad_ref, ur_ref, w_ref, o_ref,
    out_weight_ref, router_ref, own_router_ref, own_down_ref, own_up_ref, gain_ref, side_ref, pick_ref,
    qe_ref, ke_ref, far_ref, u_ref, made_hbm, pieces_hbm, q_hbm, kv_hbm, lse_hbm, turned_hbm, weight_hbm, tokens_hbm, xn_hbm,
    input_grad_ref, share_ref, mixed_ref,
    q_ref, kv_ref, lse_ref, turned_ref, weight_ref, tokens_ref, xn_ref, dh_ref, do_ref, grad_down, grad_up, grad_router, uo_ref,
    dq_ref, dkv_ref, other_ref, qx_ref, gx_ref, dq_sum, kv_made, ret_ref, piece_ref, load_sem, kv_send, kv_recv,
    ret_send, ret_recv, ret_own, *rest,
):
    part, me = lax.axis_index("ctx"), lax.axis_index("exp")
    cores, experts = lax.axis_size("ctx"), lax.axis_size("exp")
    passing, closing = rest[:7], rest[7:]
    loads = [
        pltpu.make_async_copy(source, target, load_sem.at[i])
        for i, (source, target) in enumerate(
            (
                (q_hbm, q_ref), (kv_hbm, kv_ref), (lse_hbm, lse_ref), (turned_hbm, turned_ref), (weight_hbm, weight_ref),
                (tokens_hbm, tokens_ref), (xn_hbm, xn_ref),
            )
        )
    ]
    for load in loads:
        load.start()
    barrier = pltpu.get_barrier_semaphore()

    def greet(turn, carry):
        core, peer = lax.div(turn, experts), lax.rem(turn, experts)

        @pl.when((core != part) | (peer != me))
        def _():
            pl.semaphore_signal(barrier, inc=1, device_id={"ctx": core, "exp": peer}, device_id_type=MESH)

        return carry

    lax.fori_loop(0, cores * experts, greet, 0)
    pl.semaphore_wait(barrier, cores * experts - 1)
    begin, middle, end = pass_pieces(pieces_hbm, piece_ref, *passing)
    begin()

    def ret_spot(slot):
        return ret_ref.at[pl.ds(pl.multiple_of(slot * capacity, 16), capacity)]

    def ret_copy(peer, slot):
        return pltpu.make_async_remote_copy(
            src_ref=made_hbm.at[peer], dst_ref=ret_spot(slot), send_sem=ret_send.at[peer],
            recv_sem=ret_recv.at[slot], device_id={"exp": peer}, device_id_type=MESH,
        )

    own_ret = pltpu.make_async_copy(made_hbm.at[me], ret_spot(me), ret_own.at[0])
    own_ret.start()
    push_rows(me, experts, lambda peer: ret_copy(peer, me).start(), (2, 1, 0))
    back_kernel(
        capacity, dx_ref, dgate_ref, dest_cols_ref, routes_ref, gates_ref, hidden_ref, xn_two_ref, grad_ref,
        ur_ref, w_ref, o_ref, out_weight_ref, router_ref, own_router_ref, own_down_ref, own_up_ref, gain_ref, side_ref,
        dh_ref, do_ref, grad_down, grad_up, grad_router, uo_ref,
    )
    for load in loads[:4]:
        load.wait()
    half = tokens_ref.shape[0] // 2
    pairs = HEADS // 2

    def attend(pair, carry):
        spot = pl.ds(pl.multiple_of(pair * LANES, LANES), LANES)
        attend_back_pair(
            cores, half, pair, pairs, q_ref.at[:, spot], kv_ref.at[:, pl.ds(0, 1), :, spot],
            kv_ref.at[:, pl.ds(1, 1), :, spot], do_ref.at[:, spot], o_ref.at[:, spot], lse_ref.at[:, spot],
            qe_ref, ke_ref, far_ref.at[pl.ds(pair, 1)], turned_ref.at[pl.ds(2 * pair, 2)],
            dq_ref.at[:, spot], dkv_ref.at[:, :, spot], other_ref, qx_ref, gx_ref, dq_sum, kv_made, kv_send, kv_recv,
        )

        @pl.when(pair == 1)
        def _():
            middle()
            push_rows(me, experts, lambda peer: ret_copy(peer, me).start(), (3,))

        return carry

    lax.fori_loop(0, pairs, attend, 0)
    end()
    for load in loads[4:]:
        load.wait()

    dxn = jnp.zeros(dh_ref.shape, jnp.float32)
    du = jnp.zeros(u_ref.shape, jnp.float32)
    for group in range(3):
        if group == 0:
            grad = dq_ref[...]
        else:
            grad = dkv_ref[group - 1].astype(jnp.float32)
            for turn in range(1, cores):
                grad = grad + other_ref[turn - 1, group - 1].astype(jnp.float32)
            grad = grad.astype(jnp.bfloat16)
        spot = slice(group * MODEL_WIDTH, (group + 1) * MODEL_WIDTH)
        dxn = dxn + product_last(grad, weight_ref[:, spot])
        own = group_mask(group, group + 1)
        du = du + jnp.where(own, ADAPTER_SCALE * product_last(grad, own_up_ref[...]), 0.0)
        inner = jnp.where(own, u_ref[...], jnp.zeros((), jnp.bfloat16))
        grad_up[...] += ADAPTER_SCALE * product_first(inner, grad)
    du = du.astype(jnp.bfloat16)
    grad_down[...] += product_first(xn_ref[...], du)

    def mix():
        finish = (dxn + product_last(du, own_down_ref[...])) * gain_ref[0:1, :]
        tokens = tokens_ref[...].astype(jnp.float32)
        scale = lax.rsqrt(jnp.mean(tokens * tokens, axis=-1, keepdims=True) + NORM_EPS)
        inner = jnp.mean(tokens * finish, axis=-1, keepdims=True)
        input_grad_ref[...] = dh_ref[...] + scale * finish - tokens * (scale * scale * scale * inner)
        own_ret.wait()

        def arrive(turn, carry):
            peer = lax.rem(me + turn, experts)
            ret_copy(peer, peer).wait_recv()
            ret_copy(peer, me).wait_send()
            return carry

        lax.fori_loop(1, experts, arrive, 0)
        mix_kernel(ret_ref, dest_cols_ref, gates_ref, hidden_ref, uo_ref, own_up_ref, mixed_ref)

    close_parts(
        share, tiles, window, cuts, mix, grad_down, grad_up, grad_router, pick_ref, piece_ref, share_ref, *closing
    )


def backward(share, tiles, cuts, capacity, cores, near, far_away):
    dx, hidden, o = near[0], near[5], near[10]
    made, pieces, q, kv, lse, turned, weight, tokens, xn = far_away
    rows, experts = hidden.shape[0], made.shape[0]
    window = -(-(15 + tiles) // 16) * 16
    length = max(share * owner // LANES // 16 * 16 for owner in range(experts)) + window
    bf16, f32 = jnp.bfloat16, jnp.float32
    vmem, anywhere = pl.BlockSpec(memory_space=pltpu.VMEM), pl.BlockSpec(memory_space=pl.ANY)
    dma = pltpu.SemaphoreType.DMA
    model, lanes = (rows, MODEL_WIDTH), (rows, LANES)
    piece = pieces.shape[1:]
    outs = [(model, f32), ((ADAPTER_COUNT, tiles * LANES), f32), (model, bf16)]
    return pl.pallas_call(
        functools.partial(backward_kernel, share, tiles, window, cuts, capacity),
        in_specs=[
            pl.BlockSpec(memory_space=pltpu.SMEM) if one.ndim == 1 else vmem for one in near
        ]
        + [anywhere] * len(far_away),
        out_specs=[vmem] * 3,
        out_shape=[whole(shape) for shape in outs],
        scratch_shapes=[
            pltpu.VMEM(q.shape, bf16),
            pltpu.VMEM(kv.shape, bf16),
            pltpu.VMEM(lse.shape, f32),
            pltpu.VMEM(turned.shape, f32),
            pltpu.VMEM(weight.shape, bf16),
            pltpu.VMEM(tokens.shape, bf16),
            pltpu.VMEM(xn.shape, bf16),
            pltpu.VMEM(model, f32),
            pltpu.VMEM(model, bf16),
            pltpu.VMEM((MODEL_WIDTH, LANES), f32),
            pltpu.VMEM((LANES, MODEL_WIDTH), f32),
            pltpu.VMEM((LANES, LANES), f32),
            pltpu.VMEM((2,) + lanes, bf16),
            pltpu.VMEM(model, bf16),
            pltpu.VMEM((2,) + model, bf16),
            pltpu.VMEM((cores - 1, 2) + model, bf16),
            pltpu.VMEM((2,) + lanes, bf16),
            pltpu.VMEM((2,) + lanes, bf16),
            pltpu.VMEM((2, LANES, rows), f32),
            pltpu.VMEM((2, cores, 2) + lanes, bf16),
            pltpu.VMEM(dx.shape, bf16),
            pltpu.VMEM(piece, bf16),
            dma((7,)),
            dma((2, cores - 1)),
            dma((HEADS // 2, cores - 1)),
            dma((experts,)),
            dma((experts,)),
            dma((1,)),
            *pieces_scratch(pieces),
            pltpu.VMEM((length, LANES), f32),
            pltpu.VMEM((length, LANES), bf16),
            pltpu.VMEM((cores - 1, length, LANES), bf16),
            pltpu.VMEM((experts, window, LANES), bf16),
            pltpu.VMEM((ADAPTER_COUNT * window, LANES), f32),
            pltpu.VMEM((ADAPTER_COUNT, tiles * LANES), f32),
            pltpu.VMEM((ADAPTER_COUNT, tiles * LANES), f32),
            pltpu.VMEM((2 * ADAPTER_RANK,) + piece, bf16),
            pltpu.VMEM((2 * ADAPTER_RANK,) + piece, f32),
            dma((2,)),
            dma((2,)),
            dma((cores - 1,)),
            dma((cores - 1,)),
            dma((experts,)),
            dma((experts,)),
            dma((cores, experts)),
            dma((2 * ADAPTER_RANK,)),
        ],
        compiler_params=pltpu.CompilerParams(
            vmem_limit_bytes=VMEM_BYTES, collective_id=3, has_side_effects=True
        ),
        cost_estimate=SMALL_COST,
        name="backward",
    )(*near, *far_away)


def back_kernel(
    capacity, dx_ref, dgate_slots_ref, dest_cols_ref, route_cols_ref, gates_ref, hidden_ref, xn_ref, grad_ref,
    ur_ref, w_ref, o_ref, weight_ref, router_ref, router_up_ref, down_ref, up_ref, gain_ref, side_ref,
    dh_ref, do_ref, grad_down_ref, grad_up_ref, grad_router_ref, uo_ref,
):
    count = hidden_ref.shape[0]
    lane = lane_ids()
    dests = [dest_cols_ref[:, k : k + 1] for k in range(2)]
    back = jnp.zeros((count, MODEL_WIDTH), jnp.float32)
    for start in range(0, dx_ref.shape[0], ROW_BLOCK):
        size = min(ROW_BLOCK, dx_ref.shape[0] - start)
        slot = lax.broadcasted_iota(jnp.int32, (count, size), 1) + start
        hot = jnp.where((slot == dests[0]) | (slot == dests[1]), 1.0, 0.0).astype(jnp.bfloat16)
        back = back + matrix_multiply(hot, dx_ref[start : start + size, :])
    dgates = []
    sides = []
    blank = jnp.zeros((LANES, LANES), jnp.bfloat16)
    for k in range(2):
        sums = jnp.zeros((count, LANES), jnp.float32)
        side = jnp.zeros((count, LANES), jnp.float32)
        for expert in range(dgate_slots_ref.shape[0]):
            hot = dests[k] - expert * capacity == lane
            sums = sums + jnp.where(hot, dgate_slots_ref[expert], 0.0)
            hot = jnp.where(hot, 1.0, 0.0).astype(jnp.bfloat16)
            wide = [blank[: 5 * ADAPTER_RANK], side_ref[expert], blank[: LANES - 7 * ADAPTER_RANK]]
            side = side + product_last(hot, jnp.concatenate(wide, axis=0))
        dgates.append(jnp.sum(sums, axis=1, keepdims=True))
        sides.append(side)
    gates = [gates_ref[:, k : k + 1] for k in range(2)]
    mean = gates[0] * dgates[0] + gates[1] * dgates[1]
    dlogits = jnp.zeros((count, LANES), jnp.float32)
    for k in range(2):
        dsel = gates[k] * (dgates[k] - mean)
        dlogits = dlogits + jnp.where(lane == route_cols_ref[:, k : k + 1], dsel, 0.0)
    dlogits = dlogits.astype(jnp.bfloat16)
    dur = ADAPTER_SCALE * product_last(dlogits, router_up_ref[...])
    dur = jnp.where(group_mask(4, 5), dur, sides[0] + sides[1])
    dur = keep_group(dur, 4, 6)
    dxn = back + product_last(dlogits, router_ref[...]) + product_last(dur, down_ref[...])
    dxn = dxn.astype(jnp.bfloat16).astype(jnp.float32)
    hidden = hidden_ref[...]
    scale = lax.rsqrt(jnp.mean(hidden * hidden, axis=-1, keepdims=True) + NORM_EPS)
    dxn = dxn * gain_ref[1:2, :]
    inner = jnp.mean(hidden * dxn, axis=-1, keepdims=True)
    dh = grad_ref[...].astype(jnp.float32) + scale * dxn - hidden * (scale * scale * scale * inner)
    dh_ref[...] = dh
    db = dh.astype(jnp.bfloat16)
    dw = keep_group(ADAPTER_SCALE * product_last(db, up_ref[...]), 3, 4)
    do_ref[...] = (product_last(db, weight_ref[...]) + product_last(dw, down_ref[...])).astype(jnp.bfloat16)
    grad_down_ref[...] = product_first(o_ref[...], dw) + product_first(xn_ref[...], dur)
    grad_up = product_first(w_ref[...], db)
    for k in range(2):
        uo = keep_group(pltpu.roll(sides[k], LANES - 2 * ADAPTER_RANK, 1), 4, 5)
        uo_ref[k] = uo
        deo = (gates[k] * grad_ref[...].astype(jnp.float32)).astype(jnp.bfloat16)
        grad_up = grad_up + product_first(uo, deo)
    grad_up_ref[...] = ADAPTER_SCALE * grad_up
    grad_router_ref[...] = ADAPTER_SCALE * product_first(ur_ref[...], dlogits)


def qkv_back_kernel(
    dq_ref, mine_ref, other_ref, weight_ref, down_ref, up_ref, xn_ref, u_ref, tokens_ref, gain_ref, dh_ref, grad_down_in_ref, grad_up_in_ref,
    out_ref, grad_down_ref, grad_up_ref, sum_ref, du_ref, grad_ref,
):
    step = pl.program_id(0)

    @pl.when(step == 0)
    def _():
        grad_ref[...] = dq_ref[...]
        sum_ref[...] = jnp.zeros_like(sum_ref)
        du_ref[...] = jnp.zeros_like(du_ref)
        grad_up_ref[...] = grad_up_in_ref[...]

    @pl.when(step > 0)
    def _():
        total = mine_ref[0].astype(jnp.float32) + other_ref[0].astype(jnp.float32)
        grad_ref[...] = total.astype(jnp.bfloat16)

    lane = lane_ids()
    group = (lane >= step * ADAPTER_RANK) & (lane < (step + 1) * ADAPTER_RANK)
    grad = grad_ref[...]
    sum_ref[...] += product_last(grad, weight_ref[...])
    du = jnp.where(group, ADAPTER_SCALE * product_last(grad, up_ref[...]), 0.0)
    du_ref[...] += du
    inner = jnp.where(group, u_ref[...], jnp.zeros((), jnp.bfloat16))
    grad_up_ref[...] += ADAPTER_SCALE * product_first(inner, grad)

    @pl.when(step == 2)
    def _():
        du = du_ref[...].astype(jnp.bfloat16)
        dxn = (sum_ref[...] + product_last(du, down_ref[...])) * gain_ref[0:1, :]
        tokens = tokens_ref[...].astype(jnp.float32)
        scale = lax.rsqrt(jnp.mean(tokens * tokens, axis=-1, keepdims=True) + NORM_EPS)
        inner = jnp.mean(tokens * dxn, axis=-1, keepdims=True)
        out_ref[...] = dh_ref[...] + scale * dxn - tokens * (scale * scale * scale * inner)
        grad_down_ref[...] = grad_down_in_ref[...] + product_first(xn_ref[...], du)


def qkv_back(dq, dkv, other, weight, down, up, xn, u, tokens, gains, dh, grad_down, grad_up):
    rows = tokens.shape[0]
    fixed = lambda array: pl.BlockSpec(array.shape, lambda g: (0, 0))
    later = lambda g: jnp.maximum(g - 1, 0)
    return pl.pallas_call(
        qkv_back_kernel,
        grid=(3,),
        in_specs=[
            fixed(dq),
            pl.BlockSpec((1, rows, MODEL_WIDTH), lambda g: (later(g), 0, 0)),
            pl.BlockSpec((1, rows, MODEL_WIDTH), lambda g: (later(g), 0, 0)),
            pl.BlockSpec((MODEL_WIDTH, MODEL_WIDTH), lambda g: (0, g)),
            fixed(down), fixed(up), fixed(xn), fixed(u), fixed(tokens), fixed(gains), fixed(dh),
            fixed(grad_down), fixed(grad_up),
        ],
        out_specs=[fixed(dh), fixed(grad_down), fixed(grad_up)],
        out_shape=[jax.ShapeDtypeStruct(a.shape, jnp.float32) for a in (dh, grad_down, grad_up)],
        scratch_shapes=[
            pltpu.VMEM((rows, MODEL_WIDTH), jnp.float32),
            pltpu.VMEM((rows, LANES), jnp.float32),
            pltpu.VMEM((rows, MODEL_WIDTH), jnp.bfloat16),
        ],
        compiler_params=pltpu.CompilerParams(vmem_limit_bytes=VMEM_BYTES),
        cost_estimate=SMALL_COST,
        name="qkv_back",
    )(dq, dkv, other, weight, down, up, xn, u, tokens, gains, dh, grad_down, grad_up)


def mix_kernel(ret_ref, dest_cols_ref, gates_ref, hidden_ref, uo_ref, up_ref, out_ref):
    count = hidden_ref.shape[0]
    total = hidden_ref[...]
    for k in range(2):
        dest = dest_cols_ref[:, k : k + 1]
        picked = ADAPTER_SCALE * matrix_multiply(uo_ref[k], up_ref[...])
        for start in range(0, ret_ref.shape[0], ROW_BLOCK):
            size = min(ROW_BLOCK, ret_ref.shape[0] - start)
            slot = lax.broadcasted_iota(jnp.int32, (count, size), 1) + start
            hot = jnp.where(slot == dest, 1.0, 0.0).astype(jnp.bfloat16)
            picked = picked + matrix_multiply(hot, ret_ref[start : start + size, :])
        total = total + gates_ref[:, k : k + 1] * picked
    out_ref[...] = total.astype(jnp.bfloat16)


def exchange(array, exp_count):
    blocks = array.reshape((exp_count, array.shape[0] // exp_count) + array.shape[1:])
    return lax.all_to_all(blocks, "exp", split_axis=0, concat_axis=0, tiled=True).reshape(array.shape)


def shards(
    tokens,
    cotangent,
    norm_gains,
    query_key_value_weight,
    attention_out_weight,
    rel_bias,
    router_matrix,
    expert_in,
    expert_out,
    adapters,
    first_moment,
    second_moment,
    segment_ids,
    routes,
    adapter_pick,
):
    ctx_count = lax.axis_size("ctx")
    exp_count = lax.axis_size("exp")
    ctx_index = lax.axis_index("ctx")
    bf16, f32 = jnp.bfloat16, jnp.float32
    rows = tokens.shape[2]
    token_rows, grad_rows = tokens[0, 0], cotangent[0, 0]
    share = adapters.shape[1]
    down_size = 6 * ADAPTER_RANK * MODEL_WIDTH
    up_size = 5 * ADAPTER_RANK * MODEL_WIDTH
    hidden_size = 2 * ADAPTER_RANK * FF
    cuts = (down_size, down_size + up_size, down_size + up_size + hidden_size)

    halved = ctx_count == 2 and exp_count == ADAPTER_RANK
    places, tiles = share_places(share, exp_count)
    offset = lax.rem(lax.axis_index("exp") * share, LANES)

    capacity = 5 * rows * 2 // (4 * exp_count)
    capacity = -(-capacity // 16) * 16
    slots = exp_count * capacity
    by_source = (exp_count, capacity, MODEL_WIDTH)
    (
        home, route_cols, dest_rows, dest_cols, mask,
        query, gathered, normed_one, inner_qkv, own_down, own_up, own_router, turned, mixed_rows, log_sums,
        qe, ke, far, router, hidden, normed_two, inner_out, inner_router, gates, gate_slots, side, sent, arrived_grad,
    ) = forward(
        share, tiles, cuts, halved, capacity, ctx_count, exp_count, adapters, adapter_pick, token_rows, grad_rows,
        norm_gains, rel_bias, segment_ids, router_matrix.T, routes[0, 0].T, query_key_value_weight, attention_out_weight,
    )

    if halved:
        hidden_weights = home
    else:
        per_part = -(-tiles // ctx_count)
        shifted = jnp.zeros((ADAPTER_COUNT, per_part * ctx_count * LANES), bf16)
        shifted = lax.dynamic_update_slice(shifted, adapters.astype(bf16), (0, offset))
        shifted = lax.dynamic_slice_in_dim(shifted, ctx_index * per_part * LANES, per_part * LANES, 1)
        everyone = lax.all_gather(shifted, ("ctx", "exp"), axis=0)
        hidden_weights = jnp.stack(spread_hidden(everyone, share, exp_count, cuts[1]))

    made, returned_back, returned_side, returned_dgate, grad_hidden = run_expert(
        halved, sent.reshape(by_source), side, gate_slots, arrived_grad, mask,
        expert_in, expert_out, hidden_weights,
    )
    returned_back = returned_back.reshape(slots, MODEL_WIDTH)

    pick_hot = (jnp.arange(ADAPTER_COUNT, dtype=jnp.int32)[:, None] == adapter_pick[None, :]).astype(bf16)
    back_operands = (
        returned_back, returned_dgate, dest_cols, route_cols, gates, hidden, normed_two, grad_rows, inner_router,
        inner_out, mixed_rows, attention_out_weight, router, own_router, own_down, own_up, norm_gains, returned_side,
    )
    if halved:
        input_grad, owned_grad, output_rows = backward(
            share, tiles, cuts, capacity, ctx_count,
            back_operands + (adapter_pick, qe, ke, far, inner_qkv),
            (
                made, grad_hidden, query, gathered, log_sums, turned, query_key_value_weight, token_rows, normed_one,
            ),
        )
        owned_grad = lax.dynamic_slice_in_dim(owned_grad, offset, share, 1)
    else:
        hidden_grad, out_grad, grad_down, grad_up, grad_router, inner_second = run(
            functools.partial(back_kernel, capacity),
            "back_to_attention",
            [
                ((rows, MODEL_WIDTH), f32),
                ((rows, MODEL_WIDTH), bf16),
                ((MODEL_WIDTH, LANES), f32),
                ((LANES, MODEL_WIDTH), f32),
                ((LANES, LANES), f32),
                ((2, rows, LANES), bf16),
            ],
            *back_operands,
        )
        returned = exchange(made.reshape(slots, MODEL_WIDTH), exp_count)
        query_grad, key_value_grad, others = attend_back(
            query, gathered, out_grad, mixed_rows, log_sums, qe, ke, far, turned
        )
        other = jnp.sum(others.astype(f32), axis=0).astype(bf16)
        input_grad, grad_down, grad_up = qkv_back(
            query_grad, key_value_grad, other, query_key_value_weight, own_down, own_up, normed_one, inner_qkv,
            token_rows, norm_gains, hidden_grad, grad_down, grad_up,
        )
        (output_rows,) = run(
            mix_kernel,
            "mix",
            [((rows, MODEL_WIDTH), bf16)],
            returned, dest_cols, gates, hidden, inner_second, own_up,
        )
        own_grad = jnp.concatenate(
            [
                grad_down[:, : 6 * ADAPTER_RANK].astype(bf16).reshape(-1),
                grad_up[: 5 * ADAPTER_RANK].astype(bf16).reshape(-1),
                jnp.zeros((hidden_size,), bf16),
                grad_router[4 * ADAPTER_RANK : 5 * ADAPTER_RANK, : router_matrix.shape[1]].astype(bf16).reshape(-1),
            ]
        )
        own_grad = exchange(own_grad.reshape(exp_count, share), exp_count)
        owned_grad = lax.psum(matrix_multiply(pick_hot, own_grad), "ctx")
        grad_hidden = lax.psum(grad_hidden.reshape(2 * LANES, FF), ("ctx", "exp"))
        (hidden_share,) = run(
            functools.partial(own_share_kernel, share, tiles, cuts[1] // LANES),
            "own_share",
            [((ADAPTER_COUNT, tiles * LANES), f32)],
            grad_hidden,
            scratch=[pltpu.VMEM(grad_hidden.shape, f32)],
        )
        owned_grad = owned_grad + lax.dynamic_slice_in_dim(hidden_share, offset, share, 1)
    new_first = BETA_ONE * first_moment + (1.0 - BETA_ONE) * owned_grad
    new_second = BETA_TWO * second_moment + (1.0 - BETA_TWO) * owned_grad * owned_grad
    corrected = new_first / (1.0 - BETA_ONE**STEP_NUM)
    denominator = jnp.sqrt(new_second / (1.0 - BETA_TWO**STEP_NUM)) + ADAM_EPS
    new_adapters = adapters - LEARN_RATE * (corrected / denominator + WEIGHT_DECAY * adapters)
    return (
        output_rows[None, None],
        input_grad[None, None],
        new_adapters,
        new_first,
        new_second,
    )


def solution(mesh):
    return jax.shard_map(
        shards,
        mesh=mesh,
        in_specs=(
            P("exp", "ctx", None, None),
            P("exp", "ctx", None, None),
            P(),
            P(),
            P(),
            P(),
            P(),
            P("exp", None, None),
            P("exp", None, None),
            P(None, "exp"),
            P(None, "exp"),
            P(None, "exp"),
            P("exp", None),
            P("exp", "ctx", None, None),
            P(),
        ),
        out_specs=(
            P("exp", "ctx", None, None),
            P("exp", "ctx", None, None),
            P(None, "exp"),
            P(None, "exp"),
            P(None, "exp"),
        ),
        check_vma=False,
    )
```

```python
import functools

import jax
import jax.numpy as jnp
import numpy as np
from jax import lax
from jax.experimental import pallas as pl
from jax.experimental.pallas import tpu as pltpu
from jax.sharding import PartitionSpec as P

MODEL_WIDTH = 768
HEADS = 12
HEAD_DIM = 64
FF = 3072
ADAPTER_RANK = 16
ADAPTER_COUNT = 8
STEP_NUM = 5


NORM_EPS = 1e-06
ADAPTER_SCALE = 2.0
MASKED = -1e30
BETA_ONE = 0.9
BETA_TWO = 0.999
LEARN_RATE = 0.05
WEIGHT_DECAY = 0.01
ADAM_EPS = 1e-08
VMEM_BYTES = 56 * 1024 * 1024
MESH = pl.DeviceIdType.MESH
SMALL_COST = pl.CostEstimate(flops=1, bytes_accessed=1, transcendentals=0)


def bucket_bounds():
    bounds = list(range(1, 16))
    for level_index in range(16):
        bounds.append(int(np.ceil(16.0 * 8.0 ** (level_index / 16.0) - 1e-09)))
    return bounds


def rms_scale(values, gain_row):
    return (
        values * lax.rsqrt(jnp.mean(values * values, axis=-1, keepdims=True) + NORM_EPS) * gain_row
    )


def matrix_multiply(former, latter):
    return jnp.dot(former, latter, preferred_element_type=jnp.float32)


def product_last(former, latter):
    return lax.dot_general(
        former,
        latter,
        (((former.ndim - 1,), (latter.ndim - 1,)), ((), ())),
        preferred_element_type=jnp.float32,
    )


def product_first(former, latter):
    return lax.dot_general(
        former, latter, (((0,), (0,)), ((), ())), preferred_element_type=jnp.float32
    )


LANES = 128
FAR_BUCKET = 31


def lane_ids():
    return lax.broadcasted_iota(jnp.int32, (1, LANES), 1)


def split_three(values):
    first = values.astype(jnp.bfloat16)
    rest = values - first.astype(jnp.float32)
    second = rest.astype(jnp.bfloat16)
    third = (rest - second.astype(jnp.float32)).astype(jnp.bfloat16)
    return (first, second, third)


def place_three(base, values, lane_mod, start):
    for step, part in enumerate(split_three(values)):
        base = jnp.where(lane_mod == start + step, part.astype(jnp.float32), base)
    return base


def key_place(block, n, h):
    return (block, pl.ds(0, h)) if block < n else (2 * n - 1 - block, pl.ds(h, h))


def fill_tables(bias_ref, out, turned):
    tile = (LANES, LANES)
    rows = bias_rows(bias_ref, turned)
    for head in range(HEADS):
        out[head, 0] = jnp.full(tile, MASKED, jnp.float32)
        for step in range(2):
            wide = jnp.broadcast_to(rows[step][head : head + 1, :], (LANES, 2 * LANES))
            out[head, step + 1] = pltpu.roll(wide, 0, 1, stride=1, stride_axis=0)[:, :LANES]
        out[head, 3] = jnp.zeros(tile, jnp.float32)


def bias_rows(bias_ref, turned):
    span = lax.broadcasted_iota(jnp.int32, (1, 2 * LANES), 1)
    far = bias_ref[:, FAR_BUCKET : FAR_BUCKET + 1]
    rows = []
    for step in range(2):
        if turned:
            distance = LANES * step + jnp.where(span < LANES, span, span - 2 * LANES)
        else:
            distance = LANES * step + jnp.where(span < LANES, -span, 2 * LANES - span)
        bucket = jnp.zeros(span.shape, jnp.int32)
        for threshold in bucket_bounds():
            bucket = bucket + jnp.where(distance >= threshold, 1, 0)
        picked = jnp.zeros((HEADS, 2 * LANES), jnp.float32)
        for index in range(bias_ref.shape[1]):
            picked = jnp.where(bucket == index, bias_ref[:, index : index + 1] - far, picked)
        rows.append(jnp.where(distance < 0, MASKED, picked))
    return rows


def near_tiles(table_ref, side, query_block, block, h, turned):
    per = h // LANES
    rows = []
    for outer in range(per):
        tiles = []
        for inner in range(per):
            query_tile, key_tile = (inner, outer) if turned else (outer, inner)
            gap = per * query_block + query_tile - (per * block + key_tile)
            tiles.append(table_ref[side, jnp.clip(gap, -1, 2) + 1])
        rows.append(jnp.concatenate(tiles, axis=1))
    return jnp.concatenate(rows, axis=0)


def attend_kernel(n, h, q_ref, k_ref, v_ref, qe_ref, ke_ref, far_ref, table_ref, o_ref, lse_ref):
    part = lax.axis_index("ctx")
    lane = lane_ids()
    lane_mod = lane % HEAD_DIM
    low = lane < HEAD_DIM
    for turn in range(2):
        spot = pl.ds(turn * h, h)
        query_block = part if turn == 0 else 2 * n - 1 - part
        count = n if turn == 0 else 2 * n
        outs, logs = [], []
        for side in range(2):
            mine = low if side == 0 else jnp.logical_not(low)
            extra = place_three(jnp.zeros((1, LANES), jnp.float32), far_ref[0, side : side + 1, :], lane_mod, 5)
            query = q_ref[spot, :].astype(jnp.float32) * HEAD_DIM ** (-0.5)
            query = jnp.where(mine, query, qe_ref[spot, :].astype(jnp.float32) + extra)
            query = query.astype(jnp.bfloat16)
            scores = []
            for block in range(count):
                owner, place = key_place(block, n, h)
                ahead = lax.rem(owner - part + n, n)
                key = jnp.where(mine, k_ref[ahead, 0, place, :], ke_ref[owner, place, :])
                one = product_last(query, key)
                if turn == 0 or block >= n - 1:
                    one = one + near_tiles(table_ref, side, query_block, block, h, False)
                scores.append(one)
            top = scores[0]
            for one in scores[1:]:
                top = jnp.maximum(top, one)
            top = jnp.max(top, axis=-1, keepdims=True)
            total = jnp.zeros((h, LANES), jnp.float32)
            for block in range(count):
                owner, place = key_place(block, n, h)
                ahead = lax.rem(owner - part + n, n)
                value = jnp.where(mine, v_ref[ahead, 0, place, :], jnp.ones((), jnp.bfloat16))
                weight = jnp.exp(scores[block] - top).astype(jnp.bfloat16)
                total = total + matrix_multiply(weight, value)
            spare = HEAD_DIM if side == 0 else 0
            sums = total[:, spare : spare + 1]
            outs.append(total / sums)
            logs.append(jnp.broadcast_to(top + jnp.log(sums), (h, LANES)))
        o_ref[spot, :] = jnp.where(low, outs[0], outs[1]).astype(o_ref.dtype)
        lse_ref[spot, :] = jnp.where(low, logs[1], logs[0])


def attend_back_pair(
    n, h, pair, pairs, q_ref, k_ref, v_ref, do_ref, o_ref, lse_ref, qe_ref, ke_ref, far_ref, table_ref,
    dq_ref, dkv_ref, other_ref, qx_ref, gx_ref, dq_sum, made_ref, send_sem, recv_sem,
):
    part = lax.axis_index("ctx")
    parity = lax.rem(pair, 2)

    def pass_on(turn, pair):
        slot = lax.rem(pair, 2)
        columns = pl.ds(pl.multiple_of(pair * LANES, LANES), LANES)
        return pltpu.make_async_remote_copy(
            src_ref=made_ref.at[slot, turn], dst_ref=other_ref.at[turn - 1, :, :, columns],
            send_sem=send_sem.at[slot, turn - 1], recv_sem=recv_sem.at[pair, turn - 1],
            device_id={"ctx": lax.rem(part + turn, n)}, device_id_type=MESH,
        )

    @pl.when(pair >= 2)
    def _():
        for turn in range(1, n):
            pass_on(turn, pair - 2).wait_send()

    lane = lane_ids()
    lane_mod = lane % HEAD_DIM
    low = lane < HEAD_DIM
    spare = jnp.where(lane_mod < 3, 1.0, 0.0).astype(jnp.bfloat16)
    both = do_ref[...].astype(jnp.float32) * o_ref[...].astype(jnp.float32)
    for side in range(2):
        mine = low if side == 0 else jnp.logical_not(low)
        extra = place_three(jnp.zeros((1, LANES), jnp.float32), far_ref[0, side : side + 1, :], lane_mod, 5)
        extra = place_three(qe_ref[...].astype(jnp.float32) + extra, -lse_ref[...], lane_mod, 8)
        query = q_ref[...].astype(jnp.float32) * HEAD_DIM ** (-0.5)
        qx_ref[side] = jnp.where(mine, query, extra).astype(jnp.bfloat16)
        dots = jnp.sum(jnp.where(mine, both, 0.0), axis=-1, keepdims=True)
        dots = jnp.broadcast_to(dots, both.shape)
        extra = place_three(jnp.zeros(both.shape, jnp.float32), -dots, lane_mod, 0)
        gx_ref[side] = jnp.where(mine, do_ref[...].astype(jnp.float32), extra).astype(jnp.bfloat16)
    dq_sum[...] = jnp.zeros_like(dq_sum)
    for block in range(2 * n):
        owner, place = key_place(block, n, h)
        ahead = lax.rem(owner - part + n, n)
        key_turned = jnp.transpose(k_ref[ahead, 0, place, :].astype(jnp.float32)).astype(jnp.bfloat16)
        key_grads, value_grads = [], []
        for side in range(2):
            mine = low if side == 0 else jnp.logical_not(low)
            key = jnp.where(mine, k_ref[ahead, 0, place, :], ke_ref[owner, place, :])
            value = jnp.where(mine, v_ref[ahead, 0, place, :], spare)
            key_grad = jnp.zeros((h, LANES), jnp.float32)
            value_grad = jnp.zeros((h, LANES), jnp.float32)
            for turn in range(2):
                if turn == 0 and block >= n:
                    continue
                spot = pl.ds(turn * h, h)
                query_block = part if turn == 0 else 2 * n - 1 - part
                query = qx_ref[side, spot, :]
                scores = product_last(key, query)
                if turn == 0 or block >= n - 1:
                    scores = scores + near_tiles(table_ref, side, query_block, block, h, True)
                prob = jnp.exp(scores)
                prob_grad = product_last(value, gx_ref[side, spot, :])
                score_grad = (prob * prob_grad).astype(jnp.bfloat16)
                value_grad = value_grad + matrix_multiply(prob.astype(jnp.bfloat16), do_ref[spot, :])
                key_grad = key_grad + matrix_multiply(score_grad, query)
                dq_sum[side, :, spot] += matrix_multiply(key_turned, score_grad)
            key_grads.append(key_grad)
            value_grads.append(value_grad)
        key_grad = jnp.where(low, key_grads[0], key_grads[1])
        made_ref[parity, ahead, 0, place, :] = key_grad.astype(made_ref.dtype)
        value_grad = jnp.where(low, value_grads[0], value_grads[1])
        made_ref[parity, ahead, 1, place, :] = value_grad.astype(made_ref.dtype)
    for turn in range(1, n):
        pass_on(turn, pair).start()
    dkv_ref[...] = made_ref[parity, 0]
    upper = lax.broadcasted_iota(jnp.int32, (LANES, 1), 0) < HEAD_DIM
    grads = jnp.where(upper, dq_sum[0], dq_sum[1]) * HEAD_DIM ** (-0.5)
    dq_ref[...] = jnp.transpose(grads).astype(dq_ref.dtype)

    @pl.when(pair == pairs - 1)
    def _():
        for turn in range(1, n):
            for last in (pairs - 2, pairs - 1):
                pass_on(turn, last).wait_send()
            for one in range(HEADS // 2):
                pass_on(turn, one).wait_recv()


def pass_pieces(pieces_ref, sum_ref, landed, mirror_out, mirror_in, own_sem, send_sem, recv_sem, mirror_sem):
    me = lax.axis_index("exp")
    count = pieces_ref.shape[0]
    half = count // 2
    base = lax.div(me, half) * half
    here = lax.rem(me, half)
    mirror = lax.rem(me + half, count)

    def to(peer, slot):
        return [
            pltpu.make_async_remote_copy(
                src_ref=pieces_ref.at[lax.rem(base + peer + half * k, count)], dst_ref=landed.at[k, slot],
                send_sem=send_sem.at[k, peer], recv_sem=recv_sem.at[k, slot],
                device_id={"exp": base + peer}, device_id_type=MESH,
            )
            for k in range(2)
        ]

    own = [
        pltpu.make_async_copy(pieces_ref.at[lax.rem(me + half * k, count)], landed.at[k, here], own_sem.at[k])
        for k in range(2)
    ]
    across = pltpu.make_async_remote_copy(
        src_ref=mirror_out, dst_ref=mirror_in, send_sem=mirror_sem.at[0], recv_sem=mirror_sem.at[1],
        device_id={"exp": mirror}, device_id_type=MESH,
    )

    def total(k):
        total = landed[k, 0].astype(jnp.float32)
        for source in range(1, half):
            total = total + landed[k, source].astype(jnp.float32)
        return total

    def begin(between):
        for copy in own:
            copy.start()

        def push(turn, carry):
            between(turn)
            for copy in to(lax.rem(here + turn, half), here):
                copy.start()
            return carry

        lax.fori_loop(1, half, push, 0)

    def middle():
        for copy in own:
            copy.wait()

        def settle(turn, carry):
            peer = lax.rem(here + turn, half)
            for copy in to(peer, peer):
                copy.wait_recv()
            for copy in to(peer, here):
                copy.wait_send()
            return carry

        lax.fori_loop(1, half, settle, 0)
        mirror_out[...] = total(1).astype(mirror_out.dtype)
        across.start()

    def end():
        across.wait()
        sum_ref[...] = (total(0) + mirror_in[...].astype(jnp.float32)).astype(sum_ref.dtype)

    return begin, middle, end


def pieces_scratch(pieces):
    one, half = pieces.shape[1:], pieces.shape[0] // 2
    dma = pltpu.SemaphoreType.DMA
    return [
        pltpu.VMEM((2, half) + one, pieces.dtype),
        pltpu.VMEM(one, pieces.dtype),
        pltpu.VMEM(one, pieces.dtype),
        dma((2,)),
        dma((2, half)),
        dma((2, half)),
        dma((2,)),
    ]


def attend_back_kernel(n, h, *refs):
    part = lax.axis_index("ctx")

    @pl.when(pl.program_id(0) == 0)
    def _():
        barrier = pltpu.get_barrier_semaphore()
        for turn in range(1, n):
            core = lax.rem(part + turn, n)
            pl.semaphore_signal(barrier, inc=1, device_id={"ctx": core}, device_id_type=MESH)
        pl.semaphore_wait(barrier, n - 1)

    attend_back_pair(n, h, pl.program_id(0), pl.num_programs(0), *refs)


def attend_back(query, kv, out_grad, out, lse, qe, ke, far, turned):
    rows = query.shape[0]
    n = kv.shape[0]
    every = n * rows
    h = rows // 2
    pairs = HEADS // 2
    own = pl.BlockSpec((rows, LANES), lambda i: (0, i))
    return pl.pallas_call(
        functools.partial(attend_back_kernel, n, h),
        grid=(pairs,),
        in_specs=[
            own,
            pl.BlockSpec((n, 1, rows, LANES), lambda i: (0, 0, 0, i)),
            pl.BlockSpec((n, 1, rows, LANES), lambda i: (0, 1, 0, i)),
            own,
            own,
            own,
            pl.BlockSpec((rows, LANES), lambda i: (0, 0)),
            pl.BlockSpec((n, rows, LANES), lambda i: (0, 0, 0)),
            pl.BlockSpec((1, 2, LANES), lambda i: (i, 0, 0)),
            pl.BlockSpec((2, 4, LANES, LANES), lambda i: (i, 0, 0, 0)),
        ],
        out_specs=[own, pl.BlockSpec((2, rows, LANES), lambda i: (0, 0, i)), pl.BlockSpec(memory_space=pl.ANY)],
        out_shape=[
            jax.ShapeDtypeStruct((rows, MODEL_WIDTH), jnp.bfloat16),
            jax.ShapeDtypeStruct((2, rows, MODEL_WIDTH), jnp.bfloat16),
            jax.ShapeDtypeStruct((n - 1, 2, rows, MODEL_WIDTH), jnp.bfloat16),
        ],
        scratch_shapes=[
            pltpu.VMEM((2, rows, LANES), jnp.bfloat16),
            pltpu.VMEM((2, rows, LANES), jnp.bfloat16),
            pltpu.VMEM((2, LANES, rows), jnp.float32),
            pltpu.VMEM((2, n, 2, rows, LANES), jnp.bfloat16),
            pltpu.SemaphoreType.DMA((2, n - 1)),
            pltpu.SemaphoreType.DMA((pairs, n - 1)),
        ],
        compiler_params=pltpu.CompilerParams(
            vmem_limit_bytes=VMEM_BYTES, collective_id=6, has_side_effects=True
        ),
        cost_estimate=SMALL_COST,
        name="attend_back",
    )(query, kv, kv, out_grad, out, lse, qe, ke, far, turned)


def segment_columns(row):
    wide = jnp.broadcast_to(row.astype(jnp.float32), (LANES, LANES))
    return jnp.transpose(wide).astype(jnp.int32)


def fill_segments(n, h, segments_ref, qe_ref, ke_ref):
    part = lax.axis_index("ctx")
    lane_mod = lane_ids() % HEAD_DIM
    documents = lane_mod < 5
    ones = jnp.where((lane_mod >= 5) & (lane_mod < 11), 1.0, 0.0)
    for block in range(2 * n):
        owner = block if block < n else 2 * n - 1 - block
        first = 0 if block < n else h
        for step in range(0, h, LANES):
            column = segment_columns(segments_ref[:, block * h + step : block * h + step + LANES])
            side = jnp.where(documents & (column != lane_mod), MASKED, ones)
            ke_ref[owner, first + step : first + step + LANES, :] = side.astype(jnp.bfloat16)
    for turn in range(2):
        block = part if turn == 0 else 2 * n - 1 - part
        for step in range(0, h, LANES):
            spot = pl.ds(pl.multiple_of(block * h + step, LANES), LANES)
            column = segment_columns(segments_ref[:, spot])
            side = jnp.where(documents & (column == lane_mod), 1.0, 0.0)
            qe_ref[turn * h + step : turn * h + step + LANES, :] = side.astype(jnp.bfloat16)


ROW_BLOCK = 256
FF_BLOCK = 512
GELU_SLOPE = float(np.sqrt(2.0 / np.pi))
GELU_CUBE = 0.044715


def group_mask(first, last):
    lane = lane_ids()
    return (lane >= first * ADAPTER_RANK) & (lane < last * ADAPTER_RANK)


def keep_group(values, first, last):
    return jnp.where(group_mask(first, last), values, 0.0).astype(jnp.bfloat16)


def send_rows(dest_ref, rows, out_ref):
    count = rows.shape[0]
    for start in range(0, out_ref.shape[0], ROW_BLOCK):
        size = min(ROW_BLOCK, out_ref.shape[0] - start)
        slot = lax.broadcasted_iota(jnp.int32, (size, count), 0) + start
        hot = (slot == dest_ref[0:1, :]) | (slot == dest_ref[1:2, :])
        hot = jnp.where(hot, 1.0, 0.0).astype(jnp.bfloat16)
        out_ref[start : start + size, :] = matrix_multiply(hot, rows).astype(out_ref.dtype)


def find_routes(capacity, rows_ref, grad_ref, routes_ref, dest_rows_ref, dest_cols_ref, out_ref):
    count = grad_ref.shape[0]
    wide = jnp.concatenate([rows_ref[...].astype(jnp.float32), jnp.zeros((LANES - 2, count), jnp.float32)], axis=0)
    routes_ref[...] = jnp.transpose(wide)[:, :2].astype(jnp.int32)
    experts = out_ref.shape[0] // capacity
    down = lax.broadcasted_iota(jnp.int32, (count, count), 0)
    across = lax.broadcasted_iota(jnp.int32, (count, count), 1)
    after = jnp.where(across < down, 1.0, 0.0).astype(jnp.bfloat16)
    ids = lax.broadcasted_iota(jnp.int32, (count, LANES), 1)
    hots = [jnp.where(ids == routes_ref[:, k : k + 1], 1.0, 0.0) for k in range(2)]
    ranks = matrix_multiply(after, (hots[0] + hots[1]).astype(jnp.bfloat16))
    wide = jnp.zeros((count, LANES), jnp.float32)
    for k in range(2):
        slot = jnp.sum(hots[k] * ranks, axis=1, keepdims=True).astype(jnp.int32)
        dest = routes_ref[:, k : k + 1] * capacity + slot
        dest_cols_ref[:, k : k + 1] = dest
        wide = jnp.where(ids == k, dest.astype(jnp.float32), wide)
    dest_rows_ref[...] = jnp.transpose(wide)[:2].astype(jnp.int32)
    send_rows(dest_rows_ref, grad_ref[...], out_ref)


def whole(shape):
    return jax.ShapeDtypeStruct(shape[0], shape[1])


def run(kernel, name, outs, *operands, scratch=(), outside=0, **params):
    vmem, anywhere = pl.BlockSpec(memory_space=pltpu.VMEM), pl.BlockSpec(memory_space=pl.ANY)
    return pl.pallas_call(
        kernel,
        in_specs=[vmem] * (len(operands) - outside) + [anywhere] * outside,
        out_specs=[vmem] * len(outs),
        out_shape=[whole(shape) for shape in outs],
        scratch_shapes=list(scratch),
        compiler_params=pltpu.CompilerParams(vmem_limit_bytes=VMEM_BYTES, **params),
        cost_estimate=SMALL_COST,
        name=name,
    )(*operands)


def owners_of(share, cuts):
    def has_own(owner):
        return (owner * share < cuts[1]) | ((owner + 1) * share > cuts[2])

    def owner_of(row, end):
        return lax.div(cuts[1] + row * FF + end * (FF - 1), share)

    return has_own, owner_of


def by_parity(owner, cores):
    return (lax.axis_index("ctx") == owner % 2) if cores == 2 else True


def fetch_parts(
    share, tiles, cuts, halved, capacity, adapters_ref, pick_ref, bias_ref, route_rows_ref, grad_ref,
    own_in, home_ref, table_ref, routes_ref, dest_rows_ref, dest_cols_ref, out_ref, mask_ref, push_grads,
    padded_ref, by_adapter, sent, home_out, home_in, own_send, own_recv, relay_send, relay_recv, local_sem,
    home_send, home_recv,
):
    part, me = lax.axis_index("ctx"), lax.axis_index("exp")
    cores, experts = lax.axis_size("ctx"), lax.axis_size("exp")
    window = sent.shape[1]
    per_row = FF // LANES
    has_own, owner_of = owners_of(share, cuts)

    padded_ref[...] = jnp.zeros_like(padded_ref)
    offset = lax.rem(me * share, LANES)
    lane = lane_ids()
    held = jnp.zeros((ADAPTER_COUNT, LANES), jnp.float32)
    for tile in range(tiles):
        slab = adapters_ref[:, tile * LANES : min((tile + 1) * LANES, share)] if tile * LANES < share else held * 0.0
        if slab.shape[1] < LANES:
            rest = jnp.zeros((ADAPTER_COUNT, LANES - slab.shape[1]), jnp.float32)
            slab = jnp.concatenate([slab, rest], axis=1)
        slab = pltpu.roll(slab, offset, 1)
        one = jnp.where(lane < offset, held, slab)
        padded_ref[:, (per_row + tile) * LANES : (per_row + tile + 1) * LANES] = one
        by_adapter[pl.ds(tile, ADAPTER_COUNT, stride=window), :] = one
        held = slab
    for tile in range(tiles, window):
        by_adapter[pl.ds(tile, ADAPTER_COUNT, stride=window), :] = jnp.zeros((ADAPTER_COUNT, LANES), jnp.float32)
    for peer in range(experts):
        mask_ref[peer] = jnp.where(lane % ADAPTER_COUNT == pick_ref[peer], 1.0, 0.0)
        chosen = by_adapter[:window, :]
        for adapter in range(1, ADAPTER_COUNT):
            rows = by_adapter[adapter * window : (adapter + 1) * window, :]
            chosen = jnp.where(pick_ref[peer] == adapter, rows, chosen)
        sent[peer] = chosen.astype(jnp.bfloat16)

    def own_copy(peer, slot):
        return pltpu.make_async_remote_copy(
            src_ref=sent.at[peer], dst_ref=own_in.at[slot], send_sem=own_send.at[peer],
            recv_sem=own_recv.at[slot], device_id={"exp": peer}, device_id_type=MESH,
        )

    def relay(owner):
        return pltpu.make_async_remote_copy(
            src_ref=own_in.at[owner], dst_ref=own_in.at[owner], send_sem=relay_send.at[owner],
            recv_sem=relay_recv.at[owner], device_id={"ctx": 1 - part}, device_id_type=MESH,
        )

    handled = has_own(me) & (by_parity(me, cores) if cores == 2 else has_own(me))

    def each_peer(action):
        def one(turn, carry):
            action(lax.rem(me + turn, experts))
            return carry

        lax.fori_loop(1, experts, one, 0)

    kept = pltpu.make_async_copy(sent.at[me], own_in.at[me], local_sem.at[0])

    @pl.when(handled)
    def _():
        each_peer(lambda peer: own_copy(peer, me).start())
        kept.start()

    cut = FF // 2

    def home_pack(row, peer):
        tile = per_row + cuts[1] // LANES + row * per_row - lax.div(me * share, LANES)
        halves = [padded_ref[:, pl.ds(pl.multiple_of(tile * LANES + k * cut, LANES), cut)] for k in range(2)]
        home_out[peer] = jnp.concatenate(halves, axis=0).astype(jnp.bfloat16)

    def home_copy(row, peer, slot):
        return pltpu.make_async_remote_copy(
            src_ref=home_out.at[peer], dst_ref=home_in.at[slot], send_sem=home_send.at[peer],
            recv_sem=home_recv.at[slot], device_id={"exp": peer}, device_id_type=MESH,
        )

    def each_home(action):
        def one(peer, carry):
            row = part * experts + peer
            low, high = owner_of(row, 0), owner_of(row, 1)

            @pl.when((low == me) & (peer != me))
            def _():
                action(home_copy(row, peer, 0))

            @pl.when((high == me) & (low != me) & (peer != me))
            def _():
                action(home_copy(row, peer, 1))

            return carry

        lax.fori_loop(0, experts, one, 0)

    if halved:

        def pack(peer, carry):
            row = part * experts + peer

            @pl.when((owner_of(row, 0) == me) | (owner_of(row, 1) == me))
            def _():
                home_pack(row, peer)

            return carry

        lax.fori_loop(0, experts, pack, 0)
        each_home(lambda copy: copy.start())
        my_row = part * experts + me
        my_low, my_high = owner_of(my_row, 0), owner_of(my_row, 1)
        for slot, owner, needed in ((0, my_low, True), (1, my_high, my_high != my_low)):

            @pl.when(needed & (owner == me))
            def _():
                pltpu.make_async_copy(home_out.at[me], home_in.at[slot], local_sem.at[1 + slot]).start()

    find_routes(capacity, route_rows_ref, grad_ref, routes_ref, dest_rows_ref, dest_cols_ref, out_ref)
    push_grads()
    if cores == 2:
        fill_tables(bias_ref, table_ref, False)

    def arrive():
        for owner in range(experts):
            if has_own(owner):
                here = by_parity(owner, cores)

                @pl.when((me != owner) & here)
                def _():
                    own_copy(owner, owner).wait_recv()

                if cores == 2:

                    @pl.when((me == owner) & here)
                    def _():
                        kept.wait()

                    @pl.when(here)
                    def _():
                        relay(owner).start()

        if cores != 2:

            @pl.when(has_own(me))
            def _():
                kept.wait()

        else:
            for owner in range(experts):
                if has_own(owner):
                    here = by_parity(owner, cores)

                    @pl.when(jnp.logical_not(here))
                    def _():
                        relay(owner).wait_recv()

    def finish():
        if halved:
            for slot, owner, needed in ((0, my_low, True), (1, my_high, my_high != my_low)):

                @pl.when(needed & (owner == me))
                def _():
                    pltpu.make_async_copy(home_out.at[me], home_in.at[slot], local_sem.at[1 + slot]).wait()

                @pl.when(needed & (owner != me))
                def _():
                    home_copy(my_row, me, slot).wait_recv()

            row = home_in[0].astype(jnp.float32)
            row = row + jnp.where(my_high != my_low, home_in[1].astype(jnp.float32), 0.0)
            home_ref[...] = row.astype(jnp.bfloat16)
            each_home(lambda copy: copy.wait_send())
        else:
            home_ref[...] = jnp.zeros_like(home_ref)

        @pl.when(handled)
        def _():
            each_peer(lambda peer: own_copy(peer, me).wait_send())

        if cores == 2:
            for owner in range(experts):
                if has_own(owner):

                    @pl.when(by_parity(owner, cores))
                    def _():
                        relay(owner).wait_send()

    return arrive, finish


SOURCE_GROUP = 4


def forward_kernel(
    share, tiles, cuts, halved, capacity, adapters_ref, pick_ref, tokens_ref, grad_ref, gain_ref, bias_ref, segments_ref,
    router_in_ref, route_rows_ref, weight_hbm, out_weight_hbm,
    home_ref, routes_ref, dest_rows_ref, dest_cols_ref, mask_ref,
    q_hbm, kv_hbm, xn_hbm, u_ref, own_down_ref, own_up_ref, own_router_ref, turned_hbm, o_hbm, lse_hbm,
    qe_ref, ke_ref, far_ref, router_ref, hidden_ref, xn_two_ref, w_ref, ur_ref, gates_ref, gate_slots_ref, side_ref,
    rows_ref, came_hbm,
    q_ref, kv_ref, xn_ref, o_ref, lse_ref, kv_own, table_ref, turned_ref, weight_ref, out_weight_ref, flat, down_wide,
    load_sem, store_sem, local_sem, kv_send, kv_recv, row_send, row_recv, sent_rows, own_in, *fetching,
):
    part, me = lax.axis_index("ctx"), lax.axis_index("exp")
    cores, experts = lax.axis_size("ctx"), lax.axis_size("exp")
    has_own, _ = owners_of(share, cuts)
    if cores > 2:
        turned_ref = table_ref
    loads = [
        pltpu.make_async_copy(source, target, load_sem.at[i])
        for i, (source, target) in enumerate(
            ((weight_hbm, weight_ref), (out_weight_hbm, out_weight_ref))
        )
    ]
    for load in loads:
        load.start()
    barrier = pltpu.get_barrier_semaphore()

    def greet(turn, carry):
        peer = lax.rem(me + turn, experts)
        pl.semaphore_signal(barrier, inc=1, device_id={"exp": peer}, device_id_type=MESH)
        return carry

    lax.fori_loop(1, experts, greet, 0)
    for turn in range(1, cores):
        core = lax.rem(part + turn, cores)
        pl.semaphore_signal(barrier, inc=1, device_id={"ctx": core}, device_id_type=MESH)
    pl.semaphore_wait(barrier, experts + cores - 2)

    def row_copy(peer, slot):
        return pltpu.make_async_remote_copy(
            src_ref=sent_rows.at[pl.ds(pl.multiple_of(peer * capacity, 16), capacity)], dst_ref=came_hbm.at[slot], send_sem=row_send.at[peer],
            recv_sem=row_recv.at[slot], device_id={"exp": peer}, device_id_type=MESH,
        )

    own_rows = pltpu.make_async_copy(
        sent_rows.at[pl.ds(pl.multiple_of(me * capacity, 16), capacity)], came_hbm.at[me], local_sem.at[2]
    )

    def push_grads():
        own_rows.start()
        push_rows(me, experts, lambda peer: row_copy(peer, me).start())

    arrive, finish = fetch_parts(
        share, tiles, cuts, halved, capacity, adapters_ref, pick_ref, bias_ref, route_rows_ref, grad_ref,
        own_in, home_ref, table_ref, routes_ref, dest_rows_ref, dest_cols_ref, sent_rows, mask_ref, push_grads, *fetching
    )
    xn_ref[...] = rms_scale(tokens_ref[...].astype(jnp.float32), gain_ref[0:1, :]).astype(jnp.bfloat16)
    arrive()

    flat[...] = jnp.zeros_like(flat)
    for owner in range(experts):
        if has_own(owner):
            first = owner * share // LANES
            rows = slice(first, first + tiles)
            flat[rows, :] = flat[rows, :] + own_in[owner].astype(jnp.float32)[:tiles]
    columns = 6 * ADAPTER_RANK
    quarter = MODEL_WIDTH // 4
    rows = [flat[pl.ds(step, quarter, stride=3), :] for step in range(3)]
    blank = jnp.zeros((quarter, LANES - columns), jnp.float32)
    for step in range(4):
        tile, place = divmod(step * columns, LANES)
        pieces = [rows[tile][:, place : place + columns]]
        if place + columns > LANES:
            pieces.append(rows[tile + 1][:, : place + columns - LANES])
        down_wide[pl.ds(step, quarter, stride=4), :] = jnp.concatenate(pieces + [blank], axis=1)
    own_down_ref[...] = down_wide[...].astype(jnp.bfloat16)
    per_model = MODEL_WIDTH // LANES
    empty = jnp.zeros((LANES - 5 * ADAPTER_RANK, LANES), jnp.float32)
    for step in range(per_model):
        one = flat[pl.ds(cuts[0] // LANES + step, 5 * ADAPTER_RANK, stride=per_model), :]
        one = jnp.concatenate([one, empty], axis=0).astype(jnp.bfloat16)
        own_up_ref[:, step * LANES : (step + 1) * LANES] = one

    u_ref[...] = keep_group(matrix_multiply(xn_ref[...], own_down_ref[...]), 0, 3)
    loads[0].wait()

    def made(group):
        inner = jnp.where(group_mask(group, group + 1), u_ref[...], jnp.zeros((), jnp.bfloat16))
        spot = slice(group * MODEL_WIDTH, (group + 1) * MODEL_WIDTH)
        base = matrix_multiply(xn_ref[...], weight_ref[:, spot])
        return (base + ADAPTER_SCALE * matrix_multiply(inner, own_up_ref[...])).astype(jnp.bfloat16)

    def kv_copy(which, turn):
        return pltpu.make_async_remote_copy(
            src_ref=kv_own.at[which], dst_ref=kv_ref.at[cores - turn, which],
            send_sem=kv_send.at[which, turn - 1], recv_sem=kv_recv.at[which, turn - 1],
            device_id={"ctx": lax.rem(part + turn, cores)}, device_id_type=MESH,
        )

    for which in range(2):
        kv_own[which] = made(which + 1)
        for turn in range(1, cores):
            kv_copy(which, turn).start()
        pltpu.make_async_copy(kv_own.at[which], kv_ref.at[0, which], local_sem.at[which]).start()
    q_ref[...] = made(0)
    stores = [
        pltpu.make_async_copy(source, target, store_sem.at[i])
        for i, (source, target) in enumerate(
            ((q_ref, q_hbm), (xn_ref, xn_hbm), (turned_ref, turned_hbm), (kv_ref, kv_hbm), (o_ref, o_hbm), (lse_ref, lse_hbm))
        )
    ]
    stores[0].start()
    stores[1].start()
    fill_tables(bias_ref, turned_ref, True)
    stores[2].start()
    if cores > 2:
        stores.pop(2).wait()
        fill_tables(bias_ref, table_ref, False)
    lane = lane_ids()
    router = []
    for row in range(ADAPTER_RANK):
        tile, place = divmod(row * experts, LANES)
        one = flat[cuts[2] // LANES + tile : cuts[2] // LANES + tile + 1, :]
        one = pltpu.roll(one, LANES - place, 1) if place else one
        router.append(jnp.where(lane < experts, one, 0.0))
    above = jnp.zeros((4 * ADAPTER_RANK, LANES), jnp.float32)
    below = jnp.zeros((LANES - 5 * ADAPTER_RANK, LANES), jnp.float32)
    own_router_ref[...] = jnp.concatenate([above] + router + [below], axis=0).astype(jnp.bfloat16)
    wide = jnp.zeros((LANES - experts, MODEL_WIDTH), jnp.float32)
    wide = jnp.concatenate([router_in_ref[...].astype(jnp.float32), wide], axis=0)
    router_ref[...] = jnp.transpose(wide).astype(jnp.bfloat16)
    half = tokens_ref.shape[0] // 2
    fill_segments(cores, half, segments_ref, qe_ref, ke_ref)
    far = jnp.broadcast_to(bias_ref[:, FAR_BUCKET : FAR_BUCKET + 1], (HEADS, LANES))
    for pair in range(HEADS // 2):
        far_ref[pair] = far[2 * pair : 2 * pair + 2]
    for which in range(2):
        for turn in range(1, cores):
            kv_copy(which, turn).wait()
        pltpu.make_async_copy(kv_own.at[which], kv_ref.at[0, which], local_sem.at[which]).wait()
    stores[-3].start()

    def attend(pair, carry):
        spot = pl.ds(pl.multiple_of(pair * LANES, LANES), LANES)
        attend_kernel(
            cores, half, q_ref.at[:, spot], kv_ref.at[:, pl.ds(0, 1), :, spot], kv_ref.at[:, pl.ds(1, 1), :, spot],
            qe_ref, ke_ref, far_ref.at[pl.ds(pair, 1)], table_ref.at[pl.ds(2 * pair, 2)],
            o_ref.at[:, spot], lse_ref.at[:, spot],
        )
        return carry

    lax.fori_loop(0, HEADS // 2, attend, 0)
    stores[-2].start()
    stores[-1].start()
    loads[1].wait()
    after_kernel(
        capacity, o_ref, tokens_ref, grad_ref, out_weight_ref, own_down_ref, own_up_ref, gain_ref, router_ref,
        own_router_ref, routes_ref, dest_rows_ref, dest_cols_ref,
        hidden_ref, xn_two_ref, w_ref, ur_ref, gates_ref, gate_slots_ref, side_ref, rows_ref,
    )
    own_rows.wait()

    def settle(turn, carry):
        peer = lax.rem(me + turn, experts)
        row_copy(peer, peer).wait_recv()
        row_copy(peer, me).wait_send()
        return carry

    lax.fori_loop(1, experts, settle, 0)
    finish()
    for store in stores:
        store.wait()


def push_rows(me, experts, action, orders=None, lanes=(0, SOURCE_GROUP)):
    groups = experts // SOURCE_GROUP
    count = groups if orders is None else len(orders)

    def one(step, carry):
        turn = lax.rem(step + lax.axis_index("ctx") * (count // 2), count)
        if orders is None:
            order = lax.rem(turn + groups // 2, groups)
        else:
            order = orders[0]
            for place in range(1, count):
                order = jnp.where(turn == place, orders[place], order)
        lane = lax.rem(lax.div(step, count) + me, SOURCE_GROUP)
        peer = paired(order, lax.div(me, SOURCE_GROUP), groups) * SOURCE_GROUP + lane

        @pl.when(peer != me)
        def _():
            action(peer)

        return carry

    lax.fori_loop(count * lanes[0], count * lanes[1], one, 0)


def forward(
    share, tiles, cuts, halved, capacity, cores, experts, adapters, pick, tokens, grads, gains, bias, segments, router,
    routes, weight, out_weight,
):
    rows = tokens.shape[0]
    window = -(-tiles // 16) * 16
    piece = (2 * ADAPTER_COUNT, FF // 2)
    table = (HEADS, 4, LANES, LANES)
    length = -(-max(share * owner // LANES + window for owner in range(experts)) // 16) * 16
    bf16, f32 = jnp.bfloat16, jnp.float32
    vmem, anywhere = pl.BlockSpec(memory_space=pltpu.VMEM), pl.BlockSpec(memory_space=pl.ANY)
    dma = pltpu.SemaphoreType.DMA
    model, lanes = (rows, MODEL_WIDTH), (rows, LANES)
    kv = (cores, 2, rows, MODEL_WIDTH)
    outs = [
        (piece, bf16, vmem),
        ((rows, 2), jnp.int32, vmem),
        ((2, rows), jnp.int32, vmem),
        ((rows, 2), jnp.int32, vmem),
        ((experts, 1, LANES), f32, vmem),
        (model, bf16, anywhere),
        (kv, bf16, anywhere),
        (model, bf16, anywhere),
        (lanes, bf16, vmem),
        ((MODEL_WIDTH, LANES), bf16, vmem),
        ((LANES, MODEL_WIDTH), bf16, vmem),
        ((LANES, LANES), bf16, vmem),
        (table, f32, anywhere),
        (model, bf16, anywhere),
        (model, f32, anywhere),
        (lanes, bf16, vmem),
        ((cores, rows, LANES), bf16, vmem),
        ((HEADS // 2, 2, LANES), f32, vmem),
        ((MODEL_WIDTH, LANES), bf16, vmem),
        (model, f32, vmem),
        (model, bf16, vmem),
        (lanes, bf16, vmem),
        (lanes, bf16, vmem),
        (lanes, f32, vmem),
        ((experts, 1, LANES), f32, vmem),
        ((experts, 2 * ADAPTER_RANK, LANES), bf16, vmem),
        ((experts * capacity, MODEL_WIDTH), bf16, vmem),
        ((experts, capacity, MODEL_WIDTH), bf16, anywhere),
    ]
    return pl.pallas_call(
        functools.partial(forward_kernel, share, tiles, cuts, halved, capacity),
        in_specs=[vmem, pl.BlockSpec(memory_space=pltpu.SMEM)] + [vmem] * 7 + [anywhere] * 2,
        out_specs=[spec for _, _, spec in outs],
        out_shape=[whole(shape) for shape in outs],
        scratch_shapes=[
            pltpu.VMEM(model, bf16),
            pltpu.VMEM(kv, bf16),
            pltpu.VMEM(model, bf16),
            pltpu.VMEM(model, bf16),
            pltpu.VMEM(model, f32),
            pltpu.VMEM(kv[1:], bf16),
            pltpu.VMEM(table, f32),
            pltpu.VMEM(table if cores == 2 else (1, LANES), f32),
            pltpu.VMEM(weight.shape, bf16),
            pltpu.VMEM(out_weight.shape, bf16),
            pltpu.VMEM((length, LANES), f32),
            pltpu.VMEM((MODEL_WIDTH, LANES), f32),
            dma((2,)),
            dma((6,)),
            dma((3,)),
            dma((2, cores - 1)),
            dma((2, cores - 1)),
            dma((experts,)),
            dma((experts,)),
            pltpu.VMEM((experts * capacity, MODEL_WIDTH), bf16),
            pltpu.VMEM((experts, window, LANES), bf16),
            pltpu.VMEM((ADAPTER_COUNT, (2 * (FF // LANES) + window) * LANES), f32),
            pltpu.VMEM((ADAPTER_COUNT * window, LANES), f32),
            pltpu.VMEM((experts, window, LANES), bf16),
            pltpu.VMEM((experts,) + piece if halved else (1, LANES), bf16),
            pltpu.VMEM((2,) + piece if halved else (1, LANES), bf16),
            dma((experts,)),
            dma((experts,)),
            dma((experts,)),
            dma((experts,)),
            dma((3,)),
            dma((experts,)),
            dma((2,)),
        ],
        compiler_params=pltpu.CompilerParams(
            vmem_limit_bytes=VMEM_BYTES if cores <= 2 else VMEM_BYTES + (6 << 20), collective_id=2, has_side_effects=True
        ),
        cost_estimate=SMALL_COST,
        name="forward",
    )(adapters, pick, tokens, grads, gains, bias, segments, router, routes, weight, out_weight)


def after_kernel(
    capacity, o_ref, tokens_ref, grad_ref, weight_ref, down_ref, up_ref, gain_ref, router_ref, router_up_ref,
    route_cols_ref, dest_rows_ref, dest_cols_ref,
    hidden_ref, xn_ref, w_ref, ur_ref, gates_ref, gate_slots_ref, side_ref, out_ref,
):
    mixed = o_ref[...]
    w_ref[...] = keep_group(matrix_multiply(mixed, down_ref[...]), 3, 4)
    branch = matrix_multiply(mixed, weight_ref[...])
    branch = branch + ADAPTER_SCALE * matrix_multiply(w_ref[...], up_ref[...])
    hidden = tokens_ref[...].astype(jnp.float32) + branch
    hidden_ref[...] = hidden
    xn_ref[...] = rms_scale(hidden, gain_ref[1:2, :]).astype(jnp.bfloat16)
    send_rows(dest_rows_ref, xn_ref[...], out_ref)
    normed = xn_ref[...]
    inner = matrix_multiply(normed, down_ref[...])
    ur_ref[...] = keep_group(inner, 4, 5)
    logits = matrix_multiply(normed, router_ref[...])
    logits = logits + ADAPTER_SCALE * matrix_multiply(ur_ref[...], router_up_ref[...])
    lane = lane_ids()
    chosen = [
        jnp.sum(jnp.where(lane == route_cols_ref[:, k : k + 1], logits, 0.0), axis=1, keepdims=True)
        for k in range(2)
    ]
    top = jnp.maximum(chosen[0], chosen[1])
    powers = [jnp.exp(one - top) for one in chosen]
    total = powers[0] + powers[1]
    gates = [one / total for one in powers]
    gates_ref[...] = jnp.where(lane == 0, gates[0], jnp.where(lane == 1, gates[1], 0.0))
    lifted = ADAPTER_SCALE * product_last(grad_ref[...], up_ref[...])
    side = jnp.where(group_mask(5, 6), inner, jnp.where(group_mask(4, 5), lifted, 0.0))
    turned = jnp.transpose(side)[4 * ADAPTER_RANK : 6 * ADAPTER_RANK].astype(jnp.bfloat16)
    inside = lane < capacity
    for expert in range(gate_slots_ref.shape[0]):
        hots = [
            ((dest_cols_ref[:, k : k + 1] - expert * capacity) == lane) & inside for k in range(2)
        ]
        sums = jnp.where(hots[0], gates[0], jnp.where(hots[1], gates[1], 0.0))
        gate_slots_ref[expert] = jnp.sum(sums, axis=0, keepdims=True)
        hot = jnp.where(hots[0] | hots[1], 1.0, 0.0).astype(jnp.bfloat16)
        side_ref[expert] = matrix_multiply(turned, hot).astype(jnp.bfloat16)


def paired(order, place, count):
    total, bit = 0, 1
    while bit < count:
        total = total + lax.rem(lax.div(order, bit) + lax.div(place, bit), 2) * bit
        bit *= 2
    return total


def lay_out(rows_ref, out_ref):
    cut = FF // 2
    for pair in range(ADAPTER_RANK // 2):
        ones = [rows_ref[2 * pair + k].astype(jnp.float32) for k in range(2)]
        spot = slice(2 * pair * ADAPTER_COUNT, 2 * (pair + 1) * ADAPTER_COUNT)
        for half in range(2):
            rows = [one[half * ADAPTER_COUNT : (half + 1) * ADAPTER_COUNT] for one in ones]
            out_ref[spot, half * cut : (half + 1) * cut] = jnp.concatenate(rows, axis=0).astype(jnp.bfloat16)


def expert_kernel(
    capacity, halved, x_ref, side_ref, gate_ref, g_ref, mask_ref, first_hbm, second_hbm, hidden_ref,
    eo_ref, dx_ref, back_side_ref, dgate_ref, grad_ref,
    first_ref, second_ref, x_in, side_in, gate_in, dx_out, side_out, dgate_out,
    deo_ref, ui_ref, duo_ref, lift_ref, act_ref, dpre_ref,
    grad_sum, grad_out, grad_in, hidden_rows, hidden_came, hidden_all, hidden_send, hidden_recv,
    load_sem, own_sem, send_sem, recv_sem, back_send_sem, back_recv_sem, swap_sem,
):
    other_core = 1 - lax.axis_index("ctx")
    me = lax.axis_index("exp")
    experts = x_ref.shape[0]
    groups = experts // SOURCE_GROUP
    rows = SOURCE_GROUP * capacity
    loads = [
        pltpu.make_async_copy(first_hbm.at[0], first_ref, load_sem.at[0]),
        pltpu.make_async_copy(second_hbm.at[0], second_ref, load_sem.at[1]),
    ]
    for load in loads:
        load.start()

    barrier = pltpu.get_barrier_semaphore()

    def greet(step, carry):
        peer = lax.rem(me + step, experts)
        pl.semaphore_signal(barrier, inc=1, device_id={"exp": peer}, device_id_type=MESH)
        return carry

    lax.fori_loop(1, experts, greet, 0)
    if halved:
        pl.semaphore_signal(barrier, inc=1, device_id={"ctx": other_core}, device_id_type=MESH)
    pl.semaphore_wait(barrier, experts if halved else experts - 1)

    def outward(peer, slot):
        return [
            pltpu.make_async_remote_copy(
                src_ref=source.at[peer], dst_ref=target.at[slot], send_sem=send_sem.at[i, peer],
                recv_sem=recv_sem.at[i, slot], device_id={"exp": peer}, device_id_type=MESH,
            )
            for i, (source, target) in enumerate(((x_ref, x_in), (side_ref, side_in), (gate_ref, gate_in)))
        ]

    def homeward(peer, slot, kinds=(0, 1, 2)):
        pairs = ((dx_out, dx_ref), (side_out, back_side_ref), (dgate_out, dgate_ref))
        return [
            pltpu.make_async_remote_copy(
                src_ref=pairs[i][0].at[peer], dst_ref=pairs[i][1].at[slot], send_sem=back_send_sem.at[i, peer],
                recv_sem=back_recv_sem.at[i, slot], device_id={"exp": peer}, device_id_type=MESH,
            )
            for i in kinds
        ]

    def own_in():
        return [
            pltpu.make_async_copy(source.at[me], target.at[me], own_sem.at[i])
            for i, (source, target) in enumerate(((x_ref, x_in), (side_ref, side_in), (gate_ref, gate_in)))
        ]

    def own_back():
        return [
            pltpu.make_async_copy(source.at[me], target.at[me], own_sem.at[i + 3])
            for i, (source, target) in enumerate(
                ((dx_out, dx_ref), (side_out, back_side_ref), (dgate_out, dgate_ref))
            )
        ]

    for copy in own_in():
        copy.start()
    def plane_of(order):
        return paired(order, lax.div(me, SOURCE_GROUP), groups)

    def push(step, carry):
        order, lane = lax.div(step, SOURCE_GROUP), step
        if groups == 4:
            both = (step >= SOURCE_GROUP) & (step < 3 * SOURCE_GROUP)
            order = jnp.where(both, 2 - lax.rem(step + 1 - other_core, 2), order)
            lane = jnp.where(both, lax.div(step, 2), step)
        peer = plane_of(order) * SOURCE_GROUP + lax.rem(lane + me, SOURCE_GROUP)

        @pl.when(peer != me)
        def _():
            for copy in outward(peer, me):
                copy.start()

        return carry

    if halved:
        half = experts // 2
        base = lax.div(me, half) * half
        mirror = lax.rem(me + half, experts)

        def hidden_copy(source, piece, peer, way):
            return pltpu.make_async_remote_copy(
                src_ref=source, dst_ref=hidden_rows.at[piece], send_sem=hidden_send.at[way, peer],
                recv_sem=hidden_recv.at[piece], device_id={"exp": peer}, device_id_type=MESH,
            )

        def around(action):
            def one(turn, carry):
                action(base + lax.rem(me + turn, half))
                return carry

            lax.fori_loop(1, half, one, 0)

        kept = pltpu.make_async_copy(hidden_ref, hidden_rows.at[me], own_sem.at[6])
        kept.start()
        hidden_copy(hidden_ref, me, mirror, 0).start()
        around(lambda peer: hidden_copy(hidden_ref, me, peer, 0).start())
        lax.fori_loop(0, SOURCE_GROUP, push, 0)
        hidden_copy(hidden_ref, mirror, mirror, 0).wait_recv()
        around(lambda peer: hidden_copy(hidden_rows.at[mirror], mirror, peer, 1).start())
        lax.fori_loop(SOURCE_GROUP, experts, push, 0)
    else:
        lax.fori_loop(0, experts, push, 0)
    side_out[...] = jnp.zeros_like(side_out)
    if halved:
        kept.wait()

        def arrive(peer):
            for piece in (peer, lax.rem(peer + half, experts)):
                hidden_copy(hidden_ref, piece, peer, 0).wait_recv()

        around(arrive)
        hidden_swap = pltpu.make_async_remote_copy(
            src_ref=hidden_rows, dst_ref=hidden_came, send_sem=swap_sem.at[2], recv_sem=swap_sem.at[3],
            device_id={"ctx": other_core}, device_id_type=MESH,
        )
        hidden_swap.start()
        lay_out(hidden_rows, hidden_all.at[1 - other_core])
        hidden_swap.wait()
        lay_out(hidden_came, hidden_all.at[other_core])
        hidden_in_ref, hidden_out_ref = hidden_all.at[0], hidden_all.at[1]
    else:
        hidden_in_ref, hidden_out_ref = hidden_ref.at[0], hidden_ref.at[1]
    for load in loads:
        load.wait()

    rank = lax.broadcasted_iota(jnp.int32, (ADAPTER_RANK, LANES), 0)
    place = lax.broadcasted_iota(jnp.int32, (ADAPTER_RANK, LANES), 1)
    expand = jnp.where(lax.div(place, ADAPTER_COUNT) == rank, 1.0, 0.0).astype(jnp.bfloat16)
    eye = lax.broadcasted_iota(jnp.int32, (capacity, LANES), 0) == lax.broadcasted_iota(
        jnp.int32, (capacity, LANES), 1
    )

    def group(turn, carry):
        order = jnp.where(turn == 1, 2, jnp.where(turn == 2, 1, turn))
        base = plane_of(order) * SOURCE_GROUP
        held_back = (turn == 2) if groups == 4 else False
        for step in range(SOURCE_GROUP):
            source = base + step

            @pl.when(source != me)
            def _():
                for copy in outward(source, source):
                    copy.wait_recv()

            @pl.when(source == me)
            def _():
                for copy in own_in():
                    copy.wait()

            spot = pl.ds(pl.multiple_of(source * capacity, 16), capacity)
            here = pl.ds(step * capacity, capacity)
            keep = mask_ref[source]
            ui = product_first(side_in[source, ADAPTER_RANK:, :], expand)[:capacity] * keep
            lift = product_first(side_in[source, :ADAPTER_RANK, :], expand)[:capacity] * keep
            column = jnp.sum(jnp.where(eye, gate_in[source], 0.0), axis=1, keepdims=True)
            ui_ref[spot, :] = (ADAPTER_SCALE * ui).astype(jnp.bfloat16)
            duo_ref[spot, :] = (column * lift).astype(jnp.bfloat16)
            lift_ref[here, :] = lift
            deo_ref[here, :] = (column * g_ref[source].astype(jnp.float32)).astype(jnp.bfloat16)
        spot = pl.ds(pl.multiple_of(base * capacity, 16), rows)
        x = x_in[pl.ds(base, SOURCE_GROUP)].reshape(rows, MODEL_WIDTH)
        deo, ui, duo = deo_ref[...], ui_ref[spot, :], duo_ref[spot, :]
        ff = first_ref.shape[1]

        def first_products(start):
            part = slice(start, start + FF_BLOCK)
            pre = matrix_multiply(x, first_ref[:, part]) + matrix_multiply(ui, hidden_in_ref[:, part])
            dact = product_last(deo, second_ref[part, :]) + matrix_multiply(duo, hidden_out_ref[:, part])
            return pre, dact

        ahead = first_products(0)
        for start in range(0, ff, FF_BLOCK):
            pre, dact = ahead
            if start + FF_BLOCK < ff:
                ahead = first_products(start + FF_BLOCK)
            square = pre * pre
            bent = jnp.tanh(pre * (GELU_SLOPE + GELU_SLOPE * GELU_CUBE * square))
            half = 0.5 + 0.5 * bent
            made = pre * half
            slope = half + made * (1.0 - half) * (2.0 * GELU_SLOPE + 6.0 * GELU_SLOPE * GELU_CUBE * square)
            act_ref[spot, start : start + FF_BLOCK] = made.astype(jnp.bfloat16)
            dpre_ref[spot, start : start + FF_BLOCK] = (dact * slope).astype(jnp.bfloat16)
        dx = product_last(dpre_ref[spot, :], first_ref[...])
        dx_out[pl.ds(base, SOURCE_GROUP)] = dx.astype(jnp.bfloat16).reshape(SOURCE_GROUP, capacity, MODEL_WIDTH)
        for step in range(SOURCE_GROUP):
            lane = lax.rem(step + me, SOURCE_GROUP)
            source = base + lane

            @pl.when((source != me) & jnp.logical_not(held_back))
            def _():
                homeward(source, me, (0,))[0].start()

            if groups == 4:

                @pl.when(turn == 3)
                def _():
                    homeward(plane_of(1) * SOURCE_GROUP + lane, me, (0,))[0].start()

        dui = product_last(dpre_ref[spot, :], hidden_in_ref[...])
        uo = product_last(act_ref[spot, :], hidden_out_ref[...])
        eo = matrix_multiply(act_ref[spot, :], second_ref[...])
        eo_ref[pl.ds(base, SOURCE_GROUP)] = eo.astype(jnp.bfloat16).reshape(SOURCE_GROUP, capacity, MODEL_WIDTH)
        for step in range(SOURCE_GROUP):
            source = base + step
            here = slice(step * capacity, (step + 1) * capacity)
            keep = mask_ref[source]
            one_uo = (uo[here] * keep).astype(jnp.bfloat16)
            one_dui = (ADAPTER_SCALE * dui[here] * keep).astype(jnp.bfloat16)
            side_out[source, :ADAPTER_RANK, :capacity] = product_last(expand, one_dui).astype(jnp.bfloat16)
            side_out[source, ADAPTER_RANK:, :capacity] = product_last(expand, one_uo).astype(jnp.bfloat16)
            dots = jnp.sum(g_ref[source].astype(jnp.float32) * eo[here], axis=1, keepdims=True)
            dots = dots + jnp.sum(one_uo.astype(jnp.float32) * lift_ref[here, :], axis=1, keepdims=True)
            dgate_out[source] = jnp.sum(jnp.where(eye, dots, 0.0), axis=0, keepdims=True)

            @pl.when(source != me)
            def _():
                for copy in homeward(source, me, (1, 2)):
                    copy.start()

            @pl.when(source == me)
            def _():
                for copy in own_back():
                    copy.start()

        return carry

    lax.fori_loop(0, groups, group, 0)

    def gradients(part, carry):
        spot = pl.ds(pl.multiple_of(part * FF_BLOCK, FF_BLOCK), FF_BLOCK)
        grad_sum[0, :, spot] = product_first(ui_ref[...], dpre_ref[:, spot])
        grad_sum[1, :, spot] = product_first(duo_ref[...], act_ref[:, spot])
        return carry

    lax.fori_loop(0, first_ref.shape[1] // FF_BLOCK, gradients, 0)
    if halved:
        grad_out[...] = grad_sum[other_core].astype(jnp.bfloat16)
        swap = pltpu.make_async_remote_copy(
            src_ref=grad_out, dst_ref=grad_in, send_sem=swap_sem.at[0], recv_sem=swap_sem.at[1],
            device_id={"ctx": other_core}, device_id_type=MESH,
        )
        swap.start()
        swap.wait()
        cut = grad_ref.shape[2]
        for piece in range(grad_ref.shape[0]):
            spot = slice(piece * ADAPTER_COUNT, (piece + 1) * ADAPTER_COUNT)
            halves = [
                grad_sum[1 - other_core, spot, half * cut : (half + 1) * cut]
                + grad_in[spot, half * cut : (half + 1) * cut].astype(jnp.float32)
                for half in range(2)
            ]
            grad_ref[piece] = jnp.concatenate(halves, axis=0).astype(jnp.bfloat16)
    else:
        grad_ref[...] = grad_sum[...].astype(jnp.bfloat16)
    for copy in own_back():
        copy.wait()

    def settle(step, carry):
        peer = lax.rem(me + step, experts)
        for copy in outward(peer, me):
            copy.wait_send()
        for copy in homeward(peer, peer):
            copy.wait_recv()
        for copy in homeward(peer, me):
            copy.wait_send()
        return carry

    lax.fori_loop(1, experts, settle, 0)
    if halved:
        hidden_copy(hidden_ref, me, mirror, 0).wait_send()

        def sent(peer):
            hidden_copy(hidden_ref, me, peer, 0).wait_send()
            hidden_copy(hidden_ref, me, peer, 1).wait_send()

        around(sent)


def run_expert(halved, x, side, gate_slots, g, mask, first, second, hidden):
    experts, capacity, _ = x.shape
    ff = first.shape[2]
    rows = SOURCE_GROUP * capacity
    vmem, anywhere = pl.BlockSpec(memory_space=pltpu.VMEM), pl.BlockSpec(memory_space=pl.ANY)
    bf16, f32 = jnp.bfloat16, jnp.float32
    outs = [
        (x.shape, bf16),
        (x.shape, bf16),
        (side.shape, bf16),
        (gate_slots.shape, f32),
        ((ADAPTER_RANK, 2 * ADAPTER_COUNT, ff // 2) if halved else (2, LANES, ff), bf16),
    ]
    return pl.pallas_call(
        functools.partial(expert_kernel, capacity, halved),
        in_specs=[anywhere, anywhere, anywhere, vmem, vmem, anywhere, anywhere, vmem],
        out_specs=[vmem, anywhere, anywhere, anywhere, vmem],
        out_shape=[whole(shape) for shape in outs],
        scratch_shapes=[
            pltpu.VMEM(first.shape[1:], bf16),
            pltpu.VMEM(second.shape[1:], bf16),
            pltpu.VMEM(x.shape, bf16),
            pltpu.VMEM(side.shape, bf16),
            pltpu.VMEM(gate_slots.shape, f32),
            pltpu.VMEM(x.shape, bf16),
            pltpu.VMEM(side.shape, bf16),
            pltpu.VMEM(gate_slots.shape, f32),
            pltpu.VMEM((rows, MODEL_WIDTH), bf16),
            pltpu.VMEM((experts * capacity, LANES), bf16),
            pltpu.VMEM((experts * capacity, LANES), bf16),
            pltpu.VMEM((rows, LANES), f32),
            pltpu.VMEM((experts * capacity, ff), bf16),
            pltpu.VMEM((experts * capacity, ff), bf16),
            pltpu.VMEM((2, LANES, ff), f32),
            pltpu.VMEM((LANES, ff), bf16),
            pltpu.VMEM((LANES, ff), bf16),
            pltpu.VMEM((experts,) + hidden.shape if halved else (1, LANES), bf16),
            pltpu.VMEM((experts,) + hidden.shape if halved else (1, LANES), bf16),
            pltpu.VMEM((2, LANES, ff) if halved else (1, LANES), bf16),
            pltpu.SemaphoreType.DMA((2, experts)),
            pltpu.SemaphoreType.DMA((experts,)),
            pltpu.SemaphoreType.DMA((2,)),
            pltpu.SemaphoreType.DMA((7,)),
            pltpu.SemaphoreType.DMA((3, experts)),
            pltpu.SemaphoreType.DMA((3, experts)),
            pltpu.SemaphoreType.DMA((3, experts)),
            pltpu.SemaphoreType.DMA((3, experts)),
            pltpu.SemaphoreType.DMA((4,)),
        ],
        compiler_params=pltpu.CompilerParams(
            vmem_limit_bytes=VMEM_BYTES, collective_id=1, has_side_effects=True
        ),
        cost_estimate=SMALL_COST,
        name="run_expert",
    )(x, side, gate_slots, g, mask, first, second, hidden)


def share_places(share, experts):
    starts = [share * owner for owner in range(experts)]
    tiles = max(-(-(start % LANES + share) // LANES) for start in starts)
    return [(start // LANES, start % LANES) for start in starts], tiles


def spread_kernel(runs, all_ref, in_ref, out_ref, sum_ref):
    for row, first, count, sources in runs:
        total = None
        for owner, start in sources:
            one = all_ref[owner, :, start * LANES : (start + count) * LANES].astype(jnp.float32)
            total = one if total is None else total + one
        sum_ref[row * ADAPTER_COUNT : (row + 1) * ADAPTER_COUNT, first * LANES : (first + count) * LANES] = total
    in_ref[...] = sum_ref[:LANES, :].astype(jnp.bfloat16)
    out_ref[...] = sum_ref[LANES:, :].astype(jnp.bfloat16)


def spread_hidden(everyone, share, experts, first_lane):
    parts = everyone.shape[0] // experts
    per_part = everyone.shape[2] // LANES
    places, tiles = share_places(share, experts)
    per_row = FF // LANES
    runs = []
    for tile in range(2 * ADAPTER_RANK * per_row):
        at = first_lane // LANES + tile
        sources = []
        for owner, (start, offset) in enumerate(places):
            local = at - start
            if 0 <= local and local * LANES < offset + share:
                sources.append((local // per_part * experts + owner, local % per_part))
        row, column = divmod(tile, per_row)
        last = runs[-1] if runs else None
        if last and last[0] == row and len(last[3]) == 1 and len(sources) == 1:
            owner, start = last[3][0]
            if sources[0] == (owner, start + last[2]):
                runs[-1] = (row, last[1], last[2] + 1, last[3])
                continue
        runs.append((row, column, 1, sources))
    shape = ((ADAPTER_COUNT * ADAPTER_RANK, FF), jnp.bfloat16)
    return run(
        functools.partial(spread_kernel, runs),
        "spread_hidden",
        [shape, shape],
        everyone,
        scratch=[pltpu.VMEM((2 * ADAPTER_COUNT * ADAPTER_RANK, FF), jnp.float32)],
    )


def own_share_kernel(share, tiles, first_tile, grad_ref, out_ref, sum_ref):
    per_row = FF // LANES
    held_rows = grad_ref.shape[0] // ADAPTER_COUNT
    start = lax.div(lax.axis_index("exp") * share, LANES)
    sum_ref[...] = grad_ref[...].astype(jnp.float32)
    for step in range(tiles):
        tile = start + step - first_tile
        held = jnp.clip(tile, 0, held_rows * per_row - 1)
        row = pl.multiple_of(lax.div(held, per_row) * ADAPTER_COUNT, ADAPTER_COUNT)
        column = pl.multiple_of(lax.rem(held, per_row) * LANES, LANES)
        slab = sum_ref[pl.ds(row, ADAPTER_COUNT), pl.ds(column, LANES)]
        out_ref[:, step * LANES : (step + 1) * LANES] = jnp.where(held == tile, slab, 0.0)


def close_parts(
    share, tiles, window, cuts, mix, down_ref, up_ref, router_ref, pick_ref, piece_ref, out_ref,
    flat, sent, came, own_in, own_wide, own_total, own_came, hidden_in, hidden_wide,
    total_sem, local_sem, swap_send, swap_recv, own_send, own_recv, hidden_send, hidden_recv,
):
    part, me = lax.axis_index("ctx"), lax.axis_index("exp")
    cores, experts = lax.axis_size("ctx"), lax.axis_size("exp")
    per_row = FF // LANES
    first_hidden, last_hidden = cuts[1] // LANES, cuts[2] // LANES
    hidden_row = part * experts + me

    def owner_of(row, end):
        return lax.div((first_hidden + row * per_row) * LANES + end * (FF - 1), share)

    def hidden_copy(row, core, owner):
        return pltpu.make_async_remote_copy(
            src_ref=piece_ref, dst_ref=hidden_in.at[row], send_sem=hidden_send.at[core, owner],
            recv_sem=hidden_recv.at[row], device_id={"ctx": core, "exp": owner}, device_id_type=MESH,
        )

    def hidden_targets(action):
        low, high = owner_of(hidden_row, 0), owner_of(hidden_row, 1)
        for core in range(cores):
            for owner, needed in ((low, True), (high, high != low)):
                elsewhere = (core != part) | (owner != me)

                @pl.when(needed & elsewhere)
                def _():
                    action(hidden_copy(hidden_row, core, owner))

    hidden_targets(lambda copy: copy.start())
    own_hidden = pltpu.make_async_copy(piece_ref, hidden_in.at[hidden_row], local_sem.at[0])
    own_hidden.start()

    flat[...] = jnp.zeros_like(flat)
    columns = 6 * ADAPTER_RANK
    quarter = MODEL_WIDTH // 4
    rows = [down_ref[pl.ds(step, quarter, stride=4), :] for step in range(4)]
    for step in range(3):
        left = rows[step][:, step * (LANES - columns) : columns]
        right = rows[step + 1][:, : LANES - left.shape[1]]
        flat[pl.ds(step, quarter, stride=3), :] = jnp.concatenate([left, right], axis=1)
    per_model = MODEL_WIDTH // LANES
    for step in range(per_model):
        spot = pl.ds(cuts[0] // LANES + step, 5 * ADAPTER_RANK, stride=per_model)
        flat[spot, :] = up_ref[: 5 * ADAPTER_RANK, step * LANES : (step + 1) * LANES]
    per_tile = LANES // experts
    for tile in range(ADAPTER_RANK // per_tile):
        total = jnp.zeros((1, LANES), jnp.float32)
        for step in range(per_tile):
            row = 4 * ADAPTER_RANK + tile * per_tile + step
            one = router_ref[row : row + 1, :]
            total = total + (pltpu.roll(one, step * experts, 1) if step else one)
        flat[last_hidden + tile : last_hidden + tile + 1, :] = total
    sent[...] = flat[...].astype(jnp.bfloat16)

    def swap(turn):
        core = lax.rem(part + turn, cores)
        return pltpu.make_async_remote_copy(
            src_ref=sent, dst_ref=came.at[turn - 1], send_sem=swap_send.at[turn - 1],
            recv_sem=swap_recv.at[turn - 1], device_id={"ctx": core}, device_id_type=MESH,
        )

    for turn in range(1, cores):
        swap(turn).start()
    for turn in range(1, cores):
        swap(turn).wait()
    total = flat[...]
    for turn in range(1, cores):
        total = total + came[turn - 1].astype(jnp.float32)
    sent[...] = total.astype(jnp.bfloat16)

    def has_own(owner):
        return (owner * share < cuts[1]) | ((owner + 1) * share > cuts[2])

    def window_of(owner):
        start = lax.div(lax.div(owner * share, LANES), 16) * 16
        return sent.at[pl.ds(pl.multiple_of(start, 16), window)]

    def own_copy(owner, slot):
        return pltpu.make_async_remote_copy(
            src_ref=window_of(owner), dst_ref=own_in.at[slot], send_sem=own_send.at[owner],
            recv_sem=own_recv.at[slot], device_id={"exp": owner}, device_id_type=MESH,
        )

    def push(turn, carry):
        owner = lax.rem(me + turn, experts)

        @pl.when(has_own(owner) & (lax.rem(owner, 2) == part))
        def _():
            own_copy(owner, me).start()

        return carry

    lax.fori_loop(1, experts, push, 0)
    kept = pltpu.make_async_copy(window_of(me), own_in.at[me], local_sem.at[1])
    kept.start()
    start = lax.div(me * share, LANES)
    offset = lax.rem(start, 16)

    mix()

    own_hidden.wait()

    def arrive(row, carry):
        sender_core, sender = lax.div(row, experts), lax.rem(row, experts)
        mine = (owner_of(row, 0) == me) | (owner_of(row, 1) == me)

        @pl.when(mine & ((sender_core != part) | (sender != me)))
        def _():
            hidden_copy(row, part, me).wait_recv()

        return carry

    lax.fori_loop(0, 2 * ADAPTER_RANK, arrive, 0)
    hidden_wide[...] = hidden_in[...].astype(jnp.float32)
    half = per_row // 2
    for step in range(tiles):
        tile = start + step - first_hidden
        held = jnp.clip(tile, 0, 2 * ADAPTER_RANK * per_row - 1)
        row, column = lax.div(held, per_row), lax.rem(held, per_row)
        upper = pl.multiple_of(lax.div(column, half) * ADAPTER_COUNT, ADAPTER_COUNT)
        column = pl.multiple_of(lax.rem(column, half) * LANES, LANES)
        slab = hidden_wide[row, pl.ds(upper, ADAPTER_COUNT), pl.ds(column, LANES)]
        out_ref[:, step * LANES : (step + 1) * LANES] = jnp.where(held == tile, slab, 0.0)

    kept.wait()
    totals = pltpu.make_async_remote_copy(
        src_ref=own_total, dst_ref=own_came, send_sem=total_sem.at[0], recv_sem=total_sem.at[1],
        device_id={"ctx": 1 - part}, device_id_type=MESH,
    )
    summing = lax.rem(me, 2) == part

    @pl.when(has_own(me) & summing)
    def _():
        def arrive(turn, carry):
            sender = lax.rem(me + turn, experts)
            own_copy(sender, sender).wait_recv()
            return carry

        lax.fori_loop(1, experts, arrive, 0)
        for adapter in range(ADAPTER_COUNT):
            total = jnp.zeros((window, LANES), jnp.float32)
            for sender in range(experts):
                total = total + jnp.where(pick_ref[sender] == adapter, own_in[sender].astype(jnp.float32), 0.0)
            own_wide[adapter * window : (adapter + 1) * window, :] = total
        for step in range(tiles):
            slab = own_wide[pl.ds(offset + step, ADAPTER_COUNT, stride=window), :]
            own_total[:, step * LANES : (step + 1) * LANES] = slab
        totals.start()
        out_ref[...] = out_ref[...] + own_total[...]
        totals.wait_send()

    @pl.when(has_own(me) & jnp.logical_not(summing))
    def _():
        totals.wait_recv()
        out_ref[...] = out_ref[...] + own_came[...]

    def settle(turn, carry):
        owner = lax.rem(me + turn, experts)

        @pl.when(has_own(owner) & (lax.rem(owner, 2) == part))
        def _():
            own_copy(owner, me).wait_send()

        return carry

    lax.fori_loop(1, experts, settle, 0)
    hidden_targets(lambda copy: copy.wait_send())


def backward_kernel(
    share, tiles, window, cuts, capacity,
    dx_ref, dgate_ref, dest_cols_ref, routes_ref, gates_ref, hidden_ref, xn_two_ref, grad_ref, ur_ref, w_ref, o_ref,
    out_weight_ref, router_ref, own_router_ref, own_down_ref, own_up_ref, gain_ref, side_ref, pick_ref,
    qe_ref, ke_ref, far_ref, u_ref, made_hbm, pieces_hbm, q_hbm, kv_hbm, lse_hbm, turned_hbm, weight_hbm, tokens_hbm, xn_hbm,
    input_grad_ref, share_ref, mixed_ref,
    q_ref, kv_ref, lse_ref, turned_ref, weight_ref, tokens_ref, xn_ref, dh_ref, do_ref, grad_down, grad_up, grad_router, uo_ref,
    dq_ref, dkv_ref, other_ref, qx_ref, gx_ref, dq_sum, kv_made, ret_ref, piece_ref, load_sem, kv_send, kv_recv,
    ret_send, ret_recv, ret_own, *rest,
):
    part, me = lax.axis_index("ctx"), lax.axis_index("exp")
    cores, experts = lax.axis_size("ctx"), lax.axis_size("exp")
    passing, closing = rest[:7], rest[7:]
    mix_sum = dh_ref
    loads = [
        pltpu.make_async_copy(source, target, load_sem.at[i])
        for i, (source, target) in enumerate(
            (
                (q_hbm, q_ref), (kv_hbm, kv_ref), (lse_hbm, lse_ref), (turned_hbm, turned_ref), (weight_hbm, weight_ref),
                (tokens_hbm, tokens_ref), (xn_hbm, xn_ref),
            )
        )
    ]
    for load in loads:
        load.start()
    barrier = pltpu.get_barrier_semaphore()

    def greet(turn, carry):
        core, peer = lax.div(turn, experts), lax.rem(turn, experts)

        @pl.when((core != part) | (peer != me))
        def _():
            pl.semaphore_signal(barrier, inc=1, device_id={"ctx": core, "exp": peer}, device_id_type=MESH)

        return carry

    lax.fori_loop(0, cores * experts, greet, 0)
    pl.semaphore_wait(barrier, cores * experts - 1)
    begin, middle, end = pass_pieces(pieces_hbm, piece_ref, *passing)

    def ret_spot(slot):
        return ret_ref.at[pl.ds(pl.multiple_of(slot * capacity, 16), capacity)]

    def ret_copy(peer, slot):
        return pltpu.make_async_remote_copy(
            src_ref=made_hbm.at[peer], dst_ref=ret_spot(slot), send_sem=ret_send.at[peer],
            recv_sem=ret_recv.at[slot], device_id={"exp": peer}, device_id_type=MESH,
        )

    own_ret = pltpu.make_async_copy(made_hbm.at[me], ret_spot(me), ret_own.at[0])
    own_ret.start()

    def push(orders, lanes=(0, SOURCE_GROUP)):
        push_rows(me, experts, lambda peer: ret_copy(peer, me).start(), orders, lanes)

    def between(turn):
        @pl.when(turn <= SOURCE_GROUP)
        def _():
            plane = paired(2, lax.div(me, SOURCE_GROUP), experts // SOURCE_GROUP)
            ret_copy(plane * SOURCE_GROUP + lax.rem(turn + me, SOURCE_GROUP), me).start()

    begin(between)
    push((1, 0))
    back_kernel(
        capacity, dx_ref, dgate_ref, dest_cols_ref, routes_ref, gates_ref, hidden_ref, xn_two_ref, grad_ref,
        ur_ref, w_ref, o_ref, out_weight_ref, router_ref, own_router_ref, own_down_ref, own_up_ref, gain_ref, side_ref,
        dh_ref, do_ref, grad_down, grad_up, grad_router, uo_ref,
    )
    for load in loads[:4]:
        load.wait()
    half = tokens_ref.shape[0] // 2
    pairs = HEADS // 2

    def attend(pair, carry):
        spot = pl.ds(pl.multiple_of(pair * LANES, LANES), LANES)
        attend_back_pair(
            cores, half, pair, pairs, q_ref.at[:, spot], kv_ref.at[:, pl.ds(0, 1), :, spot],
            kv_ref.at[:, pl.ds(1, 1), :, spot], do_ref.at[:, spot], o_ref.at[:, spot], lse_ref.at[:, spot],
            qe_ref, ke_ref, far_ref.at[pl.ds(pair, 1)], turned_ref.at[pl.ds(2 * pair, 2)],
            dq_ref.at[:, spot], dkv_ref.at[:, :, spot], other_ref, qx_ref, gx_ref, dq_sum, kv_made, kv_send, kv_recv,
        )

        @pl.when(pair == 2)
        def _():
            middle()
            push((3,), (0, 3))

        return carry

    lax.fori_loop(0, pairs, attend, 0)
    end()
    for load in loads[4:]:
        load.wait()

    dxn = jnp.zeros(dh_ref.shape, jnp.float32)
    du = jnp.zeros(u_ref.shape, jnp.float32)
    for group in range(3):
        if group == 0:
            grad = dq_ref[...]
        else:
            grad = dkv_ref[group - 1].astype(jnp.float32)
            for turn in range(1, cores):
                grad = grad + other_ref[turn - 1, group - 1].astype(jnp.float32)
            grad = grad.astype(jnp.bfloat16)
        spot = slice(group * MODEL_WIDTH, (group + 1) * MODEL_WIDTH)
        dxn = dxn + product_last(grad, weight_ref[:, spot])
        own = group_mask(group, group + 1)
        du = du + jnp.where(own, ADAPTER_SCALE * product_last(grad, own_up_ref[...]), 0.0)
        inner = jnp.where(own, u_ref[...], jnp.zeros((), jnp.bfloat16))
        grad_up[...] += ADAPTER_SCALE * product_first(inner, grad)
    du = du.astype(jnp.bfloat16)
    grad_down[...] += product_first(xn_ref[...], du)

    def mix():
        finish = (dxn + product_last(du, own_down_ref[...])) * gain_ref[0:1, :]
        tokens = tokens_ref[...].astype(jnp.float32)
        scale = lax.rsqrt(jnp.mean(tokens * tokens, axis=-1, keepdims=True) + NORM_EPS)
        inner = jnp.mean(tokens * finish, axis=-1, keepdims=True)
        input_grad_ref[...] = dh_ref[...] + scale * finish - tokens * (scale * scale * scale * inner)
        push((3,), (3, SOURCE_GROUP))
        total = hidden_ref[...]
        for k in range(2):
            lifted = ADAPTER_SCALE * matrix_multiply(uo_ref[k], own_up_ref[...])
            total = total + gates_ref[:, k : k + 1] * lifted
        mix_sum[...] = total
        own_ret.wait()
        for order in (0, 1, 2):
            mix_plane(order)

    plane_slots = SOURCE_GROUP * capacity

    def mix_plane(order):
        plane = paired(order, lax.div(me, SOURCE_GROUP), experts // SOURCE_GROUP)

        def arrive(lane, carry):
            peer = plane * SOURCE_GROUP + lane

            @pl.when(peer != me)
            def _():
                ret_copy(peer, peer).wait_recv()

            return carry

        lax.fori_loop(0, SOURCE_GROUP, arrive, 0)
        first = plane * plane_slots
        rows = ret_ref[pl.ds(pl.multiple_of(first, 16), plane_slots), :]
        slot = lax.broadcasted_iota(jnp.int32, (hidden_ref.shape[0], plane_slots), 1) + first
        total = mix_sum[...]
        for k in range(2):
            hot = jnp.where(slot == dest_cols_ref[:, k : k + 1], 1.0, 0.0).astype(jnp.bfloat16)
            total = total + gates_ref[:, k : k + 1] * matrix_multiply(hot, rows)
        mix_sum[...] = total

    close_parts(
        share, tiles, window, cuts, mix, grad_down, grad_up, grad_router, pick_ref, piece_ref, share_ref, *closing
    )
    mix_plane(3)
    mixed_ref[...] = mix_sum[...].astype(jnp.bfloat16)

    def settle(turn, carry):
        ret_copy(lax.rem(me + turn, experts), me).wait_send()
        return carry

    lax.fori_loop(1, experts, settle, 0)


def backward(share, tiles, cuts, capacity, cores, near, far_away):
    dx, hidden, o = near[0], near[5], near[10]
    made, pieces, q, kv, lse, turned, weight, tokens, xn = far_away
    rows, experts = hidden.shape[0], made.shape[0]
    window = -(-(15 + tiles) // 16) * 16
    length = max(share * owner // LANES // 16 * 16 for owner in range(experts)) + window
    bf16, f32 = jnp.bfloat16, jnp.float32
    vmem, anywhere = pl.BlockSpec(memory_space=pltpu.VMEM), pl.BlockSpec(memory_space=pl.ANY)
    dma = pltpu.SemaphoreType.DMA
    model, lanes = (rows, MODEL_WIDTH), (rows, LANES)
    piece = pieces.shape[1:]
    outs = [(model, f32), ((ADAPTER_COUNT, tiles * LANES), f32), (model, bf16)]
    return pl.pallas_call(
        functools.partial(backward_kernel, share, tiles, window, cuts, capacity),
        in_specs=[
            pl.BlockSpec(memory_space=pltpu.SMEM) if one.ndim == 1 else vmem for one in near
        ]
        + [anywhere] * len(far_away),
        out_specs=[vmem] * 3,
        out_shape=[whole(shape) for shape in outs],
        scratch_shapes=[
            pltpu.VMEM(q.shape, bf16),
            pltpu.VMEM(kv.shape, bf16),
            pltpu.VMEM(lse.shape, f32),
            pltpu.VMEM(turned.shape, f32),
            pltpu.VMEM(weight.shape, bf16),
            pltpu.VMEM(tokens.shape, bf16),
            pltpu.VMEM(xn.shape, bf16),
            pltpu.VMEM(model, f32),
            pltpu.VMEM(model, bf16),
            pltpu.VMEM((MODEL_WIDTH, LANES), f32),
            pltpu.VMEM((LANES, MODEL_WIDTH), f32),
            pltpu.VMEM((LANES, LANES), f32),
            pltpu.VMEM((2,) + lanes, bf16),
            pltpu.VMEM(model, bf16),
            pltpu.VMEM((2,) + model, bf16),
            pltpu.VMEM((cores - 1, 2) + model, bf16),
            pltpu.VMEM((2,) + lanes, bf16),
            pltpu.VMEM((2,) + lanes, bf16),
            pltpu.VMEM((2, LANES, rows), f32),
            pltpu.VMEM((2, cores, 2) + lanes, bf16),
            pltpu.VMEM(dx.shape, bf16),
            pltpu.VMEM(piece, bf16),
            dma((7,)),
            dma((2, cores - 1)),
            dma((HEADS // 2, cores - 1)),
            dma((experts,)),
            dma((experts,)),
            dma((1,)),
            *pieces_scratch(pieces),
            pltpu.VMEM((length, LANES), f32),
            pltpu.VMEM((length, LANES), bf16),
            pltpu.VMEM((cores - 1, length, LANES), bf16),
            pltpu.VMEM((experts, window, LANES), bf16),
            pltpu.VMEM((ADAPTER_COUNT * window, LANES), f32),
            pltpu.VMEM((ADAPTER_COUNT, tiles * LANES), f32),
            pltpu.VMEM((ADAPTER_COUNT, tiles * LANES), f32),
            pltpu.VMEM((2 * ADAPTER_RANK,) + piece, bf16),
            pltpu.VMEM((2 * ADAPTER_RANK,) + piece, f32),
            dma((2,)),
            dma((2,)),
            dma((cores - 1,)),
            dma((cores - 1,)),
            dma((experts,)),
            dma((experts,)),
            dma((cores, experts)),
            dma((2 * ADAPTER_RANK,)),
        ],
        compiler_params=pltpu.CompilerParams(
            vmem_limit_bytes=VMEM_BYTES + (4 << 20), collective_id=3, has_side_effects=True
        ),
        cost_estimate=SMALL_COST,
        name="backward",
    )(*near, *far_away)


def back_kernel(
    capacity, dx_ref, dgate_slots_ref, dest_cols_ref, route_cols_ref, gates_ref, hidden_ref, xn_ref, grad_ref,
    ur_ref, w_ref, o_ref, weight_ref, router_ref, router_up_ref, down_ref, up_ref, gain_ref, side_ref,
    dh_ref, do_ref, grad_down_ref, grad_up_ref, grad_router_ref, uo_ref,
):
    count = hidden_ref.shape[0]
    lane = lane_ids()
    dests = [dest_cols_ref[:, k : k + 1] for k in range(2)]
    back = jnp.zeros((count, MODEL_WIDTH), jnp.float32)
    for start in range(0, dx_ref.shape[0], ROW_BLOCK):
        size = min(ROW_BLOCK, dx_ref.shape[0] - start)
        slot = lax.broadcasted_iota(jnp.int32, (count, size), 1) + start
        hot = jnp.where((slot == dests[0]) | (slot == dests[1]), 1.0, 0.0).astype(jnp.bfloat16)
        back = back + matrix_multiply(hot, dx_ref[start : start + size, :])
    dgates = []
    sides = []
    blank = jnp.zeros((LANES, LANES), jnp.bfloat16)
    for k in range(2):
        sums = jnp.zeros((count, LANES), jnp.float32)
        side = jnp.zeros((count, LANES), jnp.float32)
        for expert in range(dgate_slots_ref.shape[0]):
            hot = dests[k] - expert * capacity == lane
            sums = sums + jnp.where(hot, dgate_slots_ref[expert], 0.0)
            hot = jnp.where(hot, 1.0, 0.0).astype(jnp.bfloat16)
            wide = [blank[: 5 * ADAPTER_RANK], side_ref[expert], blank[: LANES - 7 * ADAPTER_RANK]]
            side = side + product_last(hot, jnp.concatenate(wide, axis=0))
        dgates.append(jnp.sum(sums, axis=1, keepdims=True))
        sides.append(side)
    gates = [gates_ref[:, k : k + 1] for k in range(2)]
    mean = gates[0] * dgates[0] + gates[1] * dgates[1]
    dlogits = jnp.zeros((count, LANES), jnp.float32)
    for k in range(2):
        dsel = gates[k] * (dgates[k] - mean)
        dlogits = dlogits + jnp.where(lane == route_cols_ref[:, k : k + 1], dsel, 0.0)
    dlogits = dlogits.astype(jnp.bfloat16)
    dur = ADAPTER_SCALE * product_last(dlogits, router_up_ref[...])
    dur = jnp.where(group_mask(4, 5), dur, sides[0] + sides[1])
    dur = keep_group(dur, 4, 6)
    dxn = back + product_last(dlogits, router_ref[...]) + product_last(dur, down_ref[...])
    dxn = dxn.astype(jnp.bfloat16).astype(jnp.float32)
    hidden = hidden_ref[...]
    scale = lax.rsqrt(jnp.mean(hidden * hidden, axis=-1, keepdims=True) + NORM_EPS)
    dxn = dxn * gain_ref[1:2, :]
    inner = jnp.mean(hidden * dxn, axis=-1, keepdims=True)
    dh = grad_ref[...].astype(jnp.float32) + scale * dxn - hidden * (scale * scale * scale * inner)
    dh_ref[...] = dh
    db = dh.astype(jnp.bfloat16)
    dw = keep_group(ADAPTER_SCALE * product_last(db, up_ref[...]), 3, 4)
    do_ref[...] = (product_last(db, weight_ref[...]) + product_last(dw, down_ref[...])).astype(jnp.bfloat16)
    grad_down_ref[...] = product_first(o_ref[...], dw) + product_first(xn_ref[...], dur)
    grad_up = product_first(w_ref[...], db)
    for k in range(2):
        uo = keep_group(pltpu.roll(sides[k], LANES - 2 * ADAPTER_RANK, 1), 4, 5)
        uo_ref[k] = uo
        deo = (gates[k] * grad_ref[...].astype(jnp.float32)).astype(jnp.bfloat16)
        grad_up = grad_up + product_first(uo, deo)
    grad_up_ref[...] = ADAPTER_SCALE * grad_up
    grad_router_ref[...] = ADAPTER_SCALE * product_first(ur_ref[...], dlogits)


def qkv_back_kernel(
    dq_ref, mine_ref, other_ref, weight_ref, down_ref, up_ref, xn_ref, u_ref, tokens_ref, gain_ref, dh_ref, grad_down_in_ref, grad_up_in_ref,
    out_ref, grad_down_ref, grad_up_ref, sum_ref, du_ref, grad_ref,
):
    step = pl.program_id(0)

    @pl.when(step == 0)
    def _():
        grad_ref[...] = dq_ref[...]
        sum_ref[...] = jnp.zeros_like(sum_ref)
        du_ref[...] = jnp.zeros_like(du_ref)
        grad_up_ref[...] = grad_up_in_ref[...]

    @pl.when(step > 0)
    def _():
        total = mine_ref[0].astype(jnp.float32) + other_ref[0].astype(jnp.float32)
        grad_ref[...] = total.astype(jnp.bfloat16)

    lane = lane_ids()
    group = (lane >= step * ADAPTER_RANK) & (lane < (step + 1) * ADAPTER_RANK)
    grad = grad_ref[...]
    sum_ref[...] += product_last(grad, weight_ref[...])
    du = jnp.where(group, ADAPTER_SCALE * product_last(grad, up_ref[...]), 0.0)
    du_ref[...] += du
    inner = jnp.where(group, u_ref[...], jnp.zeros((), jnp.bfloat16))
    grad_up_ref[...] += ADAPTER_SCALE * product_first(inner, grad)

    @pl.when(step == 2)
    def _():
        du = du_ref[...].astype(jnp.bfloat16)
        dxn = (sum_ref[...] + product_last(du, down_ref[...])) * gain_ref[0:1, :]
        tokens = tokens_ref[...].astype(jnp.float32)
        scale = lax.rsqrt(jnp.mean(tokens * tokens, axis=-1, keepdims=True) + NORM_EPS)
        inner = jnp.mean(tokens * dxn, axis=-1, keepdims=True)
        out_ref[...] = dh_ref[...] + scale * dxn - tokens * (scale * scale * scale * inner)
        grad_down_ref[...] = grad_down_in_ref[...] + product_first(xn_ref[...], du)


def qkv_back(dq, dkv, other, weight, down, up, xn, u, tokens, gains, dh, grad_down, grad_up):
    rows = tokens.shape[0]
    fixed = lambda array: pl.BlockSpec(array.shape, lambda g: (0, 0))
    later = lambda g: jnp.maximum(g - 1, 0)
    return pl.pallas_call(
        qkv_back_kernel,
        grid=(3,),
        in_specs=[
            fixed(dq),
            pl.BlockSpec((1, rows, MODEL_WIDTH), lambda g: (later(g), 0, 0)),
            pl.BlockSpec((1, rows, MODEL_WIDTH), lambda g: (later(g), 0, 0)),
            pl.BlockSpec((MODEL_WIDTH, MODEL_WIDTH), lambda g: (0, g)),
            fixed(down), fixed(up), fixed(xn), fixed(u), fixed(tokens), fixed(gains), fixed(dh),
            fixed(grad_down), fixed(grad_up),
        ],
        out_specs=[fixed(dh), fixed(grad_down), fixed(grad_up)],
        out_shape=[jax.ShapeDtypeStruct(a.shape, jnp.float32) for a in (dh, grad_down, grad_up)],
        scratch_shapes=[
            pltpu.VMEM((rows, MODEL_WIDTH), jnp.float32),
            pltpu.VMEM((rows, LANES), jnp.float32),
            pltpu.VMEM((rows, MODEL_WIDTH), jnp.bfloat16),
        ],
        compiler_params=pltpu.CompilerParams(vmem_limit_bytes=VMEM_BYTES),
        cost_estimate=SMALL_COST,
        name="qkv_back",
    )(dq, dkv, other, weight, down, up, xn, u, tokens, gains, dh, grad_down, grad_up)


def mix_kernel(ret_ref, dest_cols_ref, gates_ref, hidden_ref, uo_ref, up_ref, out_ref):
    count = hidden_ref.shape[0]
    total = hidden_ref[...]
    for k in range(2):
        dest = dest_cols_ref[:, k : k + 1]
        picked = ADAPTER_SCALE * matrix_multiply(uo_ref[k], up_ref[...])
        for start in range(0, ret_ref.shape[0], ROW_BLOCK):
            size = min(ROW_BLOCK, ret_ref.shape[0] - start)
            slot = lax.broadcasted_iota(jnp.int32, (count, size), 1) + start
            hot = jnp.where(slot == dest, 1.0, 0.0).astype(jnp.bfloat16)
            picked = picked + matrix_multiply(hot, ret_ref[start : start + size, :])
        total = total + gates_ref[:, k : k + 1] * picked
    out_ref[...] = total.astype(jnp.bfloat16)


def exchange(array, exp_count):
    blocks = array.reshape((exp_count, array.shape[0] // exp_count) + array.shape[1:])
    return lax.all_to_all(blocks, "exp", split_axis=0, concat_axis=0, tiled=True).reshape(array.shape)


def shards(
    tokens,
    cotangent,
    norm_gains,
    query_key_value_weight,
    attention_out_weight,
    rel_bias,
    router_matrix,
    expert_in,
    expert_out,
    adapters,
    first_moment,
    second_moment,
    segment_ids,
    routes,
    adapter_pick,
):
    ctx_count = lax.axis_size("ctx")
    exp_count = lax.axis_size("exp")
    ctx_index = lax.axis_index("ctx")
    bf16, f32 = jnp.bfloat16, jnp.float32
    rows = tokens.shape[2]
    token_rows, grad_rows = tokens[0, 0], cotangent[0, 0]
    share = adapters.shape[1]
    down_size = 6 * ADAPTER_RANK * MODEL_WIDTH
    up_size = 5 * ADAPTER_RANK * MODEL_WIDTH
    hidden_size = 2 * ADAPTER_RANK * FF
    cuts = (down_size, down_size + up_size, down_size + up_size + hidden_size)

    halved = ctx_count == 2 and exp_count == ADAPTER_RANK
    places, tiles = share_places(share, exp_count)
    offset = lax.rem(lax.axis_index("exp") * share, LANES)

    capacity = 5 * rows * 2 // (4 * exp_count)
    capacity = -(-capacity // 16) * 16
    slots = exp_count * capacity
    by_source = (exp_count, capacity, MODEL_WIDTH)
    (
        home, route_cols, dest_rows, dest_cols, mask,
        query, gathered, normed_one, inner_qkv, own_down, own_up, own_router, turned, mixed_rows, log_sums,
        qe, ke, far, router, hidden, normed_two, inner_out, inner_router, gates, gate_slots, side, sent, arrived_grad,
    ) = forward(
        share, tiles, cuts, halved, capacity, ctx_count, exp_count, adapters, adapter_pick, token_rows, grad_rows,
        norm_gains, rel_bias, segment_ids, router_matrix.T, routes[0, 0].T, query_key_value_weight, attention_out_weight,
    )

    if halved:
        hidden_weights = home
    else:
        per_part = -(-tiles // ctx_count)
        shifted = jnp.zeros((ADAPTER_COUNT, per_part * ctx_count * LANES), bf16)
        shifted = lax.dynamic_update_slice(shifted, adapters.astype(bf16), (0, offset))
        shifted = lax.dynamic_slice_in_dim(shifted, ctx_index * per_part * LANES, per_part * LANES, 1)
        everyone = lax.all_gather(shifted, ("ctx", "exp"), axis=0)
        hidden_weights = jnp.stack(spread_hidden(everyone, share, exp_count, cuts[1]))

    made, returned_back, returned_side, returned_dgate, grad_hidden = run_expert(
        halved, sent.reshape(by_source), side, gate_slots, arrived_grad, mask,
        expert_in, expert_out, hidden_weights,
    )
    returned_back = returned_back.reshape(slots, MODEL_WIDTH)

    pick_hot = (jnp.arange(ADAPTER_COUNT, dtype=jnp.int32)[:, None] == adapter_pick[None, :]).astype(bf16)
    back_operands = (
        returned_back, returned_dgate, dest_cols, route_cols, gates, hidden, normed_two, grad_rows, inner_router,
        inner_out, mixed_rows, attention_out_weight, router, own_router, own_down, own_up, norm_gains, returned_side,
    )
    if halved:
        input_grad, owned_grad, output_rows = backward(
            share, tiles, cuts, capacity, ctx_count,
            back_operands + (adapter_pick, qe, ke, far, inner_qkv),
            (
                made, grad_hidden, query, gathered, log_sums, turned, query_key_value_weight, token_rows, normed_one,
            ),
        )
        owned_grad = lax.dynamic_slice_in_dim(owned_grad, offset, share, 1)
    else:
        hidden_grad, out_grad, grad_down, grad_up, grad_router, inner_second = run(
            functools.partial(back_kernel, capacity),
            "back_to_attention",
            [
                ((rows, MODEL_WIDTH), f32),
                ((rows, MODEL_WIDTH), bf16),
                ((MODEL_WIDTH, LANES), f32),
                ((LANES, MODEL_WIDTH), f32),
                ((LANES, LANES), f32),
                ((2, rows, LANES), bf16),
            ],
            *back_operands,
        )
        returned = exchange(made.reshape(slots, MODEL_WIDTH), exp_count)
        query_grad, key_value_grad, others = attend_back(
            query, gathered, out_grad, mixed_rows, log_sums, qe, ke, far, turned
        )
        other = jnp.sum(others.astype(f32), axis=0).astype(bf16)
        input_grad, grad_down, grad_up = qkv_back(
            query_grad, key_value_grad, other, query_key_value_weight, own_down, own_up, normed_one, inner_qkv,
            token_rows, norm_gains, hidden_grad, grad_down, grad_up,
        )
        (output_rows,) = run(
            mix_kernel,
            "mix",
            [((rows, MODEL_WIDTH), bf16)],
            returned, dest_cols, gates, hidden, inner_second, own_up,
        )
        own_grad = jnp.concatenate(
            [
                grad_down[:, : 6 * ADAPTER_RANK].astype(bf16).reshape(-1),
                grad_up[: 5 * ADAPTER_RANK].astype(bf16).reshape(-1),
                jnp.zeros((hidden_size,), bf16),
                grad_router[4 * ADAPTER_RANK : 5 * ADAPTER_RANK, : router_matrix.shape[1]].astype(bf16).reshape(-1),
            ]
        )
        own_grad = exchange(own_grad.reshape(exp_count, share), exp_count)
        owned_grad = lax.psum(matrix_multiply(pick_hot, own_grad), "ctx")
        grad_hidden = lax.psum(grad_hidden.reshape(2 * LANES, FF), ("ctx", "exp"))
        (hidden_share,) = run(
            functools.partial(own_share_kernel, share, tiles, cuts[1] // LANES),
            "own_share",
            [((ADAPTER_COUNT, tiles * LANES), f32)],
            grad_hidden,
            scratch=[pltpu.VMEM(grad_hidden.shape, f32)],
        )
        owned_grad = owned_grad + lax.dynamic_slice_in_dim(hidden_share, offset, share, 1)
    new_first = BETA_ONE * first_moment + (1.0 - BETA_ONE) * owned_grad
    new_second = BETA_TWO * second_moment + (1.0 - BETA_TWO) * owned_grad * owned_grad
    corrected = new_first / (1.0 - BETA_ONE**STEP_NUM)
    denominator = jnp.sqrt(new_second / (1.0 - BETA_TWO**STEP_NUM)) + ADAM_EPS
    new_adapters = adapters - LEARN_RATE * (corrected / denominator + WEIGHT_DECAY * adapters)
    return (
        output_rows[None, None],
        input_grad[None, None],
        new_adapters,
        new_first,
        new_second,
    )


def solution(mesh):
    return jax.shard_map(
        shards,
        mesh=mesh,
        in_specs=(
            P("exp", "ctx", None, None),
            P("exp", "ctx", None, None),
            P(),
            P(),
            P(),
            P(),
            P(),
            P("exp", None, None),
            P("exp", None, None),
            P(None, "exp"),
            P(None, "exp"),
            P(None, "exp"),
            P("exp", None),
            P("exp", "ctx", None, None),
            P(),
        ),
        out_specs=(
            P("exp", "ctx", None, None),
            P("exp", "ctx", None, None),
            P(None, "exp"),
            P(None, "exp"),
            P(None, "exp"),
        ),
        check_vma=False,
    )
```
